512 devices in a mesh: lat: 4 (over y_lo, core), lon: 32 (over y_hi, z), head: 4 (over x).
Axes of the slice: x: 4, y: 4 (y_hi: 2, y_lo: 2; y = y_hi * 2 + y_lo), z: 16, core: 2. Of those that a mesh axis runs over, the one named last changes fastest.
Arguments:
- activations: bfloat16 [32, 1024, 768], P('lat', ('lon', 'head')), may hold values from -6 to 6
- qkv_weight: bfloat16 [3, 768, 768], P(None, 'head'), may hold values from -0.21875 to 0.21875
- out_weight: bfloat16 [768, 768], P('head'), may hold values from -0.21875 to 0.21875
- valid: int32 [32, 1024], P('lat', 'lon'), may hold values 0 or 1
- grad_y: bfloat16 [32, 1024, 768], P('lat', ('lon', 'head')), may hold values from -6 to 6
Outputs:
- mixed: bfloat16 [32, 1024, 768], P('lat', ('lon', 'head'))
- grad_x: bfloat16 [32, 1024, 768], P('lat', ('lon', 'head'))
- grad_qkv_weight: bfloat16 [3, 768, 768], P(None, 'head')
- grad_out_weight: bfloat16 [768, 768], P('head')
The draws below stay inside these ranges and needn't reach their ends.
All inputs are finite; a program needn't handle non-finite values. No bound on the sum of `valid` on one device may be relied on, other than what follows from the above.
Results may differ from the reference program's by a relative error of at most 0.011.
Values may be sent and summed in bfloat16 or wider, within the bound.
A program may use at most 64 MiB of HBM per device.

```python
import jax
import jax.numpy as jnp
from jax import lax

HEADS = 12
HEAD_SIZE = 64
D = 768
REACH = 6
NLAT = 32
NLON = 1024
N_HEAD = 4


def plant(result, own_key, smallest, largest):
    longest = result.shape.index(max(result.shape))
    spots = []
    for shift in (0, 1):
        where = [jax.random.randint(jax.random.fold_in(own_key, axis), (), 0, length) for axis, length in enumerate(result.shape)]
        where[longest] = (where[longest] + shift) % result.shape[longest]
        spots.append(tuple(where))
    return result.at[spots[0]].set(smallest).at[spots[1]].set(largest)


def block_levels(stream_key, dims, cuts, smallest, largest):
    def one(position, shards_of):
        heights = jax.random.uniform(jax.random.fold_in(jax.random.fold_in(stream_key, 6), position), (shards_of,), jnp.float32, smallest / len(cuts), largest / len(cuts))
        return jnp.repeat(jnp.exp(heights), dims[position] // shards_of).reshape((-1,) + (1,) * (len(dims) - position - 1))

    level = one(*cuts[0])
    for cut in cuts[1:]:
        level = level * one(*cut)
    return level


def gaussian(rng, shape, deviation, most, split=(), held_as=jnp.bfloat16):
    entries = jax.random.normal(rng, shape, jnp.float32) * deviation
    if len(split) > 0:
        entries = block_levels(rng, shape, split, -0.22, 0.18) * entries
    return jnp.clip(entries, min=-most, max=most).astype(held_as)


def setup_inputs(seed: int = 0) -> dict:
    seeds = jax.random.split(jax.random.key(seed), 6)
    activations = gaussian(seeds[0], (NLAT, NLON, D), 1.0, 6.0, ((0, 4), (1, 128)))
    qkv_weight = gaussian(seeds[1], (3, D, D), D ** -0.5, 0.21875, ((1, 4),))
    out_weight = gaussian(seeds[2], (D, D), D ** -0.5, 0.21875, ((0, 4),))
    valid = plant((jax.random.randint(seeds[3], (NLAT, NLON), 0, 8) < 7).astype(jnp.int32), jax.random.fold_in(seeds[3], 1), 0, 1)
    grad_y = gaussian(seeds[4], (NLAT, NLON, D), 1.0, 6.0, ((0, 4), (1, 128)))
    return dict(activations=activations, qkv_weight=qkv_weight, out_weight=out_weight, valid=valid, grad_y=grad_y)


def normalize(values):
    wide = values.astype(jnp.float32)
    center = wide - lax.optimization_barrier(jnp.mean(wide, axis=-1, keepdims=True))
    spread = lax.optimization_barrier(jnp.mean(center * center, axis=-1, keepdims=True))
    inv_spread = lax.rsqrt(spread + 1e-05)
    return (center * inv_spread, inv_spread)

def moved(field, shift_lat, shift_lon):
    widths = [(REACH, REACH)] + [(0, 0)] * (field.ndim - 1)
    padded = jnp.pad(field, widths)
    start = (shift_lat + REACH).astype(jnp.int32)
    rows = lax.dynamic_slice_in_dim(padded, start, field.shape[0], 0)
    return jnp.roll(rows, -shift_lon, axis=1)

def rounded(values):
    return lax.optimization_barrier(values.astype(jnp.bfloat16)).astype(jnp.float32)

def reference(activations, qkv_weight, out_weight, valid, grad_y):
    lat_n, lon_n, width = activations.shape
    cells = lat_n * lon_n
    scale = HEAD_SIZE ** (-0.5)
    side = 2 * REACH + 1
    middle = REACH * side + REACH
    group = width // N_HEAD
    norm32, inv_spread = normalize(activations)
    normed = norm32.astype(jnp.bfloat16)
    flat_weight = qkv_weight.reshape(3 * width, width)
    projected = lax.dot_general(normed.reshape(cells, width), flat_weight, (((1,), (1,)), ((), ())), preferred_element_type=jnp.float32)
    projected = projected.astype(jnp.bfloat16).reshape(lat_n, lon_n, 3, HEADS, HEAD_SIZE)
    query = projected[:, :, 0].astype(jnp.float32)
    key = projected[:, :, 1].astype(jnp.float32)
    value = projected[:, :, 2].astype(jnp.float32)
    flag = valid.astype(jnp.float32)
    offsets = jnp.arange(side * side, dtype=jnp.int32)

    def scores(step):
        shift_lat = step // side - REACH
        shift_lon = step % side - REACH
        key_at = moved(key, shift_lat, shift_lon)
        flag_at = moved(flag, shift_lat, shift_lon)
        allowed = (flag_at > 0) | (step == middle)
        score = scale * lax.optimization_barrier(jnp.sum(query * key_at, axis=-1))
        return (score, allowed[:, :, None], key_at, shift_lat, shift_lon)

    def top(best, step):
        score, allowed, key_at, shift_lat, shift_lon = scores(step)
        return (jnp.maximum(best, jnp.where(allowed, score, -1e+30)), None)
    best, _ = lax.scan(top, jnp.full((lat_n, lon_n, HEADS), -1e+30, jnp.float32), offsets)

    def total(acc, step):
        score, allowed, key_at, shift_lat, shift_lon = scores(step)
        return (acc + jnp.where(allowed, jnp.exp(score - best), 0.0), None)
    denom, _ = lax.scan(total, jnp.zeros((lat_n, lon_n, HEADS), jnp.float32), offsets)
    level = best + jnp.log(denom)

    def weigh(acc, step):
        score, allowed, key_at, shift_lat, shift_lon = scores(step)
        soft = jnp.where(allowed, jnp.exp(score - level), 0.0).astype(jnp.bfloat16).astype(jnp.float32)
        return (acc + soft[..., None] * moved(value, shift_lat, shift_lon), None)
    summed, _ = lax.scan(weigh, jnp.zeros((lat_n, lon_n, HEADS, HEAD_SIZE), jnp.float32), offsets)
    attended = summed.astype(jnp.bfloat16)
    attended_rows = attended.reshape(cells, width)
    projection = jnp.zeros((cells, width), jnp.float32)
    for part in range(N_HEAD):
        lo = part * group
        term = jnp.dot(attended_rows[:, lo:lo + group], out_weight[lo:lo + group], preferred_element_type=jnp.float32)
        projection = projection + rounded(term)
    mixed = (activations.astype(jnp.float32) + projection.reshape(lat_n, lon_n, width)).astype(jnp.bfloat16)
    grad_rows = grad_y.reshape(cells, width)
    grad_out_weight = jnp.dot(attended_rows.T, grad_rows, preferred_element_type=jnp.float32).astype(jnp.bfloat16)
    d_attended = jnp.dot(grad_rows, out_weight.T, preferred_element_type=jnp.float32).astype(jnp.bfloat16)
    d_attended = d_attended.reshape(lat_n, lon_n, HEADS, HEAD_SIZE).astype(jnp.float32)
    carried = lax.optimization_barrier(jnp.sum(d_attended * attended.astype(jnp.float32), axis=-1))

    def backward(carry, step):
        grad_query, grad_key, grad_value = carry
        score, allowed, key_at, shift_lat, shift_lon = scores(step)
        value_at = moved(value, shift_lat, shift_lon)
        chance = jnp.where(allowed, jnp.exp(score - level), 0.0)
        inner = lax.optimization_barrier(jnp.sum(d_attended * value_at, axis=-1))
        soft_grad = (chance * (inner - carried)).astype(jnp.bfloat16).astype(jnp.float32)
        soft = chance.astype(jnp.bfloat16).astype(jnp.float32)
        grad_query = grad_query + scale * soft_grad[..., None] * key_at
        grad_key = grad_key + moved(scale * soft_grad[..., None] * query, -shift_lat, -shift_lon)
        grad_value = grad_value + moved(soft[..., None] * d_attended, -shift_lat, -shift_lon)
        return ((grad_query, grad_key, grad_value), None)
    empty = jnp.zeros((lat_n, lon_n, HEADS, HEAD_SIZE), jnp.float32)
    grads, _ = lax.scan(backward, (empty, empty, empty), offsets)
    grad_projected = jnp.stack(grads, axis=2).astype(jnp.bfloat16).reshape(cells, 3, width)
    grad_qkv_weight = jnp.dot(grad_projected.reshape(cells, 3 * width).T, normed.reshape(cells, width), preferred_element_type=jnp.float32)
    grad_qkv_weight = grad_qkv_weight.reshape(3, width, width).astype(jnp.bfloat16)
    grad_normed = jnp.zeros((cells, width), jnp.float32)
    for part in range(N_HEAD):
        lo = part * group
        cols = grad_projected[:, :, lo:lo + group].reshape(cells, 3 * group)
        rows = qkv_weight[:, lo:lo + group, :].reshape(3 * group, width)
        term = jnp.dot(cols, rows, preferred_element_type=jnp.float32)
        grad_normed = grad_normed + rounded(term)
    grad_normed = grad_normed.reshape(lat_n, lon_n, width)
    first = lax.optimization_barrier(jnp.mean(grad_normed, axis=-1, keepdims=True))
    second = lax.optimization_barrier(jnp.mean(grad_normed * norm32, axis=-1, keepdims=True))
    d_input = inv_spread * (grad_normed - first - norm32 * second)
    grad_x = (grad_y.astype(jnp.float32) + d_input).astype(jnp.bfloat16)
    return (mixed, grad_x, grad_qkv_weight, grad_out_weight)
```

```python
import functools

import jax
import jax.numpy as jnp
import numpy as np
from jax import lax
from jax.experimental import pallas as pl
from jax.experimental.pallas import tpu as pltpu
from jax.sharding import PartitionSpec as P

MESH = pl.DeviceIdType.MESH
N_Z = 16
N_Y = 4
N_OWN = 9


class Place:
    def __init__(self):
        self.lat = lax.axis_index("lat")
        self.lon = lax.axis_index("lon")
        self.head = lax.axis_index("head")
        self.core = lax.rem(self.lat, 2)
        self.y = (self.lon // N_Z) * 2 + self.lat // 2
        self.z = lax.rem(self.lon, N_Z)

    def at(self, core=None, y=None, z=None):
        core = self.core if core is None else core
        y = self.y if y is None else y
        z = self.z if z is None else z
        return (lax.rem(y, 2) * 2 + core, (y // 2) * N_Z + z, self.head)


def remote(src, dst, send_sem, recv_sem, device):
    return pltpu.make_async_remote_copy(
        src_ref=src,
        dst_ref=dst,
        send_sem=send_sem,
        recv_sem=recv_sem,
        device_id=device,
        device_id_type=MESH,
    )


class Summed:
    def __init__(self, place, turn, src, res, cbuf, ybuf, zbuf, sem_c, sem_y, sem_z, sem_zg, sem_yg, sem_cg):
        self.p = place
        self.src, self.res, self.cbuf, self.ybuf, self.zbuf = src, res, cbuf, ybuf, zbuf
        self.sem_c, self.sem_y, self.sem_z = sem_c, sem_y, sem_z
        self.sem_zg, self.sem_yg, self.sem_cg = sem_zg, sem_yg, sem_cg
        self.turn = turn
        turned = lax.rem(place.z + N_Z - turn, N_Z)
        self.mine = (turned * N_OWN + N_Z - 1) // N_Z
        self.owner = (self.mine * N_Z) // N_OWN == turned
        self.mine = jnp.minimum(self.mine, N_OWN - 1)

    @staticmethod
    def scratch(t):
        bf = jnp.bfloat16
        return [
            pltpu.VMEM((2, N_Y, N_OWN, t, 128), bf),
            pltpu.VMEM((2, N_Y, N_OWN, t, 128), bf),
            pltpu.VMEM((N_Y, N_OWN, t, 128), bf),
            pltpu.VMEM((N_Y, N_OWN, t, 128), bf),
            pltpu.VMEM((N_Z, t, 128), bf),
            pltpu.SemaphoreType.DMA((2,)),
            pltpu.SemaphoreType.DMA((2, N_Y)),
            pltpu.SemaphoreType.DMA((2, N_Z)),
            pltpu.SemaphoreType.DMA((2, N_Z)),
            pltpu.SemaphoreType.DMA((2, N_Y)),
            pltpu.SemaphoreType.DMA((2, N_Y)),
        ]

    def core_copy(self):
        p = self.p
        return remote(
            self.src.at[1 - p.core], self.cbuf, self.sem_c.at[0], self.sem_c.at[1], p.at(core=1 - p.core)
        )

    def y_copy(self, step, arriving=False):
        p = self.p
        y = lax.rem(p.y + step, N_Y)
        slot = y if arriving else p.y
        return remote(
            self.src.at[p.core, y], self.ybuf.at[slot], self.sem_y.at[0, y], self.sem_y.at[1, slot], p.at(y=y)
        )

    def owner_z(self, tile):
        return lax.rem((tile * N_Z) // N_OWN + self.turn, N_Z)

    def z_copy(self, tile):
        p = self.p
        return remote(
            self.src.at[p.core, p.y, tile],
            self.zbuf.at[p.z],
            self.sem_z.at[0, tile],
            self.sem_z.at[1, p.z],
            p.at(z=self.owner_z(tile)),
        )

    def z_arrival(self, z):
        p = self.p
        return remote(
            self.src.at[p.core, p.y, 0], self.zbuf.at[z], self.sem_z.at[0, 0], self.sem_z.at[1, z], p.at(z=z)
        )

    def zg_copy(self, z, tile):
        p = self.p
        here = self.res.at[p.core, p.y, tile]
        return remote(here, here, self.sem_zg.at[0, z], self.sem_zg.at[1, tile], p.at(z=z))

    def yg_copy(self, step, arriving=False):
        p = self.p
        y = lax.rem(p.y + step, N_Y)
        slot = y if arriving else p.y
        here = self.res.at[p.core, slot]
        return remote(here, here, self.sem_yg.at[0, y], self.sem_yg.at[1, slot], p.at(y=y))

    def cg_copy(self, y, arriving=False):
        p = self.p
        here = self.res.at[1 - p.core if arriving else p.core, y]
        return remote(here, here, self.sem_cg.at[0, y], self.sem_cg.at[1, y], p.at(core=1 - p.core))

    def send_core(self):
        self.core_copy().start()

    def core_to_y(self):
        p = self.p
        self.core_copy().wait_recv()
        for step in (2, 1, 3, 0):
            y = lax.rem(p.y + step, N_Y)
            both = self.src[p.core, y].astype(jnp.float32) + self.cbuf[y].astype(jnp.float32)
            self.src[p.core, y] = both.astype(jnp.bfloat16)
            if step:
                self.y_copy(step).start()

    def y_to_z(self):
        p = self.p
        for step in (1, 3, 2):
            self.y_copy(step, True).wait_recv()
        total = self.src[p.core, p.y].astype(jnp.float32)
        for step in (1, 2, 3):
            total = total + self.ybuf[lax.rem(p.y + step, N_Y)].astype(jnp.float32)
        self.src[p.core, p.y] = total.astype(jnp.bfloat16)

        @pl.loop(0, N_OWN)
        def _(tile):
            @pl.when(self.owner_z(tile) != p.z)
            def _():
                self.z_copy(tile).start()

    def z_to_all(self):
        p = self.p

        @pl.when(self.owner)
        def _():
            @pl.loop(1, N_Z)
            def _(step):
                self.z_arrival(lax.rem(p.z + step, N_Z)).wait_recv()

            def add(step, total):
                return total + self.zbuf[lax.rem(p.z + step, N_Z)].astype(jnp.float32)

            own = self.src[p.core, p.y, self.mine].astype(jnp.float32)
            total = lax.fori_loop(1, N_Z, add, own)
            self.res[p.core, p.y, self.mine] = total.astype(jnp.bfloat16)

            @pl.loop(1, N_Z)
            def _(step):
                self.zg_copy(lax.rem(p.z + step, N_Z), self.mine).start()

    def all_to_y(self):
        p = self.p

        @pl.loop(0, N_OWN)
        def _(tile):
            @pl.when(self.owner_z(tile) != p.z)
            def _():
                self.zg_copy(0, tile).wait_recv()

        for step in (2, 1, 3):
            self.yg_copy(step).start()
        self.cg_copy(p.y).start()

    def y_to_core(self):
        p = self.p
        for step in (1, 3, 2):
            self.yg_copy(step, True).wait_recv()
            self.cg_copy(lax.rem(p.y + step, N_Y)).start()

    def finish(self):
        p = self.p
        for y in range(N_Y):
            self.cg_copy(y, True).wait_recv()
        self.core_copy().wait_send()
        for step in (1, 2, 3):
            self.y_copy(step).wait_send()
            self.yg_copy(step).wait_send()
        for y in range(N_Y):
            self.cg_copy(y).wait_send()

        @pl.loop(0, N_OWN)
        def _(tile):
            @pl.when(self.owner_z(tile) != p.z)
            def _():
                self.z_copy(tile).wait_send()

        @pl.when(self.owner)
        def _():
            @pl.loop(1, N_Z)
            def _(step):
                self.zg_copy(lax.rem(p.z + step, N_Z), self.mine).wait_send()


def sum_kernel(t, part_ref, out_ref, *scratch):
    place = Place()
    barrier = pltpu.get_barrier_semaphore()
    pl.semaphore_signal(barrier, inc=1, device_id=place.at(core=1 - place.core), device_id_type=MESH)
    for step in range(1, N_Y):
        pl.semaphore_signal(
            barrier, inc=1, device_id=place.at(y=lax.rem(place.y + step, N_Y)), device_id_type=MESH
        )

    @pl.loop(1, N_Z)
    def _(step):
        pl.semaphore_signal(
            barrier, inc=1, device_id=place.at(z=lax.rem(place.z + step, N_Z)), device_id_type=MESH
        )

    summed = Summed(place, 0, *scratch)
    for core in range(2):
        for y in range(N_Y):
            for tile in range(N_OWN):
                top = y * 3 * t + tile // 3 * t
                left = core * 384 + tile % 3 * 128
                summed.src[core, y, tile] = part_ref[top : top + t, left : left + 128].astype(jnp.bfloat16)
    pl.semaphore_wait(barrier, 1 + N_Y - 1 + N_Z - 1)
    summed.send_core()
    summed.core_to_y()
    summed.y_to_z()
    summed.z_to_all()
    summed.all_to_y()
    summed.y_to_core()
    summed.finish()
    for core in range(2):
        for y in range(N_Y):
            for tile in range(N_OWN):
                top = y * 3 * t + tile // 3 * t
                left = core * 384 + tile % 3 * 128
                out_ref[top : top + t, left : left + 128] = summed.res[core, y, tile]


def summed_over_cells(part):
    t = part.shape[0] // 12
    return pl.pallas_call(
        functools.partial(sum_kernel, t),
        out_shape=jax.ShapeDtypeStruct(part.shape, jnp.bfloat16),
        in_specs=[pl.BlockSpec(memory_space=pltpu.VMEM)],
        out_specs=pl.BlockSpec(memory_space=pltpu.VMEM),
        scratch_shapes=Summed.scratch(t),
        compiler_params=pltpu.CompilerParams(
            collective_id=0, has_side_effects=True, vmem_limit_bytes=40 * 2**20
        ),
    )(part)

HEAD_SIZE = 64
REACH = 6


TILE_ROWS = 8
TILE_COLS = 16
NEGATIVE = -1e30


def extended(cells, sides, width):
    for axis, dim in sides:
        count = lax.axis_size(axis)
        head = lax.slice_in_dim(cells, 0, width, axis=dim)
        tail = lax.slice_in_dim(cells, cells.shape[dim] - width, cells.shape[dim], axis=dim)
        cells = jnp.concatenate(
            [
                lax.ppermute(tail, axis, [(i, (i + 1) % count) for i in range(count)]),
                cells,
                lax.ppermute(head, axis, [((i + 1) % count, i) for i in range(count)]),
            ],
            axis=dim,
        )
    return cells


def normalize(values):
    wide = values.astype(jnp.float32)
    center = wide - jnp.mean(wide, axis=-1, keepdims=True)
    spread = jnp.mean(center * center, axis=-1, keepdims=True)
    inv_spread = lax.rsqrt(spread + 1e-05)
    return (center * inv_spread, inv_spread)


def window_tables(radius):
    block_rows = TILE_ROWS + 2 * radius
    block_cols = TILE_COLS + 2 * radius
    query_cells = np.arange(TILE_ROWS * TILE_COLS)
    block_cells = np.arange(block_rows * block_cols)
    step_lat = (block_cells // block_cols)[None, :] - radius - (query_cells // TILE_COLS)[:, None]
    step_lon = (block_cells % block_cols)[None, :] - radius - (query_cells % TILE_COLS)[:, None]
    inside = (np.abs(step_lat) <= radius) & (np.abs(step_lon) <= radius)
    center = (step_lat == 0) & (step_lon == 0)
    return (jnp.asarray(inside), jnp.asarray(center))


def cut_block(field, top, left, rows, cols):
    starts = (top, left) + (0,) * (field.ndim - 2)
    piece = lax.dynamic_slice(field, starts, (rows, cols) + field.shape[2:])
    return piece.reshape((rows * cols,) + field.shape[2:])


def untile(pieces, tiles_down, tiles_across):
    rest = pieces.shape[2:]
    grid = pieces.reshape((tiles_down, tiles_across, TILE_ROWS, TILE_COLS) + rest)
    order = (0, 2, 1, 3) + tuple(range(4, grid.ndim))
    return grid.transpose(order).reshape((tiles_down * TILE_ROWS, tiles_across * TILE_COLS) + rest)


def project_rows(normed_rows, weight):
    return lax.dot_general(
        normed_rows, weight, (((1,), (2,)), ((), ())), preferred_element_type=jnp.float32
    )


def on_device(activations, qkv_weight, out_weight, valid, grad_y):
    lat_cells, own_cols, full = activations.shape
    width = qkv_weight.shape[1]
    heads = width // HEAD_SIZE
    scale = HEAD_SIZE ** (-0.5)
    radius = REACH
    block_rows = TILE_ROWS + 2 * radius
    block_cols = TILE_COLS + 2 * radius
    whole = lax.all_gather(activations, "head", axis=1, tiled=True)
    lon_cells = whole.shape[1]
    tiles_down = lat_cells // TILE_ROWS
    tiles_across = lon_cells // TILE_COLS
    tile_ids = jnp.arange(tiles_down * tiles_across, dtype=jnp.int32)
    rows_all = lat_cells * lax.axis_size("lat")
    global_rows = (
        lax.axis_index("lat") * lat_cells
        - radius
        + jnp.arange(lat_cells + 2 * radius, dtype=jnp.int32)
    )
    row_inside = ((global_rows >= 0) & (global_rows < rows_all)).astype(jnp.float32)
    row_margin = jnp.broadcast_to(
        row_inside[:, None], (lat_cells + 2 * radius, lon_cells + 2 * radius)
    )
    valid_half = valid.astype(jnp.bfloat16)
    norm32, inv_spread = normalize(whole)
    normed = norm32.astype(jnp.bfloat16)
    projected = project_rows(normed.reshape(-1, full), qkv_weight)
    projected = projected.astype(jnp.bfloat16).reshape(lat_cells, lon_cells, 3, width)
    query = projected[:, :, 0]
    paired = projected[:, :, 1:].reshape(lat_cells, lon_cells, 2 * width)
    pair_margin, margin_valid = (
        extended(paired, (("lat", 0), ("lon", 1)), REACH),
        extended(valid_half, (("lat", 0), ("lon", 1)), REACH),
    )
    key_margin = pair_margin[:, :, :width]
    value_margin = pair_margin[:, :, width:]
    key_flag = margin_valid.astype(jnp.float32) * row_margin
    inside, center = window_tables(radius)

    def by_heads(piece):
        return piece.reshape(piece.shape[0], heads, HEAD_SIZE)

    def tile_start(index):
        return (index // tiles_across * TILE_ROWS, index % tiles_across * TILE_COLS)

    def forward_tile(index):
        top, left = tile_start(index)
        query_tile = by_heads(cut_block(query, top, left, TILE_ROWS, TILE_COLS))
        key_block = by_heads(cut_block(key_margin, top, left, block_rows, block_cols))
        value_block = by_heads(cut_block(value_margin, top, left, block_rows, block_cols))
        flag_block = cut_block(key_flag, top, left, block_rows, block_cols)
        allowed = inside & ((flag_block[None, :] > 0) | center)
        score = scale * jnp.einsum(
            "qhc,khc->hqk", query_tile, key_block, preferred_element_type=jnp.float32
        )
        score = jnp.where(allowed, score, NEGATIVE)
        best = jnp.max(score, axis=2, keepdims=True)
        total = jnp.sum(jnp.where(allowed, jnp.exp(score - best), 0.0), axis=2, keepdims=True)
        level = best + jnp.log(total)
        soft = jnp.where(allowed, jnp.exp(score - level), 0.0).astype(jnp.bfloat16)
        result = jnp.einsum("hqk,khc->qhc", soft, value_block, preferred_element_type=jnp.float32)
        return (result.astype(jnp.bfloat16).reshape(TILE_ROWS * TILE_COLS, width), level[:, :, 0].T)

    attended_tiles, level_tiles = lax.map(forward_tile, tile_ids)
    attended = untile(attended_tiles, tiles_down, tiles_across)
    level = untile(level_tiles, tiles_down, tiles_across)
    attended_rows = attended.reshape(-1, width)
    partial_value = jnp.dot(attended_rows, out_weight, preferred_element_type=jnp.float32).reshape(
        lat_cells, lon_cells, full
    )
    summed = lax.psum_scatter(
        partial_value.astype(jnp.bfloat16), "head", scatter_dimension=1, tiled=True
    ).astype(jnp.float32)
    mixed = (activations.astype(jnp.float32) + summed).astype(jnp.bfloat16)
    grad_full = lax.all_gather(grad_y, "head", axis=1, tiled=True)
    grad_rows = grad_full.reshape(-1, full)
    grad_out_local = jnp.einsum(
        "nc,nd->cd", attended_rows, grad_rows, preferred_element_type=jnp.float32
    )
    d_attended = jnp.einsum("nd,cd->nc", grad_rows, out_weight, preferred_element_type=jnp.float32)
    d_attended = d_attended.astype(jnp.bfloat16).reshape(lat_cells, lon_cells, width)
    carried = jnp.einsum(
        "xyhc,xyhc->xyh",
        d_attended.reshape(lat_cells, lon_cells, heads, HEAD_SIZE),
        attended.reshape(lat_cells, lon_cells, heads, HEAD_SIZE),
        preferred_element_type=jnp.float32,
    )
    margin_pair = extended(
        jnp.concatenate([query, d_attended], axis=2), (("lat", 0), ("lon", 1)), REACH
    )
    margin_stats = extended(
        jnp.concatenate([level, carried], axis=2), (("lat", 0), ("lon", 1)), REACH
    )
    query_margin = margin_pair[:, :, :width]
    dout_margin = margin_pair[:, :, width:]
    level_margin = margin_stats[:, :, :heads]
    carried_margin = margin_stats[:, :, heads:]
    valid_own = valid.astype(jnp.float32)

    def backward_tile(index):
        top, left = tile_start(index)
        query_tile = by_heads(cut_block(query, top, left, TILE_ROWS, TILE_COLS))
        dout_tile = by_heads(cut_block(d_attended, top, left, TILE_ROWS, TILE_COLS))
        level_tile = cut_block(level, top, left, TILE_ROWS, TILE_COLS)
        carried_tile = cut_block(carried, top, left, TILE_ROWS, TILE_COLS)
        key_block = by_heads(cut_block(key_margin, top, left, block_rows, block_cols))
        value_block = by_heads(cut_block(value_margin, top, left, block_rows, block_cols))
        flag_block = cut_block(key_flag, top, left, block_rows, block_cols)
        allowed = inside & ((flag_block[None, :] > 0) | center)
        score = scale * jnp.einsum(
            "qhc,khc->hqk", query_tile, key_block, preferred_element_type=jnp.float32
        )
        chance = jnp.where(allowed, jnp.exp(score - level_tile.T[:, :, None]), 0.0)
        inner = jnp.einsum(
            "qhc,khc->hqk", dout_tile, value_block, preferred_element_type=jnp.float32
        )
        soft_grad = (chance * (inner - carried_tile.T[:, :, None])).astype(jnp.bfloat16)
        grad_query = scale * jnp.einsum(
            "hqk,khc->qhc", soft_grad, key_block, preferred_element_type=jnp.float32
        )
        key_tile = by_heads(
            cut_block(key_margin, top + radius, left + radius, TILE_ROWS, TILE_COLS)
        )
        value_tile = by_heads(
            cut_block(value_margin, top + radius, left + radius, TILE_ROWS, TILE_COLS)
        )
        own_flag = cut_block(valid_own, top, left, TILE_ROWS, TILE_COLS)
        query_block = by_heads(cut_block(query_margin, top, left, block_rows, block_cols))
        dout_block = by_heads(cut_block(dout_margin, top, left, block_rows, block_cols))
        level_block = cut_block(level_margin, top, left, block_rows, block_cols)
        carried_block = cut_block(carried_margin, top, left, block_rows, block_cols)
        rows_block = cut_block(row_margin, top, left, block_rows, block_cols)
        allowed_keys = inside & ((own_flag[:, None] > 0) | center) & (rows_block[None, :] > 0)
        score_keys = scale * jnp.einsum(
            "khc,qhc->hkq", key_tile, query_block, preferred_element_type=jnp.float32
        )
        chance_keys = jnp.where(allowed_keys, jnp.exp(score_keys - level_block.T[:, None, :]), 0.0)
        inner_keys = jnp.einsum(
            "qhc,khc->hkq", dout_block, value_tile, preferred_element_type=jnp.float32
        )
        soft_grad_keys = (chance_keys * (inner_keys - carried_block.T[:, None, :])).astype(
            jnp.bfloat16
        )
        grad_key = scale * jnp.einsum(
            "hkq,qhc->khc", soft_grad_keys, query_block, preferred_element_type=jnp.float32
        )
        grad_value = jnp.einsum(
            "hkq,qhc->khc",
            chance_keys.astype(jnp.bfloat16),
            dout_block,
            preferred_element_type=jnp.float32,
        )
        stacked = jnp.stack([grad_query, grad_key, grad_value], axis=1).astype(jnp.bfloat16)
        return stacked.reshape(TILE_ROWS * TILE_COLS, 3 * width)

    grad_tiles = lax.map(backward_tile, tile_ids)
    grad_projected = untile(grad_tiles, tiles_down, tiles_across).reshape(-1, 3, width)
    grad_qkv_local = jnp.einsum(
        "nkc,nd->kcd", grad_projected, normed.reshape(-1, full), preferred_element_type=jnp.float32
    )
    parts = jnp.concatenate([grad_qkv_local.reshape(3 * width, full), grad_out_local], axis=0)
    sums = summed_over_cells(parts)
    grad_normed = jnp.einsum(
        "nkc,kcd->nd", grad_projected, qkv_weight, preferred_element_type=jnp.float32
    )
    grad_normed = grad_normed.reshape(lat_cells, lon_cells, full)
    start = lax.axis_index("head") * own_cols
    own_grad = lax.psum_scatter(
        grad_normed.astype(jnp.bfloat16), "head", scatter_dimension=1, tiled=True
    ).astype(jnp.float32)
    norm_own = lax.dynamic_slice_in_dim(norm32, start, own_cols, 1)
    spread_own = lax.dynamic_slice_in_dim(inv_spread, start, own_cols, 1)
    first = jnp.mean(own_grad, axis=-1, keepdims=True)
    second = jnp.mean(own_grad * norm_own, axis=-1, keepdims=True)
    d_input = spread_own * (own_grad - first - norm_own * second)
    grad_x = (grad_y.astype(jnp.float32) + d_input).astype(jnp.bfloat16)
    return (mixed, grad_x, sums[: 3 * width].reshape(3, width, full), sums[3 * width :])


def solution(mesh):
    return jax.shard_map(
        on_device,
        mesh=mesh,
        in_specs=(
            P("lat", ("lon", "head"), None),
            P(None, "head", None),
            P("head", None),
            P("lat", "lon"),
            P("lat", ("lon", "head"), None),
        ),
        out_specs=(
            P("lat", ("lon", "head"), None),
            P("lat", ("lon", "head"), None),
            P(None, "head", None),
            P("head", None),
        ),
        check_vma=False,
    )
```

```python
import jax
import jax.numpy as jnp
from jax import lax
from jax.experimental import pallas as pl
from jax.experimental.pallas import tpu as pltpu
from jax.sharding import PartitionSpec as P

MESH = pl.DeviceIdType.MESH
HEAD_SIZE = 64
REACH = 6
EPSILON = 1e-05
NEGATIVE = -1e30
N_HEAD = 4
N_LAT = 4
N_LON = 32
CELLS = 64
FULL = 768
TALL = 160
AROUND = 3 * TALL
N_Z = 16
N_Y = 4
N_OWN = 9


class Place:
    def __init__(self):
        self.lat = lax.axis_index("lat")
        self.lon = lax.axis_index("lon")
        self.head = lax.axis_index("head")
        self.core = lax.rem(self.lat, 2)
        self.y = (self.lon // N_Z) * 2 + self.lat // 2
        self.z = lax.rem(self.lon, N_Z)

    def at(self, core=None, y=None, z=None):
        core = self.core if core is None else core
        y = self.y if y is None else y
        z = self.z if z is None else z
        return (lax.rem(y, 2) * 2 + core, (y // 2) * N_Z + z, self.head)


    def beside(self, step_lat, step_lon):
        return (self.lat + step_lat, lax.rem(self.lon + step_lon + N_LON, N_LON), self.head)

    def peer(self, head):
        return (self.lat, self.lon, head)


def remote(src, dst, send_sem, recv_sem, device):
    return pltpu.make_async_remote_copy(
        src_ref=src,
        dst_ref=dst,
        send_sem=send_sem,
        recv_sem=recv_sem,
        device_id=device,
        device_id_type=MESH,
    )


class Summed:
    def __init__(self, place, turn, src, res, cbuf, ybuf, zbuf, sem_c, sem_y, sem_z, sem_zg, sem_yg, sem_cg):
        self.p = place
        self.src, self.res, self.cbuf, self.ybuf, self.zbuf = src, res, cbuf, ybuf, zbuf
        self.sem_c, self.sem_y, self.sem_z = sem_c, sem_y, sem_z
        self.sem_zg, self.sem_yg, self.sem_cg = sem_zg, sem_yg, sem_cg
        self.turn = turn
        turned = lax.rem(place.z + N_Z - turn, N_Z)
        self.mine = (turned * N_OWN + N_Z - 1) // N_Z
        self.owner = (self.mine * N_Z) // N_OWN == turned
        self.mine = jnp.minimum(self.mine, N_OWN - 1)

    @staticmethod
    def scratch(t):
        bf = jnp.bfloat16
        return [
            pltpu.VMEM((2, N_Y, N_OWN, t, 128), bf),
            pltpu.VMEM((2, N_Y, N_OWN, t, 128), bf),
            pltpu.VMEM((N_Y, N_OWN, t, 128), bf),
            pltpu.VMEM((N_Y, N_OWN, t, 128), bf),
            pltpu.VMEM((N_Z, t, 128), bf),
            pltpu.SemaphoreType.DMA((2,)),
            pltpu.SemaphoreType.DMA((2, N_Y)),
            pltpu.SemaphoreType.DMA((2, N_Z)),
            pltpu.SemaphoreType.DMA((2, N_Z)),
            pltpu.SemaphoreType.DMA((2, N_Y)),
            pltpu.SemaphoreType.DMA((2, N_Y)),
        ]

    def core_copy(self):
        p = self.p
        return remote(
            self.src.at[1 - p.core], self.cbuf, self.sem_c.at[0], self.sem_c.at[1], p.at(core=1 - p.core)
        )

    def y_copy(self, step, arriving=False):
        p = self.p
        y = lax.rem(p.y + step, N_Y)
        slot = y if arriving else p.y
        return remote(
            self.src.at[p.core, y], self.ybuf.at[slot], self.sem_y.at[0, y], self.sem_y.at[1, slot], p.at(y=y)
        )

    def owner_z(self, tile):
        return lax.rem((tile * N_Z) // N_OWN + self.turn, N_Z)

    def z_copy(self, tile):
        p = self.p
        return remote(
            self.src.at[p.core, p.y, tile],
            self.zbuf.at[p.z],
            self.sem_z.at[0, tile],
            self.sem_z.at[1, p.z],
            p.at(z=self.owner_z(tile)),
        )

    def z_arrival(self, z):
        p = self.p
        return remote(
            self.src.at[p.core, p.y, 0], self.zbuf.at[z], self.sem_z.at[0, 0], self.sem_z.at[1, z], p.at(z=z)
        )

    def zg_copy(self, z, tile):
        p = self.p
        here = self.res.at[p.core, p.y, tile]
        return remote(here, here, self.sem_zg.at[0, z], self.sem_zg.at[1, tile], p.at(z=z))

    def yg_copy(self, step, arriving=False):
        p = self.p
        y = lax.rem(p.y + step, N_Y)
        slot = y if arriving else p.y
        here = self.res.at[p.core, slot]
        return remote(here, here, self.sem_yg.at[0, y], self.sem_yg.at[1, slot], p.at(y=y))

    def cg_copy(self, y, arriving=False):
        p = self.p
        here = self.res.at[1 - p.core if arriving else p.core, y]
        return remote(here, here, self.sem_cg.at[0, y], self.sem_cg.at[1, y], p.at(core=1 - p.core))

    def send_core(self):
        self.core_copy().start()

    def core_to_y(self):
        p = self.p
        self.core_copy().wait_recv()
        for step in (2, 1, 3, 0):
            y = lax.rem(p.y + step, N_Y)
            both = self.src[p.core, y].astype(jnp.float32) + self.cbuf[y].astype(jnp.float32)
            self.src[p.core, y] = both.astype(jnp.bfloat16)
            if step:
                self.y_copy(step).start()

    def y_to_z(self):
        p = self.p
        for step in (1, 3, 2):
            self.y_copy(step, True).wait_recv()
        total = self.src[p.core, p.y].astype(jnp.float32)
        for step in (1, 2, 3):
            total = total + self.ybuf[lax.rem(p.y + step, N_Y)].astype(jnp.float32)
        self.src[p.core, p.y] = total.astype(jnp.bfloat16)

        @pl.loop(0, N_OWN)
        def _(tile):
            @pl.when(self.owner_z(tile) != p.z)
            def _():
                self.z_copy(tile).start()

    def z_to_all(self):
        p = self.p

        @pl.when(self.owner)
        def _():
            @pl.loop(1, N_Z)
            def _(step):
                self.z_arrival(lax.rem(p.z + step, N_Z)).wait_recv()

            def add(step, total):
                return total + self.zbuf[lax.rem(p.z + step, N_Z)].astype(jnp.float32)

            own = self.src[p.core, p.y, self.mine].astype(jnp.float32)
            total = lax.fori_loop(1, N_Z, add, own)
            self.res[p.core, p.y, self.mine] = total.astype(jnp.bfloat16)

            @pl.loop(1, N_Z)
            def _(step):
                self.zg_copy(lax.rem(p.z + step, N_Z), self.mine).start()

    def all_to_y(self):
        p = self.p

        @pl.loop(0, N_OWN)
        def _(tile):
            @pl.when(self.owner_z(tile) != p.z)
            def _():
                self.zg_copy(0, tile).wait_recv()

        for step in (2, 1, 3):
            self.yg_copy(step).start()
        self.cg_copy(p.y).start()

    def y_to_core(self):
        p = self.p
        for step in (1, 3, 2):
            self.yg_copy(step, True).wait_recv()
            self.cg_copy(lax.rem(p.y + step, N_Y)).start()

    def finish(self):
        p = self.p
        for y in range(N_Y):
            self.cg_copy(y, True).wait_recv()
        self.core_copy().wait_send()
        for step in (1, 2, 3):
            self.y_copy(step).wait_send()
            self.yg_copy(step).wait_send()
        for y in range(N_Y):
            self.cg_copy(y).wait_send()

        @pl.loop(0, N_OWN)
        def _(tile):
            @pl.when(self.owner_z(tile) != p.z)
            def _():
                self.z_copy(tile).wait_send()

        @pl.when(self.owner)
        def _():
            @pl.loop(1, N_Z)
            def _(step):
                self.zg_copy(lax.rem(p.z + step, N_Z), self.mine).wait_send()


def dot(a, b):
    return lax.dot_general(a, b, (((1,), (0,)), ((), ())), preferred_element_type=jnp.float32)


def dot_rows(a, b):
    return lax.dot_general(a, b, (((1,), (1,)), ((), ())), preferred_element_type=jnp.float32)


def dot_cells(a, b):
    return lax.dot_general(a, b, (((0,), (0,)), ((), ())), preferred_element_type=jnp.float32)


def half(values):
    return values.astype(jnp.bfloat16)


def wide(values):
    return values.astype(jnp.float32)


class Halo:
    def __init__(self, place, ref, sems, by_block):
        self.p, self.ref, self.sems, self.by_block = place, ref, sems, by_block

    def message(self, index, block, src_rows, dst_block, dst_rows, step_lat, step_lon):
        src = self.ref.at[block, pl.ds(*src_rows)]
        dst = self.ref.at[dst_block, pl.ds(*dst_rows)]
        device = self.p.beside(step_lat, step_lon)
        return remote(src, dst, self.sems.at[0, index], self.sems.at[1, index], device)

    def north(self, block):
        at = block + 1 if self.by_block else pl.ds(1, 4)
        return self.message(block, at, (48, 48), at, (112, 48), -1, 0)

    def south(self, block):
        at = block + 1 if self.by_block else pl.ds(1, 4)
        return self.message(4 + block, at, (64, 48), at, (0, 48), 1, 0)

    def side(self, row, east):
        src_rows, dst_rows = {0: ((48, 64), (48, 64)), -1: ((48, 48), (112, 48)), 1: ((64, 48), (0, 48))}[row]
        index = 8 + 2 * (row % 3) + east
        return self.message(index, 4 if east else 1, src_rows, 0 if east else 5, dst_rows, row, 1 if east else -1)

    def when(self, row, then):
        if row == -1:
            pl.when(self.p.lat > 0)(then)
        elif row == 1:
            pl.when(self.p.lat < N_LAT - 1)(then)
        else:
            then()

    def send_rows(self, block):
        self.when(-1, lambda: self.north(block).start())
        self.when(1, lambda: self.south(block).start())

    def send_side(self, east):
        for row in (0, -1, 1):
            self.when(row, lambda row=row: self.side(row, east).start())

    def send_all(self):
        self.send_rows(0)
        self.send_side(0)
        self.send_side(1)

    def blocks(self):
        return range(4) if self.by_block else range(1)

    def wait_all(self):
        for block in self.blocks():
            self.when(1, lambda block=block: self.north(block).wait_recv())
            self.when(-1, lambda block=block: self.south(block).wait_recv())
        for east in (0, 1):
            for row in (0, -1, 1):
                self.when(-row, lambda row=row, east=east: self.side(row, east).wait_recv())

    def wait_sent(self):
        for block in self.blocks():
            self.when(-1, lambda block=block: self.north(block).wait_send())
            self.when(1, lambda block=block: self.south(block).wait_send())
        for east in (0, 1):
            for row in (0, -1, 1):
                self.when(row, lambda row=row, east=east: self.side(row, east).wait_send())


class Spread:
    def __init__(self, place, src, dst, sems):
        self.p, self.src, self.dst, self.sems = place, src, dst, sems

    def copy(self, head):
        src = self.src.at[head] if len(self.src.shape) == 3 else self.src
        return remote(
            src, self.dst.at[self.p.head], self.sems.at[0, head], self.sems.at[1, self.p.head], self.p.peer(head)
        )

    def arrival(self, head):
        src = self.src.at[head] if len(self.src.shape) == 3 else self.src
        return remote(src, self.dst.at[head], self.sems.at[0, head], self.sems.at[1, head], self.p.peer(head))

    def other(self, step):
        return lax.rem(self.p.head + step, N_HEAD)

    def wait_sent(self):
        for step in (1, 2, 3):
            self.copy(self.other(step)).wait_send()


def geometry(shape):
    row = lax.broadcasted_iota(jnp.int32, shape, 0)
    lane = lax.broadcasted_iota(jnp.int32, shape, 1)
    block = jnp.where(lane >= TALL, 1, 0) + jnp.where(lane >= 2 * TALL, 1, 0)
    rest = lane - TALL * block
    lat = (rest >> 3) - REACH
    step_lat = lat - (row >> 3)
    step_lon = (block - 1) * 8 + (rest & 7) - (row & 7)
    return lat, step_lat, step_lon


def put(src, t, top, values):
    for row in range(0, values.shape[0], t):
        y, third = (top + row) // (3 * t), (top + row) // t % 3
        for column in range(6):
            src[column // 3, y, third * 3 + column % 3] = half(
                values[row : row + t, column * 128 : column * 128 + 128]
            )


def take(res, t, top, out_ref, out_top, rows):
    for row in range(0, rows, t):
        y, third = (top + row) // (3 * t), (top + row) // t % 3
        for column in range(6):
            out_ref[out_top + row : out_top + row + t, column * 128 : column * 128 + 128] = res[
                column // 3, y, third * 3 + column % 3
            ]


T = 32
N_SUM = 11


def block_kernel(
    x_ref, gy_ref, wqkv_ref, wo_ref, valid_ref, mixed_ref, gx_ref, gqkv_ref, gwo_ref,
    ng, gg, norm32, spread, wp, wop, ext, flags, stats, mask_q, mask_k, gp, pvs, pvr, gns, gnr,
    sem_n, sem_g, sem_pv, sem_gn, sem_ext, sem_flags, sem_stats, *sums,
):
    p = Place()
    barrier = pltpu.get_barrier_semaphore()

    def greet(device):
        pl.semaphore_signal(barrier, inc=1, device_id=device, device_id_type=MESH)

    for step in range(1, N_HEAD):
        greet(p.peer(lax.rem(p.head + step, N_HEAD)))
    for step_lon in (-1, 0, 1):
        if step_lon:
            greet(p.beside(0, step_lon))

        @pl.when(p.lat > 0)
        def _():
            greet(p.beside(-1, step_lon))

        @pl.when(p.lat < N_LAT - 1)
        def _():
            greet(p.beside(1, step_lon))

    for step in range(1, N_Y):
        greet(p.at(y=lax.rem(p.y + step, N_Y)))

    @pl.loop(1, N_Z)
    def _(step):
        greet(p.at(z=lax.rem(p.z + step, N_Z)))

    early = Summed(p, 0, *sums[:N_SUM])
    late = Summed(p, 8, *sums[N_SUM:])
    normed_gather = Spread(p, ng.at[p.head], ng, sem_n)
    grad_gather = Spread(p, gg.at[p.head], gg, sem_g)
    halo = Halo(p, ext, sem_ext, True)
    flag_halo = Halo(p, flags, sem_flags, False)
    stat_halo = Halo(p, stats, sem_stats, False)

    gg[p.head] = gy_ref[...]
    values = wide(x_ref[...])
    center = values - jnp.mean(values, axis=-1, keepdims=True)
    inv = lax.rsqrt(jnp.mean(center * center, axis=-1, keepdims=True) + EPSILON)
    norm32[...] = center * inv
    spread[...] = jnp.broadcast_to(inv, spread.shape)
    ng[p.head] = half(center * inv)
    for top, at_edge in ((0, p.lat == 0), (112, p.lat == N_LAT - 1)):

        @pl.when(at_edge)
        def _():
            for ref in (ext, flags, stats):
                ref[:, top : top + 48, :] = jnp.zeros((6, 48, ref.shape[2]), jnp.bfloat16)

    row = lax.broadcasted_iota(jnp.int32, (CELLS, 8), 0)
    column = lax.broadcasted_iota(jnp.int32, (CELLS, 8), 1)
    by_lat = dot(half(jnp.where((row >> 3) == column, 1.0, 0.0)), half(wide(valid_ref[...])))
    row = lax.broadcasted_iota(jnp.int32, (CELLS, N_LON), 0)
    column = lax.broadcasted_iota(jnp.int32, (CELLS, N_LON), 1)
    for block in range(4):
        own_flag = half(jnp.where(column == 8 * block + (row & 7), by_lat, 0.0))
        flags[block + 1, 48:112] = half(dot(own_flag, jnp.ones((N_LON, 128), jnp.bfloat16)))

    greeted = 3 + 2 + 1 + (N_Y - 1) + (N_Z - 1) - 1
    edge = jnp.where(p.lat > 0, 3, 0) + jnp.where(p.lat < N_LAT - 1, 3, 0)
    pl.semaphore_wait(barrier, greeted + edge)

    for step in (1, 3, 2):
        normed_gather.copy(normed_gather.other(step)).start()
        grad_gather.copy(grad_gather.other(step)).start()
    flag_halo.send_all()

    nothing = jnp.zeros((64, FULL), jnp.bfloat16)
    for part in range(3):
        wp[128 * part : 128 * part + 128] = wqkv_ref[part, 0:128]
    wp[384:448] = wqkv_ref[0, 128:192]
    wp[448:512] = nothing
    wp[512:576] = wqkv_ref[1, 128:192]
    wp[576:640] = wqkv_ref[2, 128:192]
    wop[0:128] = wo_ref[0:128]
    wop[128:192] = nothing
    wop[192:256] = wo_ref[128:192]

    lat, step_lat, step_lon = geometry((CELLS, AROUND))
    inside = (jnp.abs(step_lat) <= REACH) & (jnp.abs(step_lon) <= REACH)
    middle = (step_lat == 0) & (step_lon == 0)
    there = lat + p.lat * 8
    inside_rows = inside & (there >= 0) & (there < 8 * N_LAT)
    for block in range(4):
        own_flag = wide(flags[block + 1, 48:112])[:, 0:1]
        mask_k[block] = jnp.where(inside_rows & ((own_flag > 0) | middle), 0.0, NEGATIVE)

    low = lax.broadcasted_iota(jnp.int32, (CELLS, 128), 1) < HEAD_SIZE
    zero = jnp.zeros((CELLS, 128), jnp.bfloat16)
    lane = lax.broadcasted_iota(jnp.int32, (CELLS, 128), 1)

    def first(values):
        return jnp.where(low, values, zero)

    def second(values):
        return jnp.where(low, zero, values)

    @pl.loop(0, N_HEAD)
    def _(step):
        order = jnp.where(step == 2, 3, jnp.where(step == 3, 2, step))
        block = lax.rem(p.head + order, N_HEAD)

        @pl.when(step > 0)
        def _():
            normed_gather.arrival(block).wait_recv()
            grad_gather.arrival(block).wait_recv()

        projected = dot_rows(ng[block], wp[...])
        d_attended = dot_rows(gg[block], wop[...])
        scale = HEAD_SIZE ** (-0.5)
        ext[block + 1, 48:112, 0:128] = half(half(projected[:, 0:128]) * scale)
        ext[block + 1, 48:112, 128:384] = half(projected[:, 128:384])
        ext[block + 1, 48:112, 384:512] = half(d_attended[:, 0:128])
        ext[block + 1, 48:112, 512:640] = jnp.where(
            low, half(projected[:, 384:512] * scale), half(d_attended[:, 128:256])
        )
        ext[block + 1, 48:112, 640:768] = half(projected[:, 512:640])
        halo.send_rows(block)

        @pl.when(block == 0)
        def _():
            halo.send_side(0)

        @pl.when(block == 3)
        def _():
            halo.send_side(1)

    flag_halo.wait_all()
    ones = half(jnp.where(lane == 0, 1.0, 0.0))
    for block in range(4):
        flag = dot_rows(ones, flags[block : block + 3].reshape(AROUND, 128))
        mask_q[block] = jnp.where(inside & ((flag > 0) | middle), 0.0, NEGATIVE)
    halo.wait_all()

    def stacked(a, b, c):
        return jnp.concatenate(
            [jnp.concatenate(part, axis=1) for part in (a, b, c)],
            axis=0,
        )

    def thrice(mask):
        return jnp.concatenate([mask, mask, mask], axis=0)

    def around(block, *groups):
        parts = [
            (stats if g == 6 else ext)[pl.ds(block, 3), :, (0 if g == 6 else g * 128) : (0 if g == 6 else g * 128) + 128]
            for g in groups
        ]
        return jnp.concatenate([part.reshape(AROUND, 128) for part in parts], axis=1)

    def own(block, group):
        return ext[block + 1, 48:112, group * 128 : group * 128 + 128]

    @pl.loop(0, 4)
    def _(block):
        keys, values = around(block, 1, 5), around(block, 2, 5)
        q01, d01, qd2 = own(block, 0), own(block, 3), own(block, 4)
        queries = stacked((first(q01), zero), (second(q01), zero), (zero, first(qd2)))
        douts = stacked((first(d01), zero), (second(d01), zero), (zero, second(qd2)))
        score = dot_rows(queries, keys) + thrice(mask_q[block])
        best = jnp.max(score, axis=1, keepdims=True)
        chance = jnp.exp(score - best)
        total = jnp.sum(chance, axis=1, keepdims=True)
        level = best + jnp.log(total)
        chance = chance * (1.0 / total)
        inner = dot_rows(douts, values)
        carried = jnp.sum(chance * inner, axis=1, keepdims=True)
        soft_grad = half(chance * (inner - carried))
        attended = dot(half(chance), values)
        grad_query = dot(soft_grad, keys) * HEAD_SIZE ** (-0.5)
        gp[block, :, 640:768] = half(jnp.where(low, attended[0:64, 0:128], attended[64:128, 0:128]))
        gp[block, :, 0:128] = half(jnp.where(low, grad_query[0:64, 0:128], grad_query[64:128, 0:128]))
        gp[block, :, 384:512] = half(jnp.where(low, grad_query[128:192, 128:256], attended[128:192, 128:256]))
        tile = jnp.zeros((CELLS, 128), jnp.float32)
        for kind, column in enumerate((level, carried)):
            for head in range(3):
                rest = column[64 * head : 64 * head + 64]
                for digit in range(3):
                    piece = wide(half(rest))
                    rest = rest - piece
                    tile = jnp.where(lane == 9 * kind + 3 * head + digit, piece, tile)
        stats[block + 1, 48:112] = half(tile)

    stat_halo.send_all()

    def cells(ref, *groups):
        return jnp.concatenate([ref[:, :, g * 128 : g * 128 + 128].reshape(4 * CELLS, 128) for g in groups], axis=1)

    grads = gg[...].reshape(4 * CELLS, FULL)
    normed = ng[...].reshape(4 * CELLS, FULL)
    mixed_in = cells(gp, 5, 3)
    weights = dot_cells(mixed_in, grads)
    put(early.src, T, 0, weights[0:128])
    put(early.src, T, 128, weights[192:256])
    weights = dot_cells(cells(gp, 0, 3), normed)
    put(early.src, T, 192, weights[0:192])
    early.send_core()

    out_spread = Spread(p, pvs, pvr, sem_pv)
    pvs[...] = half(dot(mixed_in, wop[...])).reshape(4, CELLS, FULL)
    for step in (2, 1, 3):
        out_spread.copy(out_spread.other(step)).start()
    early.core_to_y()

    stat_halo.wait_all()

    def minus_one(start):
        return half(jnp.where((lane >= start) & (lane < start + 3), -1.0, 0.0))

    def keys_side(block):
        queries, douts = around(block, 0, 4, 6), around(block, 3, 4, 6)
        k01, v01, kv2 = own(block, 1), own(block, 2), own(block, 5)
        keys = stacked(
            (first(k01), zero, minus_one(0)), (second(k01), zero, minus_one(3)), (zero, first(kv2), minus_one(6))
        )
        values = stacked(
            (first(v01), zero, minus_one(9)), (second(v01), zero, minus_one(12)), (zero, second(kv2), minus_one(15))
        )
        chance = jnp.exp(dot_rows(keys, queries) + thrice(mask_k[block]))
        soft_grad = half(chance * dot_rows(values, douts))
        grad_key = dot(soft_grad, queries[:, 0:256])
        grad_value = dot(half(chance), douts[:, 0:256])
        gp[block, :, 128:256] = half(jnp.where(low, grad_key[0:64, 0:128], grad_key[64:128, 0:128]))
        gp[block, :, 256:384] = half(jnp.where(low, grad_value[0:64, 0:128], grad_value[64:128, 0:128]))
        gp[block, :, 512:640] = half(jnp.where(low, grad_key[128:192, 128:256], grad_value[128:192, 128:256]))

    pl.loop(0, 2)(keys_side)
    early.y_to_z()
    pl.loop(2, 4)(keys_side)

    weights = dot_cells(cells(gp, 1, 4), normed)
    put(late.src, T, 0, weights[0:192])
    weights = jnp.concatenate([dot_cells(cells(gp, 2), normed), weights[192:256]], axis=0)
    put(late.src, T, 192, weights)
    late.send_core()

    norm_spread = Spread(p, gns, gnr, sem_gn)
    gns[...] = half(dot(cells(gp, 0, 1, 2, 3, 4), wp[...])).reshape(4, CELLS, FULL)
    for step in (2, 1, 3):
        norm_spread.copy(norm_spread.other(step)).start()

    early.z_to_all()
    late.core_to_y()

    total = wide(pvs[p.head])
    for step in (1, 2, 3):
        other = out_spread.other(step)
        out_spread.arrival(other).wait_recv()
        total = total + wide(pvr[other])
    mixed_ref[...] = half(wide(x_ref[...]) + total)

    early.all_to_y()
    late.y_to_z()

    total = wide(gns[p.head])
    for step in (1, 2, 3):
        other = norm_spread.other(step)
        norm_spread.arrival(other).wait_recv()
        total = total + wide(gnr[other])
    own_norm = norm32[...]
    mean = jnp.mean(total, axis=-1, keepdims=True)
    along = jnp.mean(total * own_norm, axis=-1, keepdims=True)
    d_input = spread[:, 0:1] * (total - mean - own_norm * along)
    gx_ref[...] = half(wide(gy_ref[...]) + d_input)

    late.z_to_all()
    early.y_to_core()
    late.all_to_y()
    early.finish()
    take(early.res, T, 0, gwo_ref, 0, 192)
    take(early.res, T, 192, gqkv_ref, 0, 192)
    late.y_to_core()
    for spread_copy in (normed_gather, grad_gather, out_spread, norm_spread):
        spread_copy.wait_sent()
    for one in (halo, flag_halo, stat_halo):
        one.wait_sent()
    late.finish()
    take(late.res, T, 0, gqkv_ref, 192, 384)


def on_device(activations, qkv_weight, out_weight, valid, grad_y):
    bf, f32 = jnp.bfloat16, jnp.float32
    vmem = pl.BlockSpec(memory_space=pltpu.VMEM)
    gathered = pltpu.VMEM((N_HEAD, CELLS, FULL), bf)
    pair = pltpu.SemaphoreType.DMA((2, N_HEAD))
    around = pltpu.SemaphoreType.DMA((2, 14))
    mixed, grad_x, grad_qkv, grad_out = pl.pallas_call(
        block_kernel,
        out_shape=[
            jax.ShapeDtypeStruct((CELLS, FULL), bf),
            jax.ShapeDtypeStruct((CELLS, FULL), bf),
            jax.ShapeDtypeStruct((3 * 192, FULL), bf),
            jax.ShapeDtypeStruct((192, FULL), bf),
        ],
        in_specs=[vmem] * 5,
        out_specs=[vmem] * 4,
        scratch_shapes=[
            gathered,
            gathered,
            pltpu.VMEM((CELLS, FULL), f32),
            pltpu.VMEM((CELLS, 128), f32),
            pltpu.VMEM((640, FULL), bf),
            pltpu.VMEM((256, FULL), bf),
            pltpu.VMEM((6, TALL, FULL), bf),
            pltpu.VMEM((6, TALL, 128), bf),
            pltpu.VMEM((6, TALL, 128), bf),
            pltpu.VMEM((4, CELLS, AROUND), f32),
            pltpu.VMEM((4, CELLS, AROUND), f32),
            gathered,
            gathered,
            gathered,
            gathered,
            gathered,
            pair,
            pair,
            pair,
            pair,
            around,
            around,
            around,
            *Summed.scratch(T),
            *Summed.scratch(T),
        ],
        compiler_params=pltpu.CompilerParams(
            collective_id=0, has_side_effects=True, vmem_limit_bytes=48 * 2**20
        ),
    )(
        activations.reshape(CELLS, FULL),
        grad_y.reshape(CELLS, FULL),
        qkv_weight,
        out_weight,
        valid,
    )
    return (
        mixed.reshape(activations.shape),
        grad_x.reshape(activations.shape),
        grad_qkv.reshape(qkv_weight.shape),
        grad_out,
    )


def solution(mesh):
    return jax.shard_map(
        on_device,
        mesh=mesh,
        in_specs=(
            P("lat", ("lon", "head"), None),
            P(None, "head", None),
            P("head", None),
            P("lat", "lon"),
            P("lat", ("lon", "head"), None),
        ),
        out_specs=(
            P("lat", ("lon", "head"), None),
            P("lat", ("lon", "head"), None),
            P(None, "head", None),
            P("head", None),
        ),
        check_vma=False,
    )
```

```python
import jax
import jax.numpy as jnp
from jax import lax
from jax.experimental import pallas as pl
from jax.experimental.pallas import tpu as pltpu
from jax.sharding import PartitionSpec as P

MESH = pl.DeviceIdType.MESH
HEAD_SIZE = 64
REACH = 6
EPSILON = 1e-05
NEGATIVE = -1e30
N_HEAD = 4
N_LAT = 4
N_LON = 32
CELLS = 64
FULL = 768
TALL = 160
AROUND = 3 * TALL
N_Z = 16
N_Y = 4
N_OWN = 9


class Place:
    def __init__(self):
        self.lat = lax.axis_index("lat")
        self.lon = lax.axis_index("lon")
        self.head = lax.axis_index("head")
        self.core = lax.rem(self.lat, 2)
        self.y = (self.lon // N_Z) * 2 + self.lat // 2
        self.z = lax.rem(self.lon, N_Z)

    def at(self, core=None, y=None, z=None):
        core = self.core if core is None else core
        y = self.y if y is None else y
        z = self.z if z is None else z
        return (lax.rem(y, 2) * 2 + core, (y // 2) * N_Z + z, self.head)


    def beside(self, step_lat, step_lon):
        return (self.lat + step_lat, lax.rem(self.lon + step_lon + N_LON, N_LON), self.head)

    def peer(self, head):
        return (self.lat, self.lon, head)


def remote(src, dst, send_sem, recv_sem, device):
    return pltpu.make_async_remote_copy(
        src_ref=src,
        dst_ref=dst,
        send_sem=send_sem,
        recv_sem=recv_sem,
        device_id=device,
        device_id_type=MESH,
    )


class Summed:
    def __init__(self, place, turn, src, res, cbuf, ybuf, zbuf, sem_c, sem_y, sem_z, sem_zg, sem_yg, sem_cg):
        self.p = place
        self.src, self.res, self.cbuf, self.ybuf, self.zbuf = src, res, cbuf, ybuf, zbuf
        self.sem_c, self.sem_y, self.sem_z = sem_c, sem_y, sem_z
        self.sem_zg, self.sem_yg, self.sem_cg = sem_zg, sem_yg, sem_cg
        self.turn = turn
        turned = lax.rem(place.z + N_Z - turn, N_Z)
        self.mine = (turned * N_OWN + N_Z - 1) // N_Z
        self.owner = (self.mine * N_Z) // N_OWN == turned
        self.mine = jnp.minimum(self.mine, N_OWN - 1)

    @staticmethod
    def scratch(t):
        bf = jnp.bfloat16
        return [
            pltpu.VMEM((2, N_Y, N_OWN, t, 128), bf),
            pltpu.VMEM((2, N_Y, N_OWN, t, 128), bf),
            pltpu.VMEM((N_Y, N_OWN, t, 128), bf),
            pltpu.VMEM((N_Y, N_OWN, t, 128), bf),
            pltpu.VMEM((N_Z, t, 128), bf),
            pltpu.SemaphoreType.DMA((2,)),
            pltpu.SemaphoreType.DMA((2, N_Y)),
            pltpu.SemaphoreType.DMA((2, N_Z)),
            pltpu.SemaphoreType.DMA((2, N_Z)),
            pltpu.SemaphoreType.DMA((2, N_Y)),
            pltpu.SemaphoreType.DMA((2, N_Y)),
        ]

    def core_copy(self):
        p = self.p
        return remote(
            self.src.at[1 - p.core], self.cbuf, self.sem_c.at[0], self.sem_c.at[1], p.at(core=1 - p.core)
        )

    def y_copy(self, step, arriving=False):
        p = self.p
        y = lax.rem(p.y + step, N_Y)
        slot = y if arriving else p.y
        return remote(
            self.src.at[p.core, y], self.ybuf.at[slot], self.sem_y.at[0, y], self.sem_y.at[1, slot], p.at(y=y)
        )

    def owner_z(self, tile):
        return lax.rem((tile * N_Z) // N_OWN + self.turn, N_Z)

    def z_copy(self, tile):
        p = self.p
        return remote(
            self.src.at[p.core, p.y, tile],
            self.zbuf.at[p.z],
            self.sem_z.at[0, tile],
            self.sem_z.at[1, p.z],
            p.at(z=self.owner_z(tile)),
        )

    def z_arrival(self, z):
        p = self.p
        return remote(
            self.src.at[p.core, p.y, 0], self.zbuf.at[z], self.sem_z.at[0, 0], self.sem_z.at[1, z], p.at(z=z)
        )

    def zg_copy(self, z, tile):
        p = self.p
        here = self.res.at[p.core, p.y, tile]
        return remote(here, here, self.sem_zg.at[0, z], self.sem_zg.at[1, tile], p.at(z=z))

    def yg_copy(self, step, arriving=False):
        p = self.p
        y = lax.rem(p.y + step, N_Y)
        slot = y if arriving else p.y
        here = self.res.at[p.core, slot]
        return remote(here, here, self.sem_yg.at[0, y], self.sem_yg.at[1, slot], p.at(y=y))

    def cg_copy(self, y, arriving=False):
        p = self.p
        here = self.res.at[1 - p.core if arriving else p.core, y]
        return remote(here, here, self.sem_cg.at[0, y], self.sem_cg.at[1, y], p.at(core=1 - p.core))

    def send_core(self):
        self.core_copy().start()

    def core_to_y(self):
        p = self.p
        self.core_copy().wait_recv()
        for step in (2, 1, 3, 0):
            y = lax.rem(p.y + step, N_Y)
            both = self.src[p.core, y].astype(jnp.float32) + self.cbuf[y].astype(jnp.float32)
            self.src[p.core, y] = both.astype(jnp.bfloat16)
            if step:
                self.y_copy(step).start()

    def y_to_z(self):
        p = self.p
        for step in (1, 3, 2):
            self.y_copy(step, True).wait_recv()
        total = self.src[p.core, p.y].astype(jnp.float32)
        for step in (1, 2, 3):
            total = total + self.ybuf[lax.rem(p.y + step, N_Y)].astype(jnp.float32)
        self.src[p.core, p.y] = total.astype(jnp.bfloat16)

        @pl.loop(0, N_OWN)
        def _(tile):
            @pl.when(self.owner_z(tile) != p.z)
            def _():
                self.z_copy(tile).start()

    def z_to_all(self):
        p = self.p

        @pl.when(self.owner)
        def _():
            @pl.loop(1, N_Z)
            def _(step):
                self.z_arrival(lax.rem(p.z + step, N_Z)).wait_recv()

            def add(step, total):
                return total + self.zbuf[lax.rem(p.z + step, N_Z)].astype(jnp.float32)

            own = self.src[p.core, p.y, self.mine].astype(jnp.float32)
            total = lax.fori_loop(1, N_Z, add, own)
            self.res[p.core, p.y, self.mine] = total.astype(jnp.bfloat16)

            @pl.loop(1, N_Z)
            def _(step):
                self.zg_copy(lax.rem(p.z + step, N_Z), self.mine).start()

    def all_to_y(self):
        p = self.p

        @pl.loop(0, N_OWN)
        def _(tile):
            @pl.when(self.owner_z(tile) != p.z)
            def _():
                self.zg_copy(0, tile).wait_recv()

        for step in (2, 1, 3):
            self.yg_copy(step).start()
        self.cg_copy(p.y).start()

    def y_to_core(self):
        p = self.p
        for step in (1, 3, 2):
            self.yg_copy(step, True).wait_recv()
            self.cg_copy(lax.rem(p.y + step, N_Y)).start()

    def finish(self):
        p = self.p
        for y in range(N_Y):
            self.cg_copy(y, True).wait_recv()
        self.core_copy().wait_send()
        for step in (1, 2, 3):
            self.y_copy(step).wait_send()
            self.yg_copy(step).wait_send()
        for y in range(N_Y):
            self.cg_copy(y).wait_send()

        @pl.loop(0, N_OWN)
        def _(tile):
            @pl.when(self.owner_z(tile) != p.z)
            def _():
                self.z_copy(tile).wait_send()

        @pl.when(self.owner)
        def _():
            @pl.loop(1, N_Z)
            def _(step):
                self.zg_copy(lax.rem(p.z + step, N_Z), self.mine).wait_send()


def dot(a, b):
    return lax.dot_general(a, b, (((1,), (0,)), ((), ())), preferred_element_type=jnp.float32)


def dot_rows(a, b):
    return lax.dot_general(a, b, (((1,), (1,)), ((), ())), preferred_element_type=jnp.float32)


def dot_cells(a, b):
    return lax.dot_general(a, b, (((0,), (0,)), ((), ())), preferred_element_type=jnp.float32)


def half(values):
    return values.astype(jnp.bfloat16)


def wide(values):
    return values.astype(jnp.float32)


class Halo:
    def __init__(self, place, ref, sems, by_block):
        self.p, self.ref, self.sems, self.by_block = place, ref, sems, by_block

    def message(self, index, block, src_rows, dst_block, dst_rows, step_lat, step_lon):
        src = self.ref.at[block, pl.ds(*src_rows)]
        dst = self.ref.at[dst_block, pl.ds(*dst_rows)]
        device = self.p.beside(step_lat, step_lon)
        return remote(src, dst, self.sems.at[0, index], self.sems.at[1, index], device)

    def north(self, block):
        at = block + 1 if self.by_block else pl.ds(1, 4)
        return self.message(block, at, (48, 48), at, (112, 48), -1, 0)

    def south(self, block):
        at = block + 1 if self.by_block else pl.ds(1, 4)
        return self.message(4 + block, at, (64, 48), at, (0, 48), 1, 0)

    def side(self, row, east):
        src_rows, dst_rows = {0: ((48, 64), (48, 64)), -1: ((48, 48), (112, 48)), 1: ((64, 48), (0, 48))}[row]
        index = 8 + 2 * (row % 3) + east
        return self.message(index, 4 if east else 1, src_rows, 0 if east else 5, dst_rows, row, 1 if east else -1)

    def when(self, row, then):
        if row == -1:
            pl.when(self.p.lat > 0)(then)
        elif row == 1:
            pl.when(self.p.lat < N_LAT - 1)(then)
        else:
            then()

    def send_rows(self, block):
        self.when(-1, lambda: self.north(block).start())
        self.when(1, lambda: self.south(block).start())

    def send_side(self, east):
        for row in (0, -1, 1):
            self.when(row, lambda row=row: self.side(row, east).start())

    def send_all(self):
        self.send_rows(0)
        self.send_side(0)
        self.send_side(1)

    def blocks(self):
        return range(4) if self.by_block else range(1)

    def wait_all(self):
        for block in self.blocks():
            self.when(1, lambda block=block: self.north(block).wait_recv())
            self.when(-1, lambda block=block: self.south(block).wait_recv())
        for east in (0, 1):
            for row in (0, -1, 1):
                self.when(-row, lambda row=row, east=east: self.side(row, east).wait_recv())

    def wait_sent(self):
        for block in self.blocks():
            self.when(-1, lambda block=block: self.north(block).wait_send())
            self.when(1, lambda block=block: self.south(block).wait_send())
        for east in (0, 1):
            for row in (0, -1, 1):
                self.when(row, lambda row=row, east=east: self.side(row, east).wait_send())


class Spread:
    def __init__(self, place, src, dst, sems):
        self.p, self.src, self.dst, self.sems = place, src, dst, sems

    def copy(self, head):
        src = self.src.at[head] if len(self.src.shape) == 3 else self.src
        return remote(
            src, self.dst.at[self.p.head], self.sems.at[0, head], self.sems.at[1, self.p.head], self.p.peer(head)
        )

    def arrival(self, head):
        src = self.src.at[head] if len(self.src.shape) == 3 else self.src
        return remote(src, self.dst.at[head], self.sems.at[0, head], self.sems.at[1, head], self.p.peer(head))

    def other(self, step):
        return lax.rem(self.p.head + step, N_HEAD)

    def wait_sent(self):
        for step in (1, 2, 3):
            self.copy(self.other(step)).wait_send()


def geometry(shape):
    row = lax.broadcasted_iota(jnp.int32, shape, 0)
    lane = lax.broadcasted_iota(jnp.int32, shape, 1)
    block = jnp.where(lane >= TALL, 1, 0) + jnp.where(lane >= 2 * TALL, 1, 0)
    rest = lane - TALL * block
    lat = (rest >> 3) - REACH
    step_lat = lat - (row >> 3)
    step_lon = (block - 1) * 8 + (rest & 7) - (row & 7)
    return lat, step_lat, step_lon


def put(src, t, top, values):
    for row in range(0, values.shape[0], t):
        y, third = (top + row) // (3 * t), (top + row) // t % 3
        for column in range(6):
            src[column // 3, y, third * 3 + column % 3] = half(
                values[row : row + t, column * 128 : column * 128 + 128]
            )


def take(res, t, top, out_ref, out_top, rows):
    for row in range(0, rows, t):
        y, third = (top + row) // (3 * t), (top + row) // t % 3
        for column in range(6):
            out_ref[out_top + row : out_top + row + t, column * 128 : column * 128 + 128] = res[
                column // 3, y, third * 3 + column % 3
            ]


T = 32
N_SUM = 11


def block_kernel(
    x_ref, gy_ref, wqkv_ref, wo_ref, valid_ref, mixed_out, gx_out, gqkv_out, gwo_out,
    mixed_ref, gx_ref, gqkv_ref, gwo_ref, sem_out, xv, valid_v, ng, gg, norm32, spread, wp, wop, ext, dext, stats, mask_q, mask_k, gp, pvs, pvr, gns, gnr,
    sem_in, sem_n, sem_g, sem_pv, sem_gn, sem_ext, sem_dext, sem_stats, *sums,
):
    p = Place()
    barrier = pltpu.get_barrier_semaphore()
    loads = [
        pltpu.make_async_copy(src, dst, sem_in.at[index])
        for index, (src, dst) in enumerate(
            (
                (x_ref, xv),
                (valid_ref, valid_v),
                (gy_ref, gg.at[p.head]),
                (wqkv_ref.at[0, pl.ds(0, 128)], wp.at[pl.ds(0, 128)]),
                (wqkv_ref.at[1, pl.ds(0, 128)], wp.at[pl.ds(128, 128)]),
                (wqkv_ref.at[2, pl.ds(0, 128)], wp.at[pl.ds(256, 128)]),
                (wqkv_ref.at[0, pl.ds(128, 64)], wp.at[pl.ds(384, 64)]),
                (wqkv_ref.at[1, pl.ds(128, 64)], wp.at[pl.ds(512, 64)]),
                (wqkv_ref.at[2, pl.ds(128, 64)], wp.at[pl.ds(576, 64)]),
                (wo_ref.at[pl.ds(0, 128)], wop.at[pl.ds(0, 128)]),
                (wo_ref.at[pl.ds(128, 64)], wop.at[pl.ds(192, 64)]),
            )
        )
    ]

    query_rows, rest = pl.ds(0, 192), pl.ds(192, 384)
    mixed_store, gx_store, gwo_store, query_store, rest_store = [
        pltpu.make_async_copy(src, dst, sem_out.at[index])
        for index, (src, dst) in enumerate(
            (
                (mixed_ref, mixed_out),
                (gx_ref, gx_out),
                (gwo_ref, gwo_out),
                (gqkv_ref.at[query_rows], gqkv_out.at[query_rows]),
                (gqkv_ref.at[rest], gqkv_out.at[rest]),
            )
        )
    ]

    def greet(device):
        pl.semaphore_signal(barrier, inc=1, device_id=device, device_id_type=MESH)

    for load in loads:
        load.start()
    for step in range(1, N_HEAD):
        greet(p.peer(lax.rem(p.head + step, N_HEAD)))
    for step_lon in (-1, 0, 1):
        if step_lon:
            greet(p.beside(0, step_lon))

        @pl.when(p.lat > 0)
        def _():
            greet(p.beside(-1, step_lon))

        @pl.when(p.lat < N_LAT - 1)
        def _():
            greet(p.beside(1, step_lon))

    for step in range(1, N_Y):
        greet(p.at(y=lax.rem(p.y + step, N_Y)))

    @pl.loop(1, N_Z)
    def _(step):
        greet(p.at(z=lax.rem(p.z + step, N_Z)))

    early = Summed(p, 0, *sums[:N_SUM])
    late = Summed(p, 8, *sums[N_SUM:])
    normed_gather = Spread(p, ng.at[p.head], ng, sem_n)
    grad_gather = Spread(p, gg.at[p.head], gg, sem_g)
    halo = Halo(p, ext, sem_ext, True)
    dout_halo = Halo(p, dext, sem_dext, True)
    stat_halo = Halo(p, stats, sem_stats, False)

    loads[0].wait()
    values = wide(xv[...])
    center = values - jnp.mean(values, axis=-1, keepdims=True)
    inv = lax.rsqrt(jnp.mean(center * center, axis=-1, keepdims=True) + EPSILON)
    norm32[...] = center * inv
    spread[...] = jnp.broadcast_to(inv, spread.shape)
    ng[p.head] = half(center * inv)
    for top, at_edge in ((0, p.lat == 0), (112, p.lat == N_LAT - 1)):

        @pl.when(at_edge)
        def _():
            for ref in (ext, dext, stats):
                ref[:, top : top + 48, :] = jnp.zeros((6, 48, ref.shape[2]), jnp.bfloat16)

    loads[1].wait()
    low = lax.broadcasted_iota(jnp.int32, (CELLS, 128), 1) < HEAD_SIZE
    zero = jnp.zeros((CELLS, 128), jnp.bfloat16)
    lane = lax.broadcasted_iota(jnp.int32, (CELLS, 128), 1)
    lat, step_lat, step_lon = geometry((CELLS, AROUND))
    inside = (jnp.abs(step_lat) <= REACH) & (jnp.abs(step_lon) <= REACH)
    middle = (step_lat == 0) & (step_lon == 0)
    there = lat + p.lat * 8
    inside_rows = inside & (there >= 0) & (there < 8 * N_LAT)
    row = lax.broadcasted_iota(jnp.int32, (CELLS, 8), 0)
    column = lax.broadcasted_iota(jnp.int32, (CELLS, 8), 1)
    by_lat = dot(half(jnp.where((row >> 3) == column, 1.0, 0.0)), half(wide(valid_v[...])))
    row = lax.broadcasted_iota(jnp.int32, (CELLS, N_LON), 0)
    column = lax.broadcasted_iota(jnp.int32, (CELLS, N_LON), 1)
    for block in range(4):
        own_flag = half(jnp.where(column == 8 * block + (row & 7), by_lat, 0.0))
        flag = dot(own_flag, jnp.ones((N_LON, 128), jnp.bfloat16))
        ext[block + 1, 48:112, 512:640] = half(flag)
        mask_k[block] = jnp.where(inside_rows & ((flag[:, 0:1] > 0) | middle), 0.0, NEGATIVE)

    greeted = 3 + 2 + 1 + (N_Y - 1) + (N_Z - 1) - 1
    edge = jnp.where(p.lat > 0, 3, 0) + jnp.where(p.lat < N_LAT - 1, 3, 0)
    pl.semaphore_wait(barrier, greeted + edge)

    for step in (1, 3, 2):
        normed_gather.copy(normed_gather.other(step)).start()
    loads[2].wait()
    for step in (1, 3, 2):
        grad_gather.copy(grad_gather.other(step)).start()

    wp[448:512] = jnp.zeros((64, FULL), jnp.bfloat16)
    wop[128:192] = jnp.zeros((64, FULL), jnp.bfloat16)
    for load in loads[3:]:
        load.wait()

    def first(values):
        return jnp.where(low, values, zero)

    def second(values):
        return jnp.where(low, zero, values)

    def arrived(step, gather, margins, project):
        order = jnp.where(step == 2, 3, jnp.where(step == 3, 2, step))
        block = lax.rem(p.head + order, N_HEAD)

        @pl.when(step > 0)
        def _():
            gather.arrival(block).wait_recv()

        project(block)
        margins.send_rows(block)

        @pl.when(block == 0)
        def _():
            margins.send_side(0)

        @pl.when(block == 3)
        def _():
            margins.send_side(1)

    def project_normed(block):
        projected = dot_rows(ng[block], wp[...])
        scale = HEAD_SIZE ** (-0.5)
        ext[block + 1, 48:112, 0:128] = half(half(projected[:, 0:128]) * scale)
        ext[block + 1, 48:112, 128:384] = half(projected[:, 128:384])
        ext[block + 1, 48:112, 384:512] = half(projected[:, 512:640])
        ext[block + 1, 48:112, 512:640] = jnp.where(
            low, half(projected[:, 384:512] * scale), ext[block + 1, 48:112, 512:640]
        )

    def project_grad(block):
        dext[block + 1, 48:112] = half(dot_rows(gg[block], wop[...]))

    @pl.loop(0, N_HEAD)
    def _(step):
        arrived(step, normed_gather, halo, project_normed)

    @pl.loop(0, N_HEAD)
    def _(step):
        arrived(step, grad_gather, dout_halo, project_grad)

    halo.wait_all()
    pick = half(jnp.where(lane == HEAD_SIZE, 1.0, 0.0))
    for block in range(4):
        flag = dot_rows(pick, ext[block : block + 3, :, 512:640].reshape(AROUND, 128))
        mask_q[block] = jnp.where(inside & ((flag > 0) | middle), 0.0, NEGATIVE)
    dout_halo.wait_all()

    def stacked(a, b, c):
        return jnp.concatenate(
            [jnp.concatenate(part, axis=1) for part in (a, b, c)],
            axis=0,
        )

    def thrice(mask):
        return jnp.concatenate([mask, mask, mask], axis=0)

    def around(block, *groups):
        parts = [
            ref[pl.ds(block, 3), :, group * 128 : group * 128 + 128].reshape(AROUND, 128) for ref, group in groups
        ]
        return jnp.concatenate(parts, axis=1)

    def own(block, ref, group):
        return ref[block + 1, 48:112, group * 128 : group * 128 + 128]

    Q01, K01, V01, KV2, Q2 = ((ext, group) for group in range(5))
    D01, D2 = (dext, 0), (dext, 1)
    STAT = (stats, 0)

    @pl.loop(0, 4)
    def _(block):
        keys, values = around(block, K01, KV2), around(block, V01, KV2)
        q01, d01 = own(block, *Q01), own(block, *D01)
        queries = stacked((first(q01), zero), (second(q01), zero), (zero, first(own(block, *Q2))))
        douts = stacked((first(d01), zero), (second(d01), zero), (zero, own(block, *D2)))
        score = dot_rows(queries, keys) + thrice(mask_q[block])
        best = jnp.max(score, axis=1, keepdims=True)
        chance = jnp.exp(score - best)
        total = jnp.sum(chance, axis=1, keepdims=True)
        level = best + jnp.log(total)
        chance = chance * (1.0 / total)
        inner = dot_rows(douts, values)
        carried = jnp.sum(chance * inner, axis=1, keepdims=True)
        soft_grad = half(chance * (inner - carried))
        attended = dot(half(chance), values)
        grad_query = dot(soft_grad, keys) * HEAD_SIZE ** (-0.5)
        gp[block, :, 640:768] = half(jnp.where(low, attended[0:64, 0:128], attended[64:128, 0:128]))
        gp[block, :, 0:128] = half(jnp.where(low, grad_query[0:64, 0:128], grad_query[64:128, 0:128]))
        gp[block, :, 384:512] = half(jnp.where(low, grad_query[128:192, 128:256], attended[128:192, 128:256]))
        tile = jnp.zeros((CELLS, 128), jnp.float32)
        for kind, column in enumerate((level, carried)):
            for head in range(3):
                rest = column[64 * head : 64 * head + 64]
                for digit in range(3):
                    piece = wide(half(rest))
                    rest = rest - piece
                    tile = jnp.where(lane == 9 * kind + 3 * head + digit, piece, tile)
        stats[block + 1, 48:112] = half(tile)

    stat_halo.send_all()

    def cells(ref, *groups):
        return jnp.concatenate([ref[:, :, g * 128 : g * 128 + 128].reshape(4 * CELLS, 128) for g in groups], axis=1)

    grads = gg[...].reshape(4 * CELLS, FULL)
    normed = ng[...].reshape(4 * CELLS, FULL)
    mixed_in = cells(gp, 5, 3)
    weights = dot_cells(mixed_in, grads)
    put(early.src, T, 0, weights[0:128])
    put(early.src, T, 128, weights[192:256])
    weights = dot_cells(cells(gp, 0, 3), normed)
    put(early.src, T, 192, weights[0:192])
    early.send_core()

    out_spread = Spread(p, pvs, pvr, sem_pv)
    pvs[...] = half(dot(mixed_in, wop[...])).reshape(4, CELLS, FULL)
    for step in (2, 1, 3):
        out_spread.copy(out_spread.other(step)).start()
    early.core_to_y()
    stat_halo.wait_all()

    def minus_one(start):
        return half(jnp.where((lane >= start) & (lane < start + 3), -1.0, 0.0))

    def keys_side(block):
        queries, douts = around(block, Q01, Q2, STAT), around(block, D01, D2, STAT)
        k01, v01, kv2 = own(block, *K01), own(block, *V01), own(block, *KV2)
        keys = stacked(
            (first(k01), zero, minus_one(0)), (second(k01), zero, minus_one(3)), (zero, first(kv2), minus_one(6))
        )
        values = stacked(
            (first(v01), zero, minus_one(9)), (second(v01), zero, minus_one(12)), (zero, second(kv2), minus_one(15))
        )
        chance = jnp.exp(dot_rows(keys, queries) + thrice(mask_k[block]))
        soft_grad = half(chance * dot_rows(values, douts))
        grad_key = dot(soft_grad, queries[:, 0:256])
        grad_value = dot(half(chance), douts[:, 0:256])
        gp[block, :, 128:256] = half(jnp.where(low, grad_key[0:64, 0:128], grad_key[64:128, 0:128]))
        gp[block, :, 256:384] = half(jnp.where(low, grad_value[0:64, 0:128], grad_value[64:128, 0:128]))
        gp[block, :, 512:640] = half(jnp.where(low, grad_key[128:192, 128:256], grad_value[128:192, 128:256]))

    pl.loop(0, 4)(keys_side)

    weights = dot_cells(cells(gp, 1, 4), normed)
    put(late.src, T, 0, weights[0:192])
    weights = jnp.concatenate([dot_cells(cells(gp, 2), normed), weights[192:256]], axis=0)
    put(late.src, T, 192, weights)
    late.send_core()
    early.y_to_z()

    norm_spread = Spread(p, gns, gnr, sem_gn)
    gns[...] = half(dot(cells(gp, 0, 1, 2, 3, 4), wp[...])).reshape(4, CELLS, FULL)
    for step in (2, 1, 3):
        norm_spread.copy(norm_spread.other(step)).start()

    late.core_to_y()
    early.z_to_all()

    total = wide(pvs[p.head])
    for step in (1, 2, 3):
        other = out_spread.other(step)
        out_spread.arrival(other).wait_recv()
        total = total + wide(pvr[other])
    mixed_ref[...] = half(wide(xv[...]) + total)
    mixed_store.start()

    late.y_to_z()
    early.all_to_y()

    total = wide(gns[p.head])
    for step in (1, 2, 3):
        other = norm_spread.other(step)
        norm_spread.arrival(other).wait_recv()
        total = total + wide(gnr[other])
    own_norm = norm32[...]
    mean = jnp.mean(total, axis=-1, keepdims=True)
    along = jnp.mean(total * own_norm, axis=-1, keepdims=True)
    d_input = spread[:, 0:1] * (total - mean - own_norm * along)
    gx_ref[...] = half(wide(gg[p.head]) + d_input)
    gx_store.start()

    late.z_to_all()
    early.y_to_core()
    for spread_copy in (normed_gather, grad_gather, out_spread, norm_spread):
        spread_copy.wait_sent()
    for one in (halo, dout_halo, stat_halo):
        one.wait_sent()
    late.all_to_y()
    early.finish()
    take(early.res, T, 0, gwo_ref, 0, 192)
    take(early.res, T, 192, gqkv_ref, 0, 192)
    gwo_store.start()
    query_store.start()
    late.y_to_core()
    late.finish()
    take(late.res, T, 0, gqkv_ref, 192, 384)
    rest_store.start()
    for store in (mixed_store, gx_store, gwo_store, query_store, rest_store):
        store.wait()


def store_kernel(*refs):
    given, out, held, sems = refs[:4], refs[4:8], refs[8:12], refs[12]
    loads = [pltpu.make_async_copy(given[i], held[i], sems.at[0, i]) for i in range(4)]
    stores = [pltpu.make_async_copy(held[i], out[i], sems.at[1, i]) for i in range(4)]
    for load in loads:
        load.start()
    for load, store in zip(loads, stores):
        load.wait()
        store.start()
    for store in stores:
        store.wait()


def on_device(activations, qkv_weight, out_weight, valid, grad_y):
    bf, f32 = jnp.bfloat16, jnp.float32
    gathered = pltpu.VMEM((N_HEAD, CELLS, FULL), bf)
    pair = pltpu.SemaphoreType.DMA((2, N_HEAD))
    around = pltpu.SemaphoreType.DMA((2, 14))
    results = pl.pallas_call(
        block_kernel,
        out_shape=[
            jax.ShapeDtypeStruct((CELLS, FULL), bf),
            jax.ShapeDtypeStruct((CELLS, FULL), bf),
            jax.ShapeDtypeStruct((3 * 192, FULL), bf),
            jax.ShapeDtypeStruct((192, FULL), bf),
        ],
        in_specs=[pl.BlockSpec(memory_space=pltpu.HBM)] * 5,
        out_specs=[pl.BlockSpec(memory_space=pltpu.HBM)] * 4,
        scratch_shapes=[
            pltpu.VMEM((CELLS, FULL), bf),
            pltpu.VMEM((CELLS, FULL), bf),
            pltpu.VMEM((3 * 192, FULL), bf),
            pltpu.VMEM((192, FULL), bf),
            pltpu.SemaphoreType.DMA((5,)),
            pltpu.VMEM((CELLS, FULL), bf),
            pltpu.VMEM((8, N_LON), jnp.int32),
            gathered,
            gathered,
            pltpu.VMEM((CELLS, FULL), f32),
            pltpu.VMEM((CELLS, 128), f32),
            pltpu.VMEM((640, FULL), bf),
            pltpu.VMEM((256, FULL), bf),
            pltpu.VMEM((6, TALL, 640), bf),
            pltpu.VMEM((6, TALL, 256), bf),
            pltpu.VMEM((6, TALL, 128), bf),
            pltpu.VMEM((4, CELLS, AROUND), f32),
            pltpu.VMEM((4, CELLS, AROUND), f32),
            gathered,
            gathered,
            gathered,
            gathered,
            gathered,
            pltpu.SemaphoreType.DMA((11,)),
            pair,
            pair,
            pair,
            pair,
            around,
            around,
            around,
            *Summed.scratch(T),
            *Summed.scratch(T),
        ],
        compiler_params=pltpu.CompilerParams(
            collective_id=0, has_side_effects=True, vmem_limit_bytes=63 * 2**20
        ),
    )(
        activations.reshape(CELLS, FULL),
        grad_y.reshape(CELLS, FULL),
        qkv_weight,
        out_weight,
        valid,
    )
    mixed, grad_x, grad_qkv, grad_out = pl.pallas_call(
        store_kernel,
        out_shape=[jax.ShapeDtypeStruct(result.shape, bf) for result in results],
        in_specs=[pl.BlockSpec(memory_space=pl.ANY)] * 4,
        out_specs=[pl.BlockSpec(memory_space=pltpu.HBM)] * 4,
        scratch_shapes=[
            *(pltpu.VMEM(result.shape, bf) for result in results),
            pltpu.SemaphoreType.DMA((2, 4)),
        ],
    )(*results)
    return (
        mixed.reshape(activations.shape),
        grad_x.reshape(activations.shape),
        grad_qkv.reshape(qkv_weight.shape),
        grad_out,
    )


def solution(mesh):
    return jax.shard_map(
        on_device,
        mesh=mesh,
        in_specs=(
            P("lat", ("lon", "head"), None),
            P(None, "head", None),
            P("head", None),
            P("lat", "lon"),
            P("lat", ("lon", "head"), None),
        ),
        out_specs=(
            P("lat", ("lon", "head"), None),
            P("lat", ("lon", "head"), None),
            P(None, "head", None),
            P("head", None),
        ),
        check_vma=False,
    )
```

```python
import jax
import jax.numpy as jnp
from jax import lax
from jax.experimental import pallas as pl
from jax.experimental.pallas import tpu as pltpu
from jax.sharding import PartitionSpec as P

MESH = pl.DeviceIdType.MESH
HEAD_SIZE = 64
REACH = 6
EPSILON = 1e-05
NEGATIVE = -1e30
N_HEAD = 4
N_LAT = 4
N_LON = 32
CELLS = 64
FULL = 768
TALL = 160
AROUND = 3 * TALL
N_Z = 16
N_Y = 4
NEAR = 4
CHUNK = 5
TILES = NEAR * CHUNK


class Place:
    def __init__(self):
        self.lat = lax.axis_index("lat")
        self.lon = lax.axis_index("lon")
        self.head = lax.axis_index("head")
        self.core = lax.rem(self.lat, 2)
        self.y = (self.lon // N_Z) * 2 + self.lat // 2
        self.z = lax.rem(self.lon, N_Z)

    def at(self, core=None, y=None, z=None):
        core = self.core if core is None else core
        y = self.y if y is None else y
        z = self.z if z is None else z
        return (lax.rem(y, 2) * 2 + core, (y // 2) * N_Z + z, self.head)


    def beside(self, step_lat, step_lon):
        return (self.lat + step_lat, lax.rem(self.lon + step_lon + N_LON, N_LON), self.head)

    def peer(self, head):
        return (self.lat, self.lon, head)


def remote(src, dst, send_sem, recv_sem, device):
    return pltpu.make_async_remote_copy(
        src_ref=src,
        dst_ref=dst,
        send_sem=send_sem,
        recv_sem=recv_sem,
        device_id=device,
        device_id_type=MESH,
    )


class Summed:
    def __init__(self, place, src, res, cbuf, ybuf, nbuf, fbuf, sem_c, sem_y, sem_n, sem_f, sem_ng, sem_yg, sem_cg):
        self.p = place
        self.src, self.res, self.cbuf, self.ybuf, self.nbuf, self.fbuf = src, res, cbuf, ybuf, nbuf, fbuf
        self.sem_c, self.sem_y, self.sem_n, self.sem_f = sem_c, sem_y, sem_n, sem_f
        self.sem_ng, self.sem_yg, self.sem_cg = sem_ng, sem_yg, sem_cg
        self.two = jnp.where(place.core == 0, 2, N_Z - 2)

    @staticmethod
    def scratch():
        bf = jnp.bfloat16
        sems = pltpu.SemaphoreType.DMA
        return [
            pltpu.VMEM((2, N_Y, TILES, 16, 128), bf),
            pltpu.VMEM((2, N_Y, TILES, 16, 128), bf),
            pltpu.VMEM((N_Y, TILES, 16, 128), bf),
            pltpu.VMEM((N_Y, TILES, 16, 128), bf),
            pltpu.VMEM((NEAR, CHUNK, 16, 128), bf),
            pltpu.VMEM((NEAR, CHUNK, 16, 128), bf),
            sems((2,)),
            sems((2, N_Y, NEAR)),
            sems((2, NEAR)),
            sems((2, NEAR)),
            sems((2, NEAR)),
            sems((2, N_Y, NEAR)),
            sems((2, N_Y)),
        ]

    def clear(self):
        for ref in (self.src,):
            ref[:, :, 18:TILES] = jnp.zeros((2, N_Y, TILES - 18, 16, 128), jnp.bfloat16)

    def chunk(self, away):
        return lax.rem(self.p.z + away, NEAR)

    def tiles(self, away):
        return pl.ds(CHUNK * self.chunk(away), CHUNK)

    def along(self, away):
        step = {1: 1, 2: self.two, 3: N_Z - 1}[away]
        return lax.rem(self.p.z + step, N_Z), lax.rem(self.p.z + N_Z - step, N_Z)

    def core_copy(self):
        p = self.p
        return remote(
            self.src.at[1 - p.core], self.cbuf, self.sem_c.at[0], self.sem_c.at[1], p.at(core=1 - p.core)
        )

    def y_copy(self, step, away, arriving=False):
        p = self.p
        y = lax.rem(p.y + step, N_Y)
        slot = y if arriving else p.y
        return remote(
            self.src.at[p.core, y, self.tiles(away)],
            self.ybuf.at[slot, self.tiles(away)],
            self.sem_y.at[0, y, away],
            self.sem_y.at[1, slot, away],
            p.at(y=y),
        )

    def near_copy(self, away):
        p = self.p
        there, _ = self.along(away)
        return remote(
            self.src.at[p.core, p.y, self.tiles(away)],
            self.nbuf.at[away],
            self.sem_n.at[0, away],
            self.sem_n.at[1, away],
            p.at(z=there),
        )

    def far_copy(self, step, arriving=False):
        p = self.p
        z = lax.rem(p.z + 4 * step, N_Z)
        slot = (z if arriving else p.z) // 4
        return remote(
            self.src.at[p.core, p.y, self.tiles(0)],
            self.fbuf.at[slot],
            self.sem_f.at[0, step],
            self.sem_f.at[1, slot],
            p.at(z=z),
        )

    def back_copy(self, away, arriving=False):
        p = self.p
        _, there = self.along(away)
        here = self.res.at[p.core, p.y, self.tiles(away if arriving else 0)]
        return remote(here, here, self.sem_ng.at[0, away], self.sem_ng.at[1, away], p.at(z=there))

    def yg_copy(self, step, away, arriving=False):
        p = self.p
        y = lax.rem(p.y + step, N_Y)
        slot = y if arriving else p.y
        here = self.res.at[p.core, slot, self.tiles(away)]
        return remote(here, here, self.sem_yg.at[0, y, away], self.sem_yg.at[1, slot, away], p.at(y=y))

    def cg_copy(self, y, arriving=False):
        p = self.p
        here = self.res.at[1 - p.core if arriving else p.core, y]
        return remote(here, here, self.sem_cg.at[0, y], self.sem_cg.at[1, y], p.at(core=1 - p.core))

    def send_core(self):
        self.core_copy().start()

    def core_to_y(self):
        p = self.p
        self.core_copy().wait_recv()
        for step in (2, 1, 3, 0):
            y = lax.rem(p.y + step, N_Y)
            both = self.src[p.core, y].astype(jnp.float32) + self.cbuf[y].astype(jnp.float32)
            self.src[p.core, y] = both.astype(jnp.bfloat16)
        for away in (2, 1, 3, 0):
            for step in (2, 1, 3):
                self.y_copy(step, away).start()

    def y_to_near(self):
        p = self.p
        for away in (2, 1, 3, 0):
            for step in (1, 3, 2):
                self.y_copy(step, away, True).wait_recv()
            tiles = self.tiles(away)
            total = self.src[p.core, p.y, tiles].astype(jnp.float32)
            for step in (1, 2, 3):
                total = total + self.ybuf[lax.rem(p.y + step, N_Y), tiles].astype(jnp.float32)
            self.src[p.core, p.y, tiles] = total.astype(jnp.bfloat16)
            if away:
                self.near_copy(away).start()

    def near_to_far(self):
        p = self.p
        total = self.src[p.core, p.y, self.tiles(0)].astype(jnp.float32)
        for away in (1, 3, 2):
            self.near_copy(away).wait_recv()
            total = total + self.nbuf[away].astype(jnp.float32)
        total = total.astype(jnp.bfloat16)
        self.src[p.core, p.y, self.tiles(0)] = total
        for step in (2, 1, 3):
            self.far_copy(step).start()
        self.fbuf[p.z // 4] = total

    def far_to_all(self):
        p = self.p
        for step in (1, 3, 2):
            self.far_copy(step, True).wait_recv()
        total = self.fbuf[0].astype(jnp.float32)
        for group in range(1, NEAR):
            total = total + self.fbuf[group].astype(jnp.float32)
        self.res[p.core, p.y, self.tiles(0)] = total.astype(jnp.bfloat16)
        for away in (2, 1, 3):
            self.back_copy(away).start()
        for step in (2, 1, 3):
            self.yg_copy(step, 0).start()

    def all_to_y(self):
        for away in (1, 3, 2):
            self.back_copy(away, True).wait_recv()
            for step in (2, 1, 3):
                self.yg_copy(step, away).start()
        self.cg_copy(self.p.y).start()

    def y_to_core(self):
        p = self.p
        for step in (1, 3, 2):
            for away in range(NEAR):
                self.yg_copy(step, away, True).wait_recv()
            self.cg_copy(lax.rem(p.y + step, N_Y)).start()

    def finish(self):
        for y in range(N_Y):
            self.cg_copy(y, True).wait_recv()

    def wait_sent(self):
        self.core_copy().wait_send()
        for step in (1, 2, 3):
            for away in range(NEAR):
                self.y_copy(step, away).wait_send()
                self.yg_copy(step, away).wait_send()
            self.near_copy(step).wait_send()
            self.far_copy(step).wait_send()
            self.back_copy(step).wait_send()
        for y in range(N_Y):
            self.cg_copy(y).wait_send()


def dot(a, b):
    return lax.dot_general(a, b, (((1,), (0,)), ((), ())), preferred_element_type=jnp.float32)


def dot_rows(a, b):
    return lax.dot_general(a, b, (((1,), (1,)), ((), ())), preferred_element_type=jnp.float32)


def dot_cells(a, b):
    return lax.dot_general(a, b, (((0,), (0,)), ((), ())), preferred_element_type=jnp.float32)


def half(values):
    return values.astype(jnp.bfloat16)


def wide(values):
    return values.astype(jnp.float32)


class Halo:
    def __init__(self, place, ref, sems, by_block):
        self.p, self.ref, self.sems, self.by_block = place, ref, sems, by_block

    def message(self, index, block, src_rows, dst_block, dst_rows, step_lat, step_lon):
        src = self.ref.at[block, pl.ds(*src_rows)]
        dst = self.ref.at[dst_block, pl.ds(*dst_rows)]
        device = self.p.beside(step_lat, step_lon)
        return remote(src, dst, self.sems.at[0, index], self.sems.at[1, index], device)

    def north(self, block):
        at = block + 1 if self.by_block else pl.ds(1, 4)
        return self.message(block, at, (48, 48), at, (112, 48), -1, 0)

    def south(self, block):
        at = block + 1 if self.by_block else pl.ds(1, 4)
        return self.message(4 + block, at, (64, 48), at, (0, 48), 1, 0)

    def side(self, row, east):
        src_rows, dst_rows = {0: ((48, 64), (48, 64)), -1: ((48, 48), (112, 48)), 1: ((64, 48), (0, 48))}[row]
        index = 8 + 2 * (row % 3) + east
        return self.message(index, 4 if east else 1, src_rows, 0 if east else 5, dst_rows, row, 1 if east else -1)

    def when(self, row, then):
        if row == -1:
            pl.when(self.p.lat > 0)(then)
        elif row == 1:
            pl.when(self.p.lat < N_LAT - 1)(then)
        else:
            then()

    def send_rows(self, block):
        self.when(-1, lambda: self.north(block).start())
        self.when(1, lambda: self.south(block).start())

    def send_side(self, east):
        for row in (0, -1, 1):
            self.when(row, lambda row=row: self.side(row, east).start())

    def send_all(self):
        self.send_rows(0)
        self.send_side(0)
        self.send_side(1)

    def blocks(self):
        return range(4) if self.by_block else range(1)

    def wait_all(self):
        for block in self.blocks():
            self.when(1, lambda block=block: self.north(block).wait_recv())
            self.when(-1, lambda block=block: self.south(block).wait_recv())
        for east in (0, 1):
            for row in (0, -1, 1):
                self.when(-row, lambda row=row, east=east: self.side(row, east).wait_recv())

    def wait_sent(self):
        for block in self.blocks():
            self.when(-1, lambda block=block: self.north(block).wait_send())
            self.when(1, lambda block=block: self.south(block).wait_send())
        for east in (0, 1):
            for row in (0, -1, 1):
                self.when(row, lambda row=row, east=east: self.side(row, east).wait_send())


class Spread:
    def __init__(self, place, src, dst, sems):
        self.p, self.src, self.dst, self.sems = place, src, dst, sems

    def copy(self, head):
        src = self.src.at[head] if len(self.src.shape) == 3 else self.src
        return remote(
            src, self.dst.at[self.p.head], self.sems.at[0, head], self.sems.at[1, self.p.head], self.p.peer(head)
        )

    def arrival(self, head):
        src = self.src.at[head] if len(self.src.shape) == 3 else self.src
        return remote(src, self.dst.at[head], self.sems.at[0, head], self.sems.at[1, head], self.p.peer(head))

    def other(self, step):
        return lax.rem(self.p.head + step, N_HEAD)

    def wait_sent(self):
        for step in (1, 2, 3):
            self.copy(self.other(step)).wait_send()


def geometry(shape):
    row = lax.broadcasted_iota(jnp.int32, shape, 0)
    lane = lax.broadcasted_iota(jnp.int32, shape, 1)
    block = jnp.where(lane >= TALL, 1, 0) + jnp.where(lane >= 2 * TALL, 1, 0)
    rest = lane - TALL * block
    lat = (rest >> 3) - REACH
    step_lat = lat - (row >> 3)
    step_lon = (block - 1) * 8 + (rest & 7) - (row & 7)
    return lat, step_lat, step_lon


def place_of(row, column):
    return column // 3, row // 96, row % 96 // 16 * 3 + column % 3


def put(src, top, values):
    for row in range(0, values.shape[0], 16):
        for column in range(6):
            src[place_of(top + row, column)] = half(values[row : row + 16, column * 128 : column * 128 + 128])


def take(res, top, out_ref, out_top, rows):
    for row in range(0, rows, 16):
        for column in range(6):
            out_ref[out_top + row : out_top + row + 16, column * 128 : column * 128 + 128] = res[
                place_of(top + row, column)
            ]


N_SUM = 13


def block_kernel(
    x_ref, gy_ref, wqkv_ref, wo_ref, valid_ref, mixed_out, gx_out, gqkv_out, gwo_out,
    mixed_ref, gx_ref, gqkv_ref, gwo_ref, sem_out, xv, valid_v, ng, gg, norm32, spread, wp, wop, ext, dext, stats, mask_q, mask_k, gp, pvs, pvr, gns, gnr,
    sem_in, sem_n, sem_g, sem_pv, sem_gn, sem_ext, sem_dext, sem_stats, *sums,
):
    p = Place()
    barrier = pltpu.get_barrier_semaphore()
    loads = [
        pltpu.make_async_copy(src, dst, sem_in.at[index])
        for index, (src, dst) in enumerate(
            (
                (x_ref, xv),
                (valid_ref, valid_v),
                (gy_ref, gg.at[p.head]),
                (wqkv_ref.at[0, pl.ds(0, 128)], wp.at[pl.ds(0, 128)]),
                (wqkv_ref.at[1, pl.ds(0, 128)], wp.at[pl.ds(128, 128)]),
                (wqkv_ref.at[2, pl.ds(0, 128)], wp.at[pl.ds(256, 128)]),
                (wqkv_ref.at[0, pl.ds(128, 64)], wp.at[pl.ds(384, 64)]),
                (wqkv_ref.at[1, pl.ds(128, 64)], wp.at[pl.ds(512, 64)]),
                (wqkv_ref.at[2, pl.ds(128, 64)], wp.at[pl.ds(576, 64)]),
                (wo_ref.at[pl.ds(0, 128)], wop.at[pl.ds(0, 128)]),
                (wo_ref.at[pl.ds(128, 64)], wop.at[pl.ds(192, 64)]),
            )
        )
    ]

    query_rows, rest = pl.ds(0, 192), pl.ds(192, 384)
    mixed_store, gx_store, gwo_store, query_store, rest_store = [
        pltpu.make_async_copy(src, dst, sem_out.at[index])
        for index, (src, dst) in enumerate(
            (
                (mixed_ref, mixed_out),
                (gx_ref, gx_out),
                (gwo_ref, gwo_out),
                (gqkv_ref.at[query_rows], gqkv_out.at[query_rows]),
                (gqkv_ref.at[rest], gqkv_out.at[rest]),
            )
        )
    ]

    def greet(device):
        pl.semaphore_signal(barrier, inc=1, device_id=device, device_id_type=MESH)

    for load in loads:
        load.start()
    for step in range(1, N_HEAD):
        greet(p.peer(lax.rem(p.head + step, N_HEAD)))
    for step_lon in (-1, 0, 1):
        if step_lon:
            greet(p.beside(0, step_lon))

        @pl.when(p.lat > 0)
        def _():
            greet(p.beside(-1, step_lon))

        @pl.when(p.lat < N_LAT - 1)
        def _():
            greet(p.beside(1, step_lon))

    for step in range(1, N_Y):
        greet(p.at(y=lax.rem(p.y + step, N_Y)))

    for step in (1, 2, 4, 8, 12, 14, 15):
        greet(p.at(z=lax.rem(p.z + step, N_Z)))

    early = Summed(p, *sums[:N_SUM])
    late = Summed(p, *sums[N_SUM:])
    normed_gather = Spread(p, ng.at[p.head], ng, sem_n)
    grad_gather = Spread(p, gg.at[p.head], gg, sem_g)
    halo = Halo(p, ext, sem_ext, True)
    dout_halo = Halo(p, dext, sem_dext, True)
    stat_halo = Halo(p, stats, sem_stats, False)

    loads[0].wait()
    values = wide(xv[...])
    center = values - jnp.mean(values, axis=-1, keepdims=True)
    inv = lax.rsqrt(jnp.mean(center * center, axis=-1, keepdims=True) + EPSILON)
    norm32[...] = center * inv
    spread[...] = jnp.broadcast_to(inv, spread.shape)
    ng[p.head] = half(center * inv)
    for top, at_edge in ((0, p.lat == 0), (112, p.lat == N_LAT - 1)):

        @pl.when(at_edge)
        def _():
            for ref in (ext, dext, stats):
                ref[:, top : top + 48, :] = jnp.zeros((6, 48, ref.shape[2]), jnp.bfloat16)

    greeted = 3 + 2 + (N_Y - 1) + 7
    edge = jnp.where(p.lat > 0, 3, 0) + jnp.where(p.lat < N_LAT - 1, 3, 0)
    pl.semaphore_wait(barrier, greeted + edge)

    for step in (1, 3, 2):
        normed_gather.copy(normed_gather.other(step)).start()
    loads[2].wait()
    for step in (1, 3, 2):
        grad_gather.copy(grad_gather.other(step)).start()

    loads[1].wait()
    low = lax.broadcasted_iota(jnp.int32, (CELLS, 128), 1) < HEAD_SIZE
    zero = jnp.zeros((CELLS, 128), jnp.bfloat16)
    lane = lax.broadcasted_iota(jnp.int32, (CELLS, 128), 1)
    lat, step_lat, step_lon = geometry((CELLS, AROUND))
    inside = (jnp.abs(step_lat) <= REACH) & (jnp.abs(step_lon) <= REACH)
    middle = (step_lat == 0) & (step_lon == 0)
    there = lat + p.lat * 8
    inside_rows = inside & (there >= 0) & (there < 8 * N_LAT)
    row = lax.broadcasted_iota(jnp.int32, (CELLS, 8), 0)
    column = lax.broadcasted_iota(jnp.int32, (CELLS, 8), 1)
    by_lat = dot(half(jnp.where((row >> 3) == column, 1.0, 0.0)), half(wide(valid_v[...])))
    row = lax.broadcasted_iota(jnp.int32, (CELLS, N_LON), 0)
    column = lax.broadcasted_iota(jnp.int32, (CELLS, N_LON), 1)
    for block in range(4):
        own_flag = half(jnp.where(column == 8 * block + (row & 7), by_lat, 0.0))
        flag = dot(own_flag, jnp.ones((N_LON, 128), jnp.bfloat16))
        ext[block + 1, 48:112, 512:640] = half(flag)
        mask_k[block] = jnp.where(inside_rows & ((flag[:, 0:1] > 0) | middle), 0.0, NEGATIVE)

    early.clear()
    late.clear()
    wp[448:512] = jnp.zeros((64, FULL), jnp.bfloat16)
    wop[128:192] = jnp.zeros((64, FULL), jnp.bfloat16)
    for load in loads[3:]:
        load.wait()

    def first(values):
        return jnp.where(low, values, zero)

    def second(values):
        return jnp.where(low, zero, values)

    def arrived(step, gather, margins, project):
        order = jnp.where(step == 2, 3, jnp.where(step == 3, 2, step))
        block = lax.rem(p.head + order, N_HEAD)

        @pl.when(step > 0)
        def _():
            gather.arrival(block).wait_recv()

        project(block)
        margins.send_rows(block)

        @pl.when(block == 0)
        def _():
            margins.send_side(0)

        @pl.when(block == 3)
        def _():
            margins.send_side(1)

    def project_normed(block):
        projected = dot_rows(ng[block], wp[...])
        scale = HEAD_SIZE ** (-0.5)
        ext[block + 1, 48:112, 0:128] = half(half(projected[:, 0:128]) * scale)
        ext[block + 1, 48:112, 128:384] = half(projected[:, 128:384])
        ext[block + 1, 48:112, 384:512] = half(projected[:, 512:640])
        ext[block + 1, 48:112, 512:640] = jnp.where(
            low, half(projected[:, 384:512] * scale), ext[block + 1, 48:112, 512:640]
        )

    def project_grad(block):
        dext[block + 1, 48:112] = half(dot_rows(gg[block], wop[...]))

    @pl.loop(0, N_HEAD)
    def _(step):
        arrived(step, normed_gather, halo, project_normed)

    @pl.loop(0, N_HEAD)
    def _(step):
        arrived(step, grad_gather, dout_halo, project_grad)

    halo.wait_all()
    pick = half(jnp.where(lane == HEAD_SIZE, 1.0, 0.0))
    for block in range(4):
        flag = dot_rows(pick, ext[block : block + 3, :, 512:640].reshape(AROUND, 128))
        mask_q[block] = jnp.where(inside & ((flag > 0) | middle), 0.0, NEGATIVE)
    dout_halo.wait_all()

    def stacked(a, b, c):
        return jnp.concatenate(
            [jnp.concatenate(part, axis=1) for part in (a, b, c)],
            axis=0,
        )

    def thrice(mask):
        return jnp.concatenate([mask, mask, mask], axis=0)

    def around(block, *groups):
        parts = [
            ref[pl.ds(block, 3), :, group * 128 : group * 128 + 128].reshape(AROUND, 128) for ref, group in groups
        ]
        return jnp.concatenate(parts, axis=1)

    def own(block, ref, group):
        return ref[block + 1, 48:112, group * 128 : group * 128 + 128]

    Q01, K01, V01, KV2, Q2 = ((ext, group) for group in range(5))
    D01, D2 = (dext, 0), (dext, 1)
    STAT = (stats, 0)

    def queries_side(block):
        keys, values = around(block, K01, KV2), around(block, V01, KV2)
        q01, d01 = own(block, *Q01), own(block, *D01)
        queries = stacked((first(q01), zero), (second(q01), zero), (zero, first(own(block, *Q2))))
        douts = stacked((first(d01), zero), (second(d01), zero), (zero, own(block, *D2)))
        score = dot_rows(queries, keys) + thrice(mask_q[block])
        best = jnp.max(score, axis=1, keepdims=True)
        chance = jnp.exp(score - best)
        total = jnp.sum(chance, axis=1, keepdims=True)
        level = best + jnp.log(total)
        chance = chance * (1.0 / total)
        inner = dot_rows(douts, values)
        carried = jnp.sum(chance * inner, axis=1, keepdims=True)
        soft_grad = half(chance * (inner - carried))
        attended = dot(half(chance), values)
        grad_query = dot(soft_grad, keys) * HEAD_SIZE ** (-0.5)
        gp[block, :, 640:768] = half(jnp.where(low, attended[0:64, 0:128], attended[64:128, 0:128]))
        gp[block, :, 0:128] = half(jnp.where(low, grad_query[0:64, 0:128], grad_query[64:128, 0:128]))
        gp[block, :, 384:512] = half(jnp.where(low, grad_query[128:192, 128:256], attended[128:192, 128:256]))
        tile = jnp.zeros((CELLS, 128), jnp.float32)
        for kind, column in enumerate((level, carried)):
            for head in range(3):
                rest = column[64 * head : 64 * head + 64]
                for digit in range(3):
                    piece = wide(half(rest))
                    rest = rest - piece
                    tile = jnp.where(lane == 9 * kind + 3 * head + digit, piece, tile)
        stats[block + 1, 48:112] = half(tile)

    for block in range(4):
        queries_side(block)
    stat_halo.send_all()

    def cells(ref, *groups):
        return jnp.concatenate([ref[:, :, g * 128 : g * 128 + 128].reshape(4 * CELLS, 128) for g in groups], axis=1)

    grads = gg[...].reshape(4 * CELLS, FULL)
    normed = ng[...].reshape(4 * CELLS, FULL)
    mixed_in = cells(gp, 5, 3)
    weights = dot_cells(mixed_in, grads)
    put(early.src, 0, weights[0:128])
    put(early.src, 128, weights[192:256])
    weights = dot_cells(cells(gp, 0, 3), normed)
    put(early.src, 192, weights[0:192])
    early.send_core()

    out_spread = Spread(p, pvs, pvr, sem_pv)
    pvs[...] = half(dot(mixed_in, wop[...])).reshape(4, CELLS, FULL)
    for step in (2, 1, 3):
        out_spread.copy(out_spread.other(step)).start()
    early.core_to_y()
    stat_halo.wait_all()

    def minus_one(start):
        return half(jnp.where((lane >= start) & (lane < start + 3), -1.0, 0.0))

    def keys_side(block):
        queries, douts = around(block, Q01, Q2, STAT), around(block, D01, D2, STAT)
        k01, v01, kv2 = own(block, *K01), own(block, *V01), own(block, *KV2)
        keys = stacked(
            (first(k01), zero, minus_one(0)), (second(k01), zero, minus_one(3)), (zero, first(kv2), minus_one(6))
        )
        values = stacked(
            (first(v01), zero, minus_one(9)), (second(v01), zero, minus_one(12)), (zero, second(kv2), minus_one(15))
        )
        chance = jnp.exp(dot_rows(keys, queries) + thrice(mask_k[block]))
        soft_grad = half(chance * dot_rows(values, douts))
        grad_key = dot(soft_grad, queries[:, 0:256])
        grad_value = dot(half(chance), douts[:, 0:256])
        gp[block, :, 128:256] = half(jnp.where(low, grad_key[0:64, 0:128], grad_key[64:128, 0:128]))
        gp[block, :, 256:384] = half(jnp.where(low, grad_value[0:64, 0:128], grad_value[64:128, 0:128]))
        gp[block, :, 512:640] = half(jnp.where(low, grad_key[128:192, 128:256], grad_value[128:192, 128:256]))

    for block in range(4):
        keys_side(block)

    weights = dot_cells(cells(gp, 1, 4), normed)
    put(late.src, 0, weights[0:192])
    weights = jnp.concatenate([dot_cells(cells(gp, 2), normed), weights[192:256]], axis=0)
    put(late.src, 192, weights)
    late.send_core()
    early.y_to_near()

    norm_spread = Spread(p, gns, gnr, sem_gn)
    gns[...] = half(dot(cells(gp, 0, 1, 2, 3, 4), wp[...])).reshape(4, CELLS, FULL)
    for step in (2, 1, 3):
        norm_spread.copy(norm_spread.other(step)).start()

    late.core_to_y()
    early.near_to_far()

    total = wide(pvs[p.head])
    for step in (1, 2, 3):
        other = out_spread.other(step)
        out_spread.arrival(other).wait_recv()
        total = total + wide(pvr[other])
    mixed_ref[...] = half(wide(xv[...]) + total)
    mixed_store.start()

    late.y_to_near()
    late.near_to_far()
    early.far_to_all()

    total = wide(gns[p.head])
    for step in (1, 2, 3):
        other = norm_spread.other(step)
        norm_spread.arrival(other).wait_recv()
        total = total + wide(gnr[other])
    own_norm = norm32[...]
    mean = jnp.mean(total, axis=-1, keepdims=True)
    along = jnp.mean(total * own_norm, axis=-1, keepdims=True)
    d_input = spread[:, 0:1] * (total - mean - own_norm * along)
    gx_ref[...] = half(wide(gg[p.head]) + d_input)
    gx_store.start()

    early.all_to_y()
    late.far_to_all()
    early.y_to_core()
    for spread_copy in (normed_gather, grad_gather, out_spread, norm_spread):
        spread_copy.wait_sent()
    for one in (halo, dout_halo, stat_halo):
        one.wait_sent()
    late.all_to_y()
    early.finish()
    take(early.res, 0, gwo_ref, 0, 192)
    take(early.res, 192, gqkv_ref, 0, 192)
    gwo_store.start()
    query_store.start()
    late.y_to_core()
    early.wait_sent()
    late.finish()
    late.wait_sent()
    take(late.res, 0, gqkv_ref, 192, 384)
    rest_store.start()
    for store in (mixed_store, gx_store, gwo_store, query_store, rest_store):
        store.wait()


def store_kernel(*refs):
    given, out, held, sems = refs[:4], refs[4:8], refs[8:12], refs[12]
    loads = [pltpu.make_async_copy(given[i], held[i], sems.at[0, i]) for i in range(4)]
    stores = [pltpu.make_async_copy(held[i], out[i], sems.at[1, i]) for i in range(4)]
    for load in loads:
        load.start()
    for load, store in zip(loads, stores):
        load.wait()
        store.start()
    for store in stores:
        store.wait()


def on_device(activations, qkv_weight, out_weight, valid, grad_y):
    bf, f32 = jnp.bfloat16, jnp.float32
    gathered = pltpu.VMEM((N_HEAD, CELLS, FULL), bf)
    pair = pltpu.SemaphoreType.DMA((2, N_HEAD))
    around = pltpu.SemaphoreType.DMA((2, 14))
    results = pl.pallas_call(
        block_kernel,
        out_shape=[
            jax.ShapeDtypeStruct((CELLS, FULL), bf),
            jax.ShapeDtypeStruct((CELLS, FULL), bf),
            jax.ShapeDtypeStruct((3 * 192, FULL), bf),
            jax.ShapeDtypeStruct((192, FULL), bf),
        ],
        in_specs=[pl.BlockSpec(memory_space=pltpu.HBM)] * 5,
        out_specs=[pl.BlockSpec(memory_space=pltpu.HBM)] * 4,
        scratch_shapes=[
            pltpu.VMEM((CELLS, FULL), bf),
            pltpu.VMEM((CELLS, FULL), bf),
            pltpu.VMEM((3 * 192, FULL), bf),
            pltpu.VMEM((192, FULL), bf),
            pltpu.SemaphoreType.DMA((5,)),
            pltpu.VMEM((CELLS, FULL), bf),
            pltpu.VMEM((8, N_LON), jnp.int32),
            gathered,
            gathered,
            pltpu.VMEM((CELLS, FULL), f32),
            pltpu.VMEM((CELLS, 128), f32),
            pltpu.VMEM((640, FULL), bf),
            pltpu.VMEM((256, FULL), bf),
            pltpu.VMEM((6, TALL, 640), bf),
            pltpu.VMEM((6, TALL, 256), bf),
            pltpu.VMEM((6, TALL, 128), bf),
            pltpu.VMEM((4, CELLS, AROUND), f32),
            pltpu.VMEM((4, CELLS, AROUND), f32),
            gathered,
            gathered,
            gathered,
            gathered,
            gathered,
            pltpu.SemaphoreType.DMA((11,)),
            pair,
            pair,
            pair,
            pair,
            around,
            around,
            around,
            *Summed.scratch(),
            *Summed.scratch(),
        ],
        compiler_params=pltpu.CompilerParams(
            collective_id=0, has_side_effects=True, vmem_limit_bytes=63 * 2**20
        ),
    )(
        activations.reshape(CELLS, FULL),
        grad_y.reshape(CELLS, FULL),
        qkv_weight,
        out_weight,
        valid,
    )
    mixed, grad_x, grad_qkv, grad_out = pl.pallas_call(
        store_kernel,
        out_shape=[jax.ShapeDtypeStruct(result.shape, bf) for result in results],
        in_specs=[pl.BlockSpec(memory_space=pl.ANY)] * 4,
        out_specs=[pl.BlockSpec(memory_space=pltpu.HBM)] * 4,
        scratch_shapes=[
            *(pltpu.VMEM(result.shape, bf) for result in results),
            pltpu.SemaphoreType.DMA((2, 4)),
        ],
    )(*results)
    return (
        mixed.reshape(activations.shape),
        grad_x.reshape(activations.shape),
        grad_qkv.reshape(qkv_weight.shape),
        grad_out,
    )


def solution(mesh):
    return jax.shard_map(
        on_device,
        mesh=mesh,
        in_specs=(
            P("lat", ("lon", "head"), None),
            P(None, "head", None),
            P("head", None),
            P("lat", "lon"),
            P("lat", ("lon", "head"), None),
        ),
        out_specs=(
            P("lat", ("lon", "head"), None),
            P("lat", ("lon", "head"), None),
            P(None, "head", None),
            P("head", None),
        ),
        check_vma=False,
    )
```

```python
import jax
import jax.numpy as jnp
from jax import lax
from jax.experimental import pallas as pl
from jax.experimental.pallas import tpu as pltpu
from jax.sharding import PartitionSpec as P

MESH = pl.DeviceIdType.MESH
HEAD_SIZE = 64
REACH = 6
EPSILON = 1e-05
NEGATIVE = -1e30
N_HEAD = 4
N_LAT = 4
N_LON = 32
CELLS = 64
FULL = 768
TALL = 160
AROUND = 3 * TALL
N_Z = 16
N_Y = 4
NEAR = 4
CHUNK = 5
TILES = NEAR * CHUNK


class Place:
    def __init__(self):
        self.lat = lax.axis_index("lat")
        self.lon = lax.axis_index("lon")
        self.head = lax.axis_index("head")
        self.core = lax.rem(self.lat, 2)
        self.y = (self.lon // N_Z) * 2 + self.lat // 2
        self.z = lax.rem(self.lon, N_Z)

    def at(self, core=None, y=None, z=None):
        core = self.core if core is None else core
        y = self.y if y is None else y
        z = self.z if z is None else z
        return (lax.rem(y, 2) * 2 + core, (y // 2) * N_Z + z, self.head)


    def beside(self, step_lat, step_lon):
        return (self.lat + step_lat, lax.rem(self.lon + step_lon + N_LON, N_LON), self.head)

    def peer(self, head):
        return (self.lat, self.lon, head)


def remote(src, dst, send_sem, recv_sem, device):
    return pltpu.make_async_remote_copy(
        src_ref=src,
        dst_ref=dst,
        send_sem=send_sem,
        recv_sem=recv_sem,
        device_id=device,
        device_id_type=MESH,
    )


class Summed:
    def __init__(self, place, src, res, cbuf, ybuf, nbuf, fbuf, sem_c, sem_y, sem_n, sem_f, sem_ng, sem_yg, sem_cg):
        self.p = place
        self.src, self.res, self.cbuf, self.ybuf, self.nbuf, self.fbuf = src, res, cbuf, ybuf, nbuf, fbuf
        self.sem_c, self.sem_y, self.sem_n, self.sem_f = sem_c, sem_y, sem_n, sem_f
        self.sem_ng, self.sem_yg, self.sem_cg = sem_ng, sem_yg, sem_cg
        self.two = jnp.where(place.core == 0, 2, N_Z - 2)

    @staticmethod
    def scratch():
        bf = jnp.bfloat16
        sems = pltpu.SemaphoreType.DMA
        return [
            pltpu.VMEM((2, N_Y, TILES, 16, 128), bf),
            pltpu.VMEM((2, N_Y, TILES, 16, 128), bf),
            pltpu.VMEM((N_Y, TILES, 16, 128), bf),
            pltpu.VMEM((N_Y, TILES, 16, 128), bf),
            pltpu.VMEM((NEAR, CHUNK, 16, 128), bf),
            pltpu.VMEM((NEAR, CHUNK, 16, 128), bf),
            sems((2,)),
            sems((2, N_Y, NEAR)),
            sems((2, NEAR)),
            sems((2, NEAR)),
            sems((2, NEAR)),
            sems((2, N_Y, NEAR)),
            sems((2, N_Y)),
        ]

    def clear(self):
        for ref in (self.src,):
            ref[:, :, 18:TILES] = jnp.zeros((2, N_Y, TILES - 18, 16, 128), jnp.bfloat16)

    def chunk(self, away):
        return lax.rem(self.p.z + away, NEAR)

    def tiles(self, away):
        return pl.ds(CHUNK * self.chunk(away), CHUNK)

    def along(self, away):
        step = {1: 1, 2: self.two, 3: N_Z - 1}[away]
        return lax.rem(self.p.z + step, N_Z), lax.rem(self.p.z + N_Z - step, N_Z)

    def core_copy(self):
        p = self.p
        return remote(
            self.src.at[1 - p.core], self.cbuf, self.sem_c.at[0], self.sem_c.at[1], p.at(core=1 - p.core)
        )

    def y_copy(self, step, away, arriving=False):
        p = self.p
        y = lax.rem(p.y + step, N_Y)
        slot = y if arriving else p.y
        return remote(
            self.src.at[p.core, y, self.tiles(away)],
            self.ybuf.at[slot, self.tiles(away)],
            self.sem_y.at[0, y, away],
            self.sem_y.at[1, slot, away],
            p.at(y=y),
        )

    def near_copy(self, away):
        p = self.p
        there, _ = self.along(away)
        return remote(
            self.src.at[p.core, p.y, self.tiles(away)],
            self.nbuf.at[away],
            self.sem_n.at[0, away],
            self.sem_n.at[1, away],
            p.at(z=there),
        )

    def far_copy(self, step, arriving=False):
        p = self.p
        z = lax.rem(p.z + 4 * step, N_Z)
        slot = (z if arriving else p.z) // 4
        return remote(
            self.src.at[p.core, p.y, self.tiles(0)],
            self.fbuf.at[slot],
            self.sem_f.at[0, step],
            self.sem_f.at[1, slot],
            p.at(z=z),
        )

    def back_copy(self, away, arriving=False):
        p = self.p
        _, there = self.along(away)
        here = self.res.at[p.core, p.y, self.tiles(away if arriving else 0)]
        return remote(here, here, self.sem_ng.at[0, away], self.sem_ng.at[1, away], p.at(z=there))

    def yg_copy(self, step, away, arriving=False):
        p = self.p
        y = lax.rem(p.y + step, N_Y)
        slot = y if arriving else p.y
        here = self.res.at[p.core, slot, self.tiles(away)]
        return remote(here, here, self.sem_yg.at[0, y, away], self.sem_yg.at[1, slot, away], p.at(y=y))

    def cg_copy(self, y, arriving=False):
        p = self.p
        here = self.res.at[1 - p.core if arriving else p.core, y]
        return remote(here, here, self.sem_cg.at[0, y], self.sem_cg.at[1, y], p.at(core=1 - p.core))

    def send_core(self):
        self.core_copy().start()

    def core_to_y(self):
        p = self.p
        self.core_copy().wait_recv()
        for step in (2, 1, 3, 0):
            y = lax.rem(p.y + step, N_Y)
            both = self.src[p.core, y].astype(jnp.float32) + self.cbuf[y].astype(jnp.float32)
            self.src[p.core, y] = both.astype(jnp.bfloat16)
        for away in (2, 1, 3, 0):
            for step in (2, 1, 3):
                self.y_copy(step, away).start()

    def y_to_near(self):
        p = self.p
        for away in (2, 1, 3, 0):
            for step in (1, 3, 2):
                self.y_copy(step, away, True).wait_recv()
            tiles = self.tiles(away)
            total = self.src[p.core, p.y, tiles].astype(jnp.float32)
            for step in (1, 2, 3):
                total = total + self.ybuf[lax.rem(p.y + step, N_Y), tiles].astype(jnp.float32)
            self.src[p.core, p.y, tiles] = total.astype(jnp.bfloat16)
            if away:
                self.near_copy(away).start()

    def near_to_far(self):
        p = self.p
        total = self.src[p.core, p.y, self.tiles(0)].astype(jnp.float32)
        for away in (1, 3, 2):
            self.near_copy(away).wait_recv()
            total = total + self.nbuf[away].astype(jnp.float32)
        total = total.astype(jnp.bfloat16)
        self.src[p.core, p.y, self.tiles(0)] = total
        for step in (2, 1, 3):
            self.far_copy(step).start()
        self.fbuf[p.z // 4] = total

    def far_to_all(self):
        p = self.p
        for step in (1, 3, 2):
            self.far_copy(step, True).wait_recv()
        total = self.fbuf[0].astype(jnp.float32)
        for group in range(1, NEAR):
            total = total + self.fbuf[group].astype(jnp.float32)
        self.res[p.core, p.y, self.tiles(0)] = total.astype(jnp.bfloat16)
        for away in (2, 1, 3):
            self.back_copy(away).start()
        for step in (2, 1, 3):
            self.yg_copy(step, 0).start()

    def all_to_y(self):
        for away in (1, 3, 2):
            self.back_copy(away, True).wait_recv()
            for step in (2, 1, 3):
                self.yg_copy(step, away).start()
        self.cg_copy(self.p.y).start()

    def y_to_core(self):
        p = self.p
        for step in (1, 3, 2):
            for away in range(NEAR):
                self.yg_copy(step, away, True).wait_recv()
            self.cg_copy(lax.rem(p.y + step, N_Y)).start()

    def finish(self):
        for y in range(N_Y):
            self.cg_copy(y, True).wait_recv()

    def wait_sent(self):
        self.core_copy().wait_send()
        for step in (1, 2, 3):
            for away in range(NEAR):
                self.y_copy(step, away).wait_send()
                self.yg_copy(step, away).wait_send()
            self.near_copy(step).wait_send()
            self.far_copy(step).wait_send()
            self.back_copy(step).wait_send()
        for y in range(N_Y):
            self.cg_copy(y).wait_send()


def dot(a, b):
    return lax.dot_general(a, b, (((1,), (0,)), ((), ())), preferred_element_type=jnp.float32)


def dot_rows(a, b):
    return lax.dot_general(a, b, (((1,), (1,)), ((), ())), preferred_element_type=jnp.float32)


def dot_cells(a, b):
    return lax.dot_general(a, b, (((0,), (0,)), ((), ())), preferred_element_type=jnp.float32)


def half(values):
    return values.astype(jnp.bfloat16)


def wide(values):
    return values.astype(jnp.float32)


class Halo:
    def __init__(self, place, ref, sems, by_block):
        self.p, self.ref, self.sems, self.by_block = place, ref, sems, by_block

    def message(self, index, block, src_rows, dst_block, dst_rows, step_lat, step_lon):
        src = self.ref.at[block, pl.ds(*src_rows)]
        dst = self.ref.at[dst_block, pl.ds(*dst_rows)]
        device = self.p.beside(step_lat, step_lon)
        return remote(src, dst, self.sems.at[0, index], self.sems.at[1, index], device)

    def north(self, block):
        at = block + 1 if self.by_block else pl.ds(1, 4)
        return self.message(block, at, (48, 48), at, (112, 48), -1, 0)

    def south(self, block):
        at = block + 1 if self.by_block else pl.ds(1, 4)
        return self.message(4 + block, at, (64, 48), at, (0, 48), 1, 0)

    def side(self, row, east):
        src_rows, dst_rows = {0: ((48, 64), (48, 64)), -1: ((48, 48), (112, 48)), 1: ((64, 48), (0, 48))}[row]
        index = 8 + 2 * (row % 3) + east
        return self.message(index, 4 if east else 1, src_rows, 0 if east else 5, dst_rows, row, 1 if east else -1)

    def when(self, row, then):
        if row == -1:
            pl.when(self.p.lat > 0)(then)
        elif row == 1:
            pl.when(self.p.lat < N_LAT - 1)(then)
        else:
            then()

    def send_rows(self, block):
        self.when(-1, lambda: self.north(block).start())
        self.when(1, lambda: self.south(block).start())

    def send_side(self, east):
        for row in (0, -1, 1):
            self.when(row, lambda row=row: self.side(row, east).start())

    def send_all(self):
        self.send_rows(0)
        self.send_side(0)
        self.send_side(1)

    def blocks(self):
        return range(4) if self.by_block else range(1)

    def wait_all(self):
        for block in self.blocks():
            self.when(1, lambda block=block: self.north(block).wait_recv())
            self.when(-1, lambda block=block: self.south(block).wait_recv())
        for east in (0, 1):
            for row in (0, -1, 1):
                self.when(-row, lambda row=row, east=east: self.side(row, east).wait_recv())

    def wait_sent(self):
        for block in self.blocks():
            self.when(-1, lambda block=block: self.north(block).wait_send())
            self.when(1, lambda block=block: self.south(block).wait_send())
        for east in (0, 1):
            for row in (0, -1, 1):
                self.when(row, lambda row=row, east=east: self.side(row, east).wait_send())


class Spread:
    def __init__(self, place, src, dst, sems):
        self.p, self.src, self.dst, self.sems = place, src, dst, sems

    def copy(self, head):
        src = self.src.at[head] if len(self.src.shape) == 3 else self.src
        return remote(
            src, self.dst.at[self.p.head], self.sems.at[0, head], self.sems.at[1, self.p.head], self.p.peer(head)
        )

    def arrival(self, head):
        src = self.src.at[head] if len(self.src.shape) == 3 else self.src
        return remote(src, self.dst.at[head], self.sems.at[0, head], self.sems.at[1, head], self.p.peer(head))

    def other(self, step):
        return lax.rem(self.p.head + step, N_HEAD)

    def wait_sent(self):
        for step in (1, 2, 3):
            self.copy(self.other(step)).wait_send()


def geometry(shape):
    row = lax.broadcasted_iota(jnp.int32, shape, 0)
    lane = lax.broadcasted_iota(jnp.int32, shape, 1)
    block = jnp.where(lane >= TALL, 1, 0) + jnp.where(lane >= 2 * TALL, 1, 0)
    rest = lane - TALL * block
    lat = (rest >> 3) - REACH
    step_lat = lat - (row >> 3)
    step_lon = (block - 1) * 8 + (rest & 7) - (row & 7)
    return lat, step_lat, step_lon


def place_of(row, column):
    return column // 3, row // 96, row % 96 // 16 * 3 + column % 3


def put(src, top, values):
    for row in range(0, values.shape[0], 16):
        for column in range(6):
            src[place_of(top + row, column)] = half(values[row : row + 16, column * 128 : column * 128 + 128])


def take(res, top, out_ref, out_top, rows):
    for row in range(0, rows, 16):
        for column in range(6):
            out_ref[out_top + row : out_top + row + 16, column * 128 : column * 128 + 128] = res[
                place_of(top + row, column)
            ]


N_SUM = 13


def block_kernel(
    x_ref, gy_ref, wqkv_ref, wo_ref, valid_ref, mixed_out, gx_out, gqkv_out, gwo_out,
    mixed_ref, gx_ref, gqkv_ref, gwo_ref, soft_v, soft_grad_v, sem_out, xv, valid_v, ng, gg, norm32, spread, wp, wop, ext, dext, stats, mask_q, mask_k, gp, pvs, pvr, gns, gnr,
    sem_in, sem_n, sem_g, sem_pv, sem_gn, sem_ext, sem_dext, sem_stats, *sums,
):
    p = Place()
    barrier = pltpu.get_barrier_semaphore()
    loads = [
        pltpu.make_async_copy(src, dst, sem_in.at[index])
        for index, (src, dst) in enumerate(
            (
                (x_ref, xv),
                (valid_ref, valid_v),
                (gy_ref, gg.at[p.head]),
                (wqkv_ref.at[0, pl.ds(0, 128)], wp.at[pl.ds(0, 128)]),
                (wqkv_ref.at[1, pl.ds(0, 128)], wp.at[pl.ds(128, 128)]),
                (wqkv_ref.at[2, pl.ds(0, 128)], wp.at[pl.ds(256, 128)]),
                (wqkv_ref.at[0, pl.ds(128, 64)], wp.at[pl.ds(384, 64)]),
                (wqkv_ref.at[1, pl.ds(128, 64)], wp.at[pl.ds(512, 64)]),
                (wqkv_ref.at[2, pl.ds(128, 64)], wp.at[pl.ds(576, 64)]),
                (wo_ref.at[pl.ds(0, 128)], wop.at[pl.ds(0, 128)]),
                (wo_ref.at[pl.ds(128, 64)], wop.at[pl.ds(192, 64)]),
            )
        )
    ]

    query_rows = pl.ds(0, 192)
    mixed_store, gx_store, gwo_store, query_store = [
        pltpu.make_async_copy(src, dst, sem_out.at[index])
        for index, (src, dst) in enumerate(
            (
                (mixed_ref, mixed_out),
                (gx_ref, gx_out),
                (gwo_ref, gwo_out),
                (gqkv_ref.at[query_rows], gqkv_out.at[query_rows]),
            )
        )
    ]

    def greet(device):
        pl.semaphore_signal(barrier, inc=1, device_id=device, device_id_type=MESH)

    for load in loads:
        load.start()
    for step in range(1, N_HEAD):
        greet(p.peer(lax.rem(p.head + step, N_HEAD)))
    for step_lon in (-1, 0, 1):
        if step_lon:
            greet(p.beside(0, step_lon))

        @pl.when(p.lat > 0)
        def _():
            greet(p.beside(-1, step_lon))

        @pl.when(p.lat < N_LAT - 1)
        def _():
            greet(p.beside(1, step_lon))

    for step in range(1, N_Y):
        greet(p.at(y=lax.rem(p.y + step, N_Y)))

    for step in (1, 2, 4, 8, 12, 14, 15):
        greet(p.at(z=lax.rem(p.z + step, N_Z)))

    early = Summed(p, *sums[:N_SUM])
    late = Summed(p, *sums[N_SUM:])
    normed_gather = Spread(p, ng.at[p.head], ng, sem_n)
    grad_gather = Spread(p, gg.at[p.head], gg, sem_g)
    halo = Halo(p, ext, sem_ext, True)
    dout_halo = Halo(p, dext, sem_dext, True)
    stat_halo = Halo(p, stats, sem_stats, False)

    loads[0].wait()
    values = wide(xv[...])
    center = values - jnp.mean(values, axis=-1, keepdims=True)
    inv = lax.rsqrt(jnp.mean(center * center, axis=-1, keepdims=True) + EPSILON)
    norm32[...] = center * inv
    spread[...] = jnp.broadcast_to(inv, spread.shape)
    ng[p.head] = half(center * inv)
    for top, at_edge in ((0, p.lat == 0), (112, p.lat == N_LAT - 1)):

        @pl.when(at_edge)
        def _():
            for ref in (ext, dext, stats):
                ref[:, top : top + 48, :] = jnp.zeros((6, 48, ref.shape[2]), jnp.bfloat16)

    greeted = 3 + 2 + (N_Y - 1) + 7
    edge = jnp.where(p.lat > 0, 3, 0) + jnp.where(p.lat < N_LAT - 1, 3, 0)
    pl.semaphore_wait(barrier, greeted + edge)

    for step in (1, 3, 2):
        normed_gather.copy(normed_gather.other(step)).start()
    loads[2].wait()
    for step in (1, 3, 2):
        grad_gather.copy(grad_gather.other(step)).start()

    loads[1].wait()
    low = lax.broadcasted_iota(jnp.int32, (CELLS, 128), 1) < HEAD_SIZE
    zero = jnp.zeros((CELLS, 128), jnp.bfloat16)
    lane = lax.broadcasted_iota(jnp.int32, (CELLS, 128), 1)
    lat, step_lat, step_lon = geometry((CELLS, AROUND))
    inside = (jnp.abs(step_lat) <= REACH) & (jnp.abs(step_lon) <= REACH)
    middle = (step_lat == 0) & (step_lon == 0)
    there = lat + p.lat * 8
    inside_rows = inside & (there >= 0) & (there < 8 * N_LAT)
    row = lax.broadcasted_iota(jnp.int32, (CELLS, 8), 0)
    column = lax.broadcasted_iota(jnp.int32, (CELLS, 8), 1)
    by_lat = dot(half(jnp.where((row >> 3) == column, 1.0, 0.0)), half(wide(valid_v[...])))
    row = lax.broadcasted_iota(jnp.int32, (CELLS, N_LON), 0)
    column = lax.broadcasted_iota(jnp.int32, (CELLS, N_LON), 1)
    for block in range(4):
        own_flag = half(jnp.where(column == 8 * block + (row & 7), by_lat, 0.0))
        flag = dot(own_flag, jnp.ones((N_LON, 128), jnp.bfloat16))
        ext[block + 1, 48:112, 512:640] = half(flag)
        mask_k[block] = jnp.where(inside_rows & ((flag[:, 0:1] > 0) | middle), 0.0, NEGATIVE)

    early.clear()
    late.clear()
    wp[448:512] = jnp.zeros((64, FULL), jnp.bfloat16)
    wop[128:192] = jnp.zeros((64, FULL), jnp.bfloat16)
    for load in loads[3:]:
        load.wait()

    def first(values):
        return jnp.where(low, values, zero)

    def second(values):
        return jnp.where(low, zero, values)

    def arrived(step, gather, margins, project):
        order = jnp.where(step == 2, 3, jnp.where(step == 3, 2, step))
        block = lax.rem(p.head + order, N_HEAD)

        @pl.when(step > 0)
        def _():
            gather.arrival(block).wait_recv()

        project(block)
        margins.send_rows(block)

        @pl.when(block == 0)
        def _():
            margins.send_side(0)

        @pl.when(block == 3)
        def _():
            margins.send_side(1)

    def project_normed(block):
        projected = dot_rows(ng[block], wp[...])
        scale = HEAD_SIZE ** (-0.5)
        ext[block + 1, 48:112, 0:128] = half(half(projected[:, 0:128]) * scale)
        ext[block + 1, 48:112, 128:384] = half(projected[:, 128:384])
        ext[block + 1, 48:112, 384:512] = half(projected[:, 512:640])
        ext[block + 1, 48:112, 512:640] = jnp.where(
            low, half(projected[:, 384:512] * scale), ext[block + 1, 48:112, 512:640]
        )

    def project_grad(block):
        dext[block + 1, 48:112] = half(dot_rows(gg[block], wop[...]))

    @pl.loop(0, N_HEAD)
    def _(step):
        arrived(step, normed_gather, halo, project_normed)

    @pl.loop(0, N_HEAD)
    def _(step):
        arrived(step, grad_gather, dout_halo, project_grad)

    halo.wait_all()
    pick = half(jnp.where(lane == HEAD_SIZE, 1.0, 0.0))
    for block in range(4):
        flag = dot_rows(pick, ext[block : block + 3, :, 512:640].reshape(AROUND, 128))
        mask_q[block] = jnp.where(inside & ((flag > 0) | middle), 0.0, NEGATIVE)
    dout_halo.wait_all()

    def stacked(a, b, c):
        return jnp.concatenate(
            [jnp.concatenate(part, axis=1) for part in (a, b, c)],
            axis=0,
        )

    def thrice(mask):
        return jnp.concatenate([mask, mask, mask], axis=0)

    def around(block, *groups):
        parts = [
            ref[pl.ds(block, 3), :, group * 128 : group * 128 + 128].reshape(AROUND, 128) for ref, group in groups
        ]
        return jnp.concatenate(parts, axis=1)

    def own(block, ref, group):
        return ref[block + 1, 48:112, group * 128 : group * 128 + 128]

    Q01, K01, V01, KV2, Q2 = ((ext, group) for group in range(5))
    D01, D2 = (dext, 0), (dext, 1)
    STAT = (stats, 0)

    def queries_side(block):
        keys, values = around(block, K01, KV2), around(block, V01, KV2)
        q01, d01 = own(block, *Q01), own(block, *D01)
        queries = stacked((first(q01), zero), (second(q01), zero), (zero, first(own(block, *Q2))))
        douts = stacked((first(d01), zero), (second(d01), zero), (zero, own(block, *D2)))
        score = dot_rows(queries, keys) + thrice(mask_q[block])
        best = jnp.max(score, axis=1, keepdims=True)
        chance = jnp.exp(score - best)
        total = jnp.sum(chance, axis=1, keepdims=True)
        level = best + jnp.log(total)
        chance = chance * (1.0 / total)
        inner = dot_rows(douts, values)
        carried = jnp.sum(chance * inner, axis=1, keepdims=True)
        soft_grad = half(chance * (inner - carried))
        soft_v[block] = half(chance)
        soft_grad_v[block] = soft_grad
        tile = jnp.zeros((CELLS, 128), jnp.float32)
        for kind, column in enumerate((level, carried)):
            for head in range(3):
                rest = column[64 * head : 64 * head + 64]
                for digit in range(3):
                    piece = wide(half(rest))
                    rest = rest - piece
                    tile = jnp.where(lane == 9 * kind + 3 * head + digit, piece, tile)
        stats[block + 1, 48:112] = half(tile)

    def queries_rest(block):
        keys, values = around(block, K01, KV2), around(block, V01, KV2)
        attended = dot(soft_v[block], values)
        grad_query = dot(soft_grad_v[block], keys) * HEAD_SIZE ** (-0.5)
        gp[block, :, 640:768] = half(jnp.where(low, attended[0:64, 0:128], attended[64:128, 0:128]))
        gp[block, :, 0:128] = half(jnp.where(low, grad_query[0:64, 0:128], grad_query[64:128, 0:128]))
        gp[block, :, 384:512] = half(jnp.where(low, grad_query[128:192, 128:256], attended[128:192, 128:256]))

    for block in range(4):
        queries_side(block)
    stat_halo.send_all()
    for block in range(4):
        queries_rest(block)

    def cells(ref, *groups):
        return jnp.concatenate([ref[:, :, g * 128 : g * 128 + 128].reshape(4 * CELLS, 128) for g in groups], axis=1)

    grads = gg[...].reshape(4 * CELLS, FULL)
    normed = ng[...].reshape(4 * CELLS, FULL)
    mixed_in = cells(gp, 5, 3)
    weights = dot_cells(mixed_in, grads)
    put(early.src, 0, weights[0:128])
    put(early.src, 128, weights[192:256])
    weights = dot_cells(cells(gp, 0, 3), normed)
    put(early.src, 192, weights[0:192])
    early.send_core()

    out_spread = Spread(p, pvs, pvr, sem_pv)
    pvs[...] = half(dot(mixed_in, wop[...])).reshape(4, CELLS, FULL)
    for step in (2, 1, 3):
        out_spread.copy(out_spread.other(step)).start()
    early.core_to_y()
    stat_halo.wait_all()

    def minus_one(start):
        return half(jnp.where((lane >= start) & (lane < start + 3), -1.0, 0.0))

    def keys_side(block):
        queries, douts = around(block, Q01, Q2, STAT), around(block, D01, D2, STAT)
        k01, v01, kv2 = own(block, *K01), own(block, *V01), own(block, *KV2)
        keys = stacked(
            (first(k01), zero, minus_one(0)), (second(k01), zero, minus_one(3)), (zero, first(kv2), minus_one(6))
        )
        values = stacked(
            (first(v01), zero, minus_one(9)), (second(v01), zero, minus_one(12)), (zero, second(kv2), minus_one(15))
        )
        chance = jnp.exp(dot_rows(keys, queries) + thrice(mask_k[block]))
        soft_grad = half(chance * dot_rows(values, douts))
        grad_key = dot(soft_grad, queries[:, 0:256])
        grad_value = dot(half(chance), douts[:, 0:256])
        gp[block, :, 128:256] = half(jnp.where(low, grad_key[0:64, 0:128], grad_key[64:128, 0:128]))
        gp[block, :, 256:384] = half(jnp.where(low, grad_value[0:64, 0:128], grad_value[64:128, 0:128]))
        gp[block, :, 512:640] = half(jnp.where(low, grad_key[128:192, 128:256], grad_value[128:192, 128:256]))

    for block in range(4):
        keys_side(block)

    weights = dot_cells(cells(gp, 1, 4), normed)
    put(late.src, 0, weights[0:192])
    weights = jnp.concatenate([dot_cells(cells(gp, 2), normed), weights[192:256]], axis=0)
    put(late.src, 192, weights)
    late.send_core()
    early.y_to_near()

    late.core_to_y()

    norm_spread = Spread(p, gns, gnr, sem_gn)
    gns[...] = half(dot(cells(gp, 0, 1, 2, 3, 4), wp[...])).reshape(4, CELLS, FULL)
    for step in (2, 1, 3):
        norm_spread.copy(norm_spread.other(step)).start()

    early.near_to_far()

    late.y_to_near()
    late.near_to_far()
    early.far_to_all()

    total = wide(pvs[p.head])
    for step in (1, 2, 3):
        other = out_spread.other(step)
        out_spread.arrival(other).wait_recv()
        total = total + wide(pvr[other])
    mixed_ref[...] = half(wide(xv[...]) + total)
    mixed_store.start()

    total = wide(gns[p.head])
    for step in (1, 2, 3):
        other = norm_spread.other(step)
        norm_spread.arrival(other).wait_recv()
        total = total + wide(gnr[other])
    own_norm = norm32[...]
    mean = jnp.mean(total, axis=-1, keepdims=True)
    along = jnp.mean(total * own_norm, axis=-1, keepdims=True)
    d_input = spread[:, 0:1] * (total - mean - own_norm * along)
    gx_ref[...] = half(wide(gg[p.head]) + d_input)
    gx_store.start()


    early.all_to_y()
    late.far_to_all()
    early.y_to_core()
    for spread_copy in (normed_gather, grad_gather, out_spread, norm_spread):
        spread_copy.wait_sent()
    for one in (halo, dout_halo, stat_halo):
        one.wait_sent()
    late.all_to_y()
    early.finish()
    take(early.res, 0, gwo_ref, 0, 192)
    take(early.res, 192, gqkv_ref, 0, 192)
    gwo_store.start()
    query_store.start()
    late.y_to_core()
    early.wait_sent()
    quarters = []
    for step in (0, 1, 3, 2):
        y = lax.rem(p.y + step, N_Y)
        late.cg_copy(y, True).wait_recv()
        for third in range(6):
            to = pl.ds(pl.multiple_of(192 + 96 * y + 16 * third, 16), 16)
            for column in range(6):
                gqkv_ref[to, column * 128 : column * 128 + 128] = late.res[
                    column // 3, y, third * 3 + column % 3
                ]
        to = pl.ds(pl.multiple_of(192 + 96 * y, 16), 96)
        quarters.append(pltpu.make_async_copy(gqkv_ref.at[to], gqkv_out.at[to], sem_out.at[4 + step]))
        quarters[-1].start()
    late.wait_sent()
    for store in (mixed_store, gx_store, gwo_store, query_store, *quarters):
        store.wait()


def store_kernel(*refs):
    given, out, held, sems = refs[:4], refs[4:8], refs[8:12], refs[12]
    loads = [pltpu.make_async_copy(given[i], held[i], sems.at[0, i]) for i in range(4)]
    stores = [pltpu.make_async_copy(held[i], out[i], sems.at[1, i]) for i in range(4)]
    for load in loads:
        load.start()
    for load, store in zip(loads, stores):
        load.wait()
        store.start()
    for store in stores:
        store.wait()


def on_device(activations, qkv_weight, out_weight, valid, grad_y):
    bf, f32 = jnp.bfloat16, jnp.float32
    gathered = pltpu.VMEM((N_HEAD, CELLS, FULL), bf)
    pair = pltpu.SemaphoreType.DMA((2, N_HEAD))
    around = pltpu.SemaphoreType.DMA((2, 14))
    results = pl.pallas_call(
        block_kernel,
        out_shape=[
            jax.ShapeDtypeStruct((CELLS, FULL), bf),
            jax.ShapeDtypeStruct((CELLS, FULL), bf),
            jax.ShapeDtypeStruct((3 * 192, FULL), bf),
            jax.ShapeDtypeStruct((192, FULL), bf),
        ],
        in_specs=[pl.BlockSpec(memory_space=pltpu.HBM)] * 5,
        out_specs=[pl.BlockSpec(memory_space=pltpu.HBM)] * 4,
        scratch_shapes=[
            pltpu.VMEM((CELLS, FULL), bf),
            pltpu.VMEM((CELLS, FULL), bf),
            pltpu.VMEM((3 * 192, FULL), bf),
            pltpu.VMEM((192, FULL), bf),
            pltpu.VMEM((4, 192, AROUND), bf),
            pltpu.VMEM((4, 192, AROUND), bf),
            pltpu.SemaphoreType.DMA((8,)),
            pltpu.VMEM((CELLS, FULL), bf),
            pltpu.VMEM((8, N_LON), jnp.int32),
            gathered,
            gathered,
            pltpu.VMEM((CELLS, FULL), f32),
            pltpu.VMEM((CELLS, 128), f32),
            pltpu.VMEM((640, FULL), bf),
            pltpu.VMEM((256, FULL), bf),
            pltpu.VMEM((6, TALL, 640), bf),
            pltpu.VMEM((6, TALL, 256), bf),
            pltpu.VMEM((6, TALL, 128), bf),
            pltpu.VMEM((4, CELLS, AROUND), f32),
            pltpu.VMEM((4, CELLS, AROUND), f32),
            gathered,
            gathered,
            gathered,
            gathered,
            gathered,
            pltpu.SemaphoreType.DMA((11,)),
            pair,
            pair,
            pair,
            pair,
            around,
            around,
            around,
            *Summed.scratch(),
            *Summed.scratch(),
        ],
        compiler_params=pltpu.CompilerParams(
            collective_id=0, has_side_effects=True, vmem_limit_bytes=63 * 2**20
        ),
    )(
        activations.reshape(CELLS, FULL),
        grad_y.reshape(CELLS, FULL),
        qkv_weight,
        out_weight,
        valid,
    )
    mixed, grad_x, grad_qkv, grad_out = pl.pallas_call(
        store_kernel,
        out_shape=[jax.ShapeDtypeStruct(result.shape, bf) for result in results],
        in_specs=[pl.BlockSpec(memory_space=pl.ANY)] * 4,
        out_specs=[pl.BlockSpec(memory_space=pltpu.HBM)] * 4,
        scratch_shapes=[
            *(pltpu.VMEM(result.shape, bf) for result in results),
            pltpu.SemaphoreType.DMA((2, 4)),
        ],
    )(*results)
    return (
        mixed.reshape(activations.shape),
        grad_x.reshape(activations.shape),
        grad_qkv.reshape(qkv_weight.shape),
        grad_out,
    )


def solution(mesh):
    return jax.shard_map(
        on_device,
        mesh=mesh,
        in_specs=(
            P("lat", ("lon", "head"), None),
            P(None, "head", None),
            P("head", None),
            P("lat", "lon"),
            P("lat", ("lon", "head"), None),
        ),
        out_specs=(
            P("lat", ("lon", "head"), None),
            P("lat", ("lon", "head"), None),
            P(None, "head", None),
            P("head", None),
        ),
        check_vma=False,
    )
```

```python
import jax
import jax.numpy as jnp
from jax import lax
from jax.experimental import pallas as pl
from jax.experimental.pallas import tpu as pltpu
from jax.sharding import PartitionSpec as P

MESH = pl.DeviceIdType.MESH
HEAD_SIZE = 64
REACH = 6
EPSILON = 1e-05
NEGATIVE = -1e30
N_HEAD = 4
N_LAT = 4
N_LON = 32
CELLS = 64
FULL = 768
TALL = 160
AROUND = 3 * TALL
N_Z = 16
N_Y = 4
NEAR = 4
CHUNK = 5
TILES = NEAR * CHUNK


class Place:
    def __init__(self):
        self.lat = lax.axis_index("lat")
        self.lon = lax.axis_index("lon")
        self.head = lax.axis_index("head")
        self.core = lax.rem(self.lat, 2)
        self.y = (self.lon // N_Z) * 2 + self.lat // 2
        self.z = lax.rem(self.lon, N_Z)

    def at(self, core=None, y=None, z=None):
        core = self.core if core is None else core
        y = self.y if y is None else y
        z = self.z if z is None else z
        return (lax.rem(y, 2) * 2 + core, (y // 2) * N_Z + z, self.head)


    def beside(self, step_lat, step_lon):
        return (self.lat + step_lat, lax.rem(self.lon + step_lon + N_LON, N_LON), self.head)

    def peer(self, head):
        return (self.lat, self.lon, head)


def remote(src, dst, send_sem, recv_sem, device):
    return pltpu.make_async_remote_copy(
        src_ref=src,
        dst_ref=dst,
        send_sem=send_sem,
        recv_sem=recv_sem,
        device_id=device,
        device_id_type=MESH,
    )


class Summed:
    def __init__(self, place, src, res, cbuf, ybuf, nbuf, fbuf, sem_c, sem_y, sem_n, sem_f, sem_ng, sem_yg, sem_cg):
        self.p = place
        self.src, self.res, self.cbuf, self.ybuf, self.nbuf, self.fbuf = src, res, cbuf, ybuf, nbuf, fbuf
        self.sem_c, self.sem_y, self.sem_n, self.sem_f = sem_c, sem_y, sem_n, sem_f
        self.sem_ng, self.sem_yg, self.sem_cg = sem_ng, sem_yg, sem_cg
        self.two = jnp.where(place.core == 0, 2, N_Z - 2)

    @staticmethod
    def scratch():
        bf = jnp.bfloat16
        sems = pltpu.SemaphoreType.DMA
        return [
            pltpu.VMEM((2, N_Y, TILES, 16, 128), bf),
            pltpu.VMEM((2, N_Y, TILES, 16, 128), bf),
            pltpu.VMEM((N_Y, TILES, 16, 128), bf),
            pltpu.VMEM((N_Y, TILES, 16, 128), bf),
            pltpu.VMEM((NEAR, CHUNK, 16, 128), bf),
            pltpu.VMEM((NEAR, CHUNK, 16, 128), bf),
            sems((2,)),
            sems((2, N_Y, NEAR)),
            sems((2, NEAR)),
            sems((2, NEAR)),
            sems((2, NEAR)),
            sems((2, N_Y, NEAR)),
            sems((2, N_Y)),
        ]

    def clear(self):
        for ref in (self.src,):
            ref[:, :, 18:TILES] = jnp.zeros((2, N_Y, TILES - 18, 16, 128), jnp.bfloat16)

    def chunk(self, away):
        return lax.rem(self.p.z + away, NEAR)

    def tiles(self, away):
        return pl.ds(CHUNK * self.chunk(away), CHUNK)

    def along(self, away):
        step = {1: 1, 2: self.two, 3: N_Z - 1}[away]
        return lax.rem(self.p.z + step, N_Z), lax.rem(self.p.z + N_Z - step, N_Z)

    def core_copy(self):
        p = self.p
        return remote(
            self.src.at[1 - p.core], self.cbuf, self.sem_c.at[0], self.sem_c.at[1], p.at(core=1 - p.core)
        )

    def y_copy(self, step, away, arriving=False):
        p = self.p
        y = lax.rem(p.y + step, N_Y)
        slot = y if arriving else p.y
        return remote(
            self.src.at[p.core, y, self.tiles(away)],
            self.ybuf.at[slot, self.tiles(away)],
            self.sem_y.at[0, y, away],
            self.sem_y.at[1, slot, away],
            p.at(y=y),
        )

    def near_copy(self, away):
        p = self.p
        there, _ = self.along(away)
        return remote(
            self.src.at[p.core, p.y, self.tiles(away)],
            self.nbuf.at[away],
            self.sem_n.at[0, away],
            self.sem_n.at[1, away],
            p.at(z=there),
        )

    def far_copy(self, step, arriving=False):
        p = self.p
        z = lax.rem(p.z + 4 * step, N_Z)
        slot = (z if arriving else p.z) // 4
        return remote(
            self.src.at[p.core, p.y, self.tiles(0)],
            self.fbuf.at[slot],
            self.sem_f.at[0, step],
            self.sem_f.at[1, slot],
            p.at(z=z),
        )

    def back_copy(self, away, arriving=False):
        p = self.p
        _, there = self.along(away)
        here = self.res.at[p.core, p.y, self.tiles(away if arriving else 0)]
        return remote(here, here, self.sem_ng.at[0, away], self.sem_ng.at[1, away], p.at(z=there))

    def yg_copy(self, step, away, arriving=False):
        p = self.p
        y = lax.rem(p.y + step, N_Y)
        slot = y if arriving else p.y
        here = self.res.at[p.core, slot, self.tiles(away)]
        return remote(here, here, self.sem_yg.at[0, y, away], self.sem_yg.at[1, slot, away], p.at(y=y))

    def cg_copy(self, y, arriving=False):
        p = self.p
        here = self.res.at[1 - p.core if arriving else p.core, y]
        return remote(here, here, self.sem_cg.at[0, y], self.sem_cg.at[1, y], p.at(core=1 - p.core))

    def send_core(self):
        self.core_copy().start()

    def core_to_y(self):
        p = self.p
        self.core_copy().wait_recv()
        for step in (2, 1, 3, 0):
            y = lax.rem(p.y + step, N_Y)
            both = self.src[p.core, y].astype(jnp.float32) + self.cbuf[y].astype(jnp.float32)
            self.src[p.core, y] = both.astype(jnp.bfloat16)
        for away in (2, 1, 3, 0):
            for step in (2, 1, 3):
                self.y_copy(step, away).start()

    def y_to_near(self):
        p = self.p
        for away in (2, 1, 3, 0):
            for step in (1, 3, 2):
                self.y_copy(step, away, True).wait_recv()
            tiles = self.tiles(away)
            total = self.src[p.core, p.y, tiles].astype(jnp.float32)
            for step in (1, 2, 3):
                total = total + self.ybuf[lax.rem(p.y + step, N_Y), tiles].astype(jnp.float32)
            self.src[p.core, p.y, tiles] = total.astype(jnp.bfloat16)
            if away:
                self.near_copy(away).start()

    def near_to_far(self):
        p = self.p
        total = self.src[p.core, p.y, self.tiles(0)].astype(jnp.float32)
        for away in (1, 3, 2):
            self.near_copy(away).wait_recv()
            total = total + self.nbuf[away].astype(jnp.float32)
        total = total.astype(jnp.bfloat16)
        self.src[p.core, p.y, self.tiles(0)] = total
        for step in (2, 1, 3):
            self.far_copy(step).start()
        self.fbuf[p.z // 4] = total

    def far_to_all(self):
        p = self.p
        for step in (1, 3, 2):
            self.far_copy(step, True).wait_recv()
        total = self.fbuf[0].astype(jnp.float32)
        for group in range(1, NEAR):
            total = total + self.fbuf[group].astype(jnp.float32)
        self.res[p.core, p.y, self.tiles(0)] = total.astype(jnp.bfloat16)
        for away in (2, 1, 3):
            self.back_copy(away).start()
        for step in (2, 1, 3):
            self.yg_copy(step, 0).start()

    def all_to_y(self):
        for away in (1, 3, 2):
            self.back_copy(away, True).wait_recv()
            for step in (2, 1, 3):
                self.yg_copy(step, away).start()
        self.cg_copy(self.p.y).start()

    def y_to_core(self):
        p = self.p
        for step in (1, 3, 2):
            for away in range(NEAR):
                self.yg_copy(step, away, True).wait_recv()
            self.cg_copy(lax.rem(p.y + step, N_Y)).start()

    def finish(self):
        for y in range(N_Y):
            self.cg_copy(y, True).wait_recv()

    def wait_sent(self):
        self.core_copy().wait_send()
        for step in (1, 2, 3):
            for away in range(NEAR):
                self.y_copy(step, away).wait_send()
                self.yg_copy(step, away).wait_send()
            self.near_copy(step).wait_send()
            self.far_copy(step).wait_send()
            self.back_copy(step).wait_send()
        for y in range(N_Y):
            self.cg_copy(y).wait_send()


def dot(a, b):
    return lax.dot_general(a, b, (((1,), (0,)), ((), ())), preferred_element_type=jnp.float32)


def dot_rows(a, b):
    return lax.dot_general(a, b, (((1,), (1,)), ((), ())), preferred_element_type=jnp.float32)


def dot_cells(a, b):
    return lax.dot_general(a, b, (((0,), (0,)), ((), ())), preferred_element_type=jnp.float32)


def half(values):
    return values.astype(jnp.bfloat16)


def wide(values):
    return values.astype(jnp.float32)


class Halo:
    def __init__(self, place, ref, sems, by_block):
        self.p, self.ref, self.sems, self.by_block = place, ref, sems, by_block

    def message(self, index, block, src_rows, dst_block, dst_rows, step_lat, step_lon):
        src = self.ref.at[block, pl.ds(*src_rows)]
        dst = self.ref.at[dst_block, pl.ds(*dst_rows)]
        device = self.p.beside(step_lat, step_lon)
        return remote(src, dst, self.sems.at[0, index], self.sems.at[1, index], device)

    def north(self, block):
        at = block + 1 if self.by_block else pl.ds(1, 4)
        return self.message(block, at, (48, 48), at, (112, 48), -1, 0)

    def south(self, block):
        at = block + 1 if self.by_block else pl.ds(1, 4)
        return self.message(4 + block, at, (64, 48), at, (0, 48), 1, 0)

    def side(self, row, east):
        src_rows, dst_rows = {0: ((48, 64), (48, 64)), -1: ((48, 48), (112, 48)), 1: ((64, 48), (0, 48))}[row]
        index = 8 + 2 * (row % 3) + east
        return self.message(index, 4 if east else 1, src_rows, 0 if east else 5, dst_rows, row, 1 if east else -1)

    def when(self, row, then):
        if row == -1:
            pl.when(self.p.lat > 0)(then)
        elif row == 1:
            pl.when(self.p.lat < N_LAT - 1)(then)
        else:
            then()

    def send_rows(self, block):
        self.when(-1, lambda: self.north(block).start())
        self.when(1, lambda: self.south(block).start())

    def send_side(self, east):
        for row in (0, -1, 1):
            self.when(row, lambda row=row: self.side(row, east).start())

    def send_all(self):
        self.send_rows(0)
        self.send_side(0)
        self.send_side(1)

    def blocks(self):
        return range(4) if self.by_block else range(1)

    def wait_all(self):
        for block in self.blocks():
            self.when(1, lambda block=block: self.north(block).wait_recv())
            self.when(-1, lambda block=block: self.south(block).wait_recv())
        for east in (0, 1):
            for row in (0, -1, 1):
                self.when(-row, lambda row=row, east=east: self.side(row, east).wait_recv())

    def wait_sent(self):
        for block in self.blocks():
            self.when(-1, lambda block=block: self.north(block).wait_send())
            self.when(1, lambda block=block: self.south(block).wait_send())
        for east in (0, 1):
            for row in (0, -1, 1):
                self.when(row, lambda row=row, east=east: self.side(row, east).wait_send())


class Spread:
    def __init__(self, place, src, dst, sems):
        self.p, self.src, self.dst, self.sems = place, src, dst, sems

    def copy(self, head):
        src = self.src.at[head] if len(self.src.shape) == 3 else self.src
        return remote(
            src, self.dst.at[self.p.head], self.sems.at[0, head], self.sems.at[1, self.p.head], self.p.peer(head)
        )

    def arrival(self, head):
        src = self.src.at[head] if len(self.src.shape) == 3 else self.src
        return remote(src, self.dst.at[head], self.sems.at[0, head], self.sems.at[1, head], self.p.peer(head))

    def other(self, step):
        return lax.rem(self.p.head + step, N_HEAD)

    def wait_sent(self):
        for step in (1, 2, 3):
            self.copy(self.other(step)).wait_send()


def geometry(shape):
    row = lax.broadcasted_iota(jnp.int32, shape, 0)
    lane = lax.broadcasted_iota(jnp.int32, shape, 1)
    block = jnp.where(lane >= TALL, 1, 0) + jnp.where(lane >= 2 * TALL, 1, 0)
    rest = lane - TALL * block
    lat = (rest >> 3) - REACH
    step_lat = lat - (row >> 3)
    step_lon = (block - 1) * 8 + (rest & 7) - (row & 7)
    return lat, step_lat, step_lon


def place_of(row, column):
    return column // 3, row // 96, row % 96 // 16 * 3 + column % 3


def put(src, top, values):
    for row in range(0, values.shape[0], 16):
        for column in range(6):
            src[place_of(top + row, column)] = half(values[row : row + 16, column * 128 : column * 128 + 128])


def take(res, top, out_ref, out_top, rows):
    for row in range(0, rows, 16):
        for column in range(6):
            out_ref[out_top + row : out_top + row + 16, column * 128 : column * 128 + 128] = res[
                place_of(top + row, column)
            ]


N_SUM = 13


def block_kernel(
    x_ref, gy_ref, wqkv_ref, wo_ref, valid_ref, mixed_out, gx_out, gqkv_out, gwo_out,
    mixed_ref, gx_ref, gqkv_ref, gwo_ref, wpt, wopt, soft_v, soft_grad_v, sem_out, xv, valid_v, ng, gg, norm32, spread, wp, wop, ext, dext, stats, mask_q, mask_k, gp, pvs, pvr, gns, gnr,
    sem_in, sem_n, sem_g, sem_pv, sem_gn, sem_ext, sem_dext, sem_stats, *sums,
):
    p = Place()
    barrier = pltpu.get_barrier_semaphore()
    loads = [
        pltpu.make_async_copy(src, dst, sem_in.at[index])
        for index, (src, dst) in enumerate(
            (
                (x_ref, xv),
                (valid_ref, valid_v),
                (gy_ref, gg.at[p.head]),
                (wqkv_ref.at[0, pl.ds(0, 128)], wp.at[pl.ds(0, 128)]),
                (wqkv_ref.at[1, pl.ds(0, 128)], wp.at[pl.ds(128, 128)]),
                (wqkv_ref.at[2, pl.ds(0, 128)], wp.at[pl.ds(256, 128)]),
                (wqkv_ref.at[0, pl.ds(128, 64)], wp.at[pl.ds(384, 64)]),
                (wqkv_ref.at[1, pl.ds(128, 64)], wp.at[pl.ds(512, 64)]),
                (wqkv_ref.at[2, pl.ds(128, 64)], wp.at[pl.ds(576, 64)]),
                (wo_ref.at[pl.ds(0, 128)], wop.at[pl.ds(0, 128)]),
                (wo_ref.at[pl.ds(128, 64)], wop.at[pl.ds(192, 64)]),
            )
        )
    ]

    query_rows = pl.ds(0, 192)
    mixed_store, gx_store, gwo_store, query_store = [
        pltpu.make_async_copy(src, dst, sem_out.at[index])
        for index, (src, dst) in enumerate(
            (
                (mixed_ref, mixed_out),
                (gx_ref, gx_out),
                (gwo_ref, gwo_out),
                (gqkv_ref.at[query_rows], gqkv_out.at[query_rows]),
            )
        )
    ]

    def greet(device):
        pl.semaphore_signal(barrier, inc=1, device_id=device, device_id_type=MESH)

    for load in loads[:3]:
        load.start()
    for step in range(1, N_HEAD):
        greet(p.peer(lax.rem(p.head + step, N_HEAD)))
    for step_lon in (-1, 0, 1):
        if step_lon:
            greet(p.beside(0, step_lon))

        @pl.when(p.lat > 0)
        def _():
            greet(p.beside(-1, step_lon))

        @pl.when(p.lat < N_LAT - 1)
        def _():
            greet(p.beside(1, step_lon))

    for step in range(1, N_Y):
        greet(p.at(y=lax.rem(p.y + step, N_Y)))

    for step in (1, 2, 4, 8, 12, 14, 15):
        greet(p.at(z=lax.rem(p.z + step, N_Z)))

    early = Summed(p, *sums[:N_SUM])
    late = Summed(p, *sums[N_SUM:])
    normed_gather = Spread(p, ng.at[p.head], ng, sem_n)
    grad_gather = Spread(p, gg.at[p.head], gg, sem_g)
    halo = Halo(p, ext, sem_ext, True)
    dout_halo = Halo(p, dext, sem_dext, True)
    stat_halo = Halo(p, stats, sem_stats, False)

    loads[0].wait()
    values = wide(xv[...])
    center = values - jnp.mean(values, axis=-1, keepdims=True)
    inv = lax.rsqrt(jnp.mean(center * center, axis=-1, keepdims=True) + EPSILON)
    norm32[...] = center * inv
    spread[...] = jnp.broadcast_to(inv, spread.shape)
    ng[p.head] = half(center * inv)
    greeted = 3 + 2 + (N_Y - 1) + 7
    edge = jnp.where(p.lat > 0, 3, 0) + jnp.where(p.lat < N_LAT - 1, 3, 0)
    pl.semaphore_wait(barrier, greeted + edge)

    for step in (1, 3, 2):
        normed_gather.copy(normed_gather.other(step)).start()
    for load in loads[3:]:
        load.start()
    loads[2].wait()
    for step in (1, 3, 2):
        grad_gather.copy(grad_gather.other(step)).start()

    loads[1].wait()
    low = lax.broadcasted_iota(jnp.int32, (CELLS, 128), 1) < HEAD_SIZE
    zero = jnp.zeros((CELLS, 128), jnp.bfloat16)
    lane = lax.broadcasted_iota(jnp.int32, (CELLS, 128), 1)
    lat, step_lat, step_lon = geometry((CELLS, AROUND))
    inside = (jnp.abs(step_lat) <= REACH) & (jnp.abs(step_lon) <= REACH)
    middle = (step_lat == 0) & (step_lon == 0)
    there = lat + p.lat * 8
    inside_rows = inside & (there >= 0) & (there < 8 * N_LAT)
    row = lax.broadcasted_iota(jnp.int32, (CELLS, 8), 0)
    column = lax.broadcasted_iota(jnp.int32, (CELLS, 8), 1)
    by_lat = dot(half(jnp.where((row >> 3) == column, 1.0, 0.0)), half(wide(valid_v[...])))
    row = lax.broadcasted_iota(jnp.int32, (CELLS, N_LON), 0)
    column = lax.broadcasted_iota(jnp.int32, (CELLS, N_LON), 1)
    for block in range(4):
        own_flag = half(jnp.where(column == 8 * block + (row & 7), by_lat, 0.0))
        flag = dot(own_flag, jnp.ones((N_LON, 128), jnp.bfloat16))
        ext[block + 1, 48:112, 512:640] = half(flag)
        mask_k[block] = jnp.where(inside_rows & ((flag[:, 0:1] > 0) | middle), 0.0, NEGATIVE)

    for top, at_edge in ((0, p.lat == 0), (112, p.lat == N_LAT - 1)):

        @pl.when(at_edge)
        def _():
            for ref in (ext, dext, stats):
                ref[:, top : top + 48, :] = jnp.zeros((6, 48, ref.shape[2]), jnp.bfloat16)

    early.clear()
    late.clear()
    wp[448:512] = jnp.zeros((64, FULL), jnp.bfloat16)
    wop[128:192] = jnp.zeros((64, FULL), jnp.bfloat16)
    for load in loads[3:]:
        load.wait()
    wpt[...] = wp[...].T
    wopt[...] = wop[...].T

    def first(values):
        return jnp.where(low, values, zero)

    def second(values):
        return jnp.where(low, zero, values)

    def arrived(step, gather, margins, project):
        order = jnp.where(step == 2, 3, jnp.where(step == 3, 2, step))
        block = lax.rem(p.head + order, N_HEAD)

        @pl.when(step > 0)
        def _():
            gather.arrival(block).wait_recv()

        project(block)
        margins.send_rows(block)

        @pl.when(block == 0)
        def _():
            margins.send_side(0)

        @pl.when(block == 3)
        def _():
            margins.send_side(1)

    def project_normed(block):
        projected = dot(ng[block], wpt[...])
        scale = HEAD_SIZE ** (-0.5)
        ext[block + 1, 48:112, 0:128] = half(half(projected[:, 0:128]) * scale)
        ext[block + 1, 48:112, 128:384] = half(projected[:, 128:384])
        ext[block + 1, 48:112, 384:512] = half(projected[:, 512:640])
        ext[block + 1, 48:112, 512:640] = jnp.where(
            low, half(projected[:, 384:512] * scale), ext[block + 1, 48:112, 512:640]
        )

    def project_grad(block):
        dext[block + 1, 48:112] = half(dot(gg[block], wopt[...]))

    @pl.loop(0, N_HEAD)
    def _(step):
        arrived(step, normed_gather, halo, project_normed)

    @pl.loop(0, N_HEAD)
    def _(step):
        arrived(step, grad_gather, dout_halo, project_grad)

    halo.wait_all()
    pick = half(jnp.where(lane == HEAD_SIZE, 1.0, 0.0))
    for block in range(4):
        flag = dot_rows(pick, ext[block : block + 3, :, 512:640].reshape(AROUND, 128))
        mask_q[block] = jnp.where(inside & ((flag > 0) | middle), 0.0, NEGATIVE)
    dout_halo.wait_all()

    def stacked(a, b, c):
        return jnp.concatenate(
            [jnp.concatenate(part, axis=1) for part in (a, b, c)],
            axis=0,
        )

    def thrice(mask):
        return jnp.concatenate([mask, mask, mask], axis=0)

    def around(block, *groups):
        parts = [
            ref[pl.ds(block, 3), :, group * 128 : group * 128 + 128].reshape(AROUND, 128) for ref, group in groups
        ]
        return jnp.concatenate(parts, axis=1)

    def own(block, ref, group):
        return ref[block + 1, 48:112, group * 128 : group * 128 + 128]

    Q01, K01, V01, KV2, Q2 = ((ext, group) for group in range(5))
    D01, D2 = (dext, 0), (dext, 1)
    STAT = (stats, 0)

    def queries_side(block):
        keys, values = around(block, K01, KV2), around(block, V01, KV2)
        q01, d01 = own(block, *Q01), own(block, *D01)
        queries = stacked((first(q01), zero), (second(q01), zero), (zero, first(own(block, *Q2))))
        douts = stacked((first(d01), zero), (second(d01), zero), (zero, own(block, *D2)))
        score = dot_rows(queries, keys) + thrice(mask_q[block])
        best = jnp.max(score, axis=1, keepdims=True)
        chance = jnp.exp(score - best)
        total = jnp.sum(chance, axis=1, keepdims=True)
        level = best + jnp.log(total)
        chance = chance * (1.0 / total)
        inner = dot_rows(douts, values)
        carried = jnp.sum(chance * inner, axis=1, keepdims=True)
        soft_grad = half(chance * (inner - carried))
        soft_v[block] = half(chance)
        soft_grad_v[block] = soft_grad
        tile = jnp.zeros((CELLS, 128), jnp.float32)
        for kind, column in enumerate((level, carried)):
            for head in range(3):
                rest = column[64 * head : 64 * head + 64]
                for digit in range(3):
                    piece = wide(half(rest))
                    rest = rest - piece
                    tile = jnp.where(lane == 9 * kind + 3 * head + digit, piece, tile)
        stats[block + 1, 48:112] = half(tile)

    def queries_rest(block):
        keys, values = around(block, K01, KV2), around(block, V01, KV2)
        attended = dot(soft_v[block], values)
        grad_query = dot(soft_grad_v[block], keys) * HEAD_SIZE ** (-0.5)
        gp[block, :, 640:768] = half(jnp.where(low, attended[0:64, 0:128], attended[64:128, 0:128]))
        gp[block, :, 0:128] = half(jnp.where(low, grad_query[0:64, 0:128], grad_query[64:128, 0:128]))
        gp[block, :, 384:512] = half(jnp.where(low, grad_query[128:192, 128:256], attended[128:192, 128:256]))

    for block in range(4):
        queries_side(block)
    stat_halo.send_all()
    for block in range(4):
        queries_rest(block)

    def cells(ref, *groups):
        return jnp.concatenate([ref[:, :, g * 128 : g * 128 + 128].reshape(4 * CELLS, 128) for g in groups], axis=1)

    grads = gg[...].reshape(4 * CELLS, FULL)
    normed = ng[...].reshape(4 * CELLS, FULL)
    mixed_in = cells(gp, 5, 3)
    weights = dot_cells(mixed_in, grads)
    put(early.src, 0, weights[0:128])
    put(early.src, 128, weights[192:256])
    weights = dot_cells(cells(gp, 0, 3), normed)
    put(early.src, 192, weights[0:192])
    early.send_core()

    out_spread = Spread(p, pvs, pvr, sem_pv)
    pvs[...] = half(dot(mixed_in, wop[...])).reshape(4, CELLS, FULL)
    for step in (2, 1, 3):
        out_spread.copy(out_spread.other(step)).start()
    early.core_to_y()
    stat_halo.wait_all()

    def minus_one(start):
        return half(jnp.where((lane >= start) & (lane < start + 3), -1.0, 0.0))

    def keys_side(block):
        queries, douts = around(block, Q01, Q2, STAT), around(block, D01, D2, STAT)
        k01, v01, kv2 = own(block, *K01), own(block, *V01), own(block, *KV2)
        keys = stacked(
            (first(k01), zero, minus_one(0)), (second(k01), zero, minus_one(3)), (zero, first(kv2), minus_one(6))
        )
        values = stacked(
            (first(v01), zero, minus_one(9)), (second(v01), zero, minus_one(12)), (zero, second(kv2), minus_one(15))
        )
        chance = jnp.exp(dot_rows(keys, queries) + thrice(mask_k[block]))
        soft_grad = half(chance * dot_rows(values, douts))
        grad_key = dot(soft_grad, queries[:, 0:256])
        grad_value = dot(half(chance), douts[:, 0:256])
        gp[block, :, 128:256] = half(jnp.where(low, grad_key[0:64, 0:128], grad_key[64:128, 0:128]))
        gp[block, :, 256:384] = half(jnp.where(low, grad_value[0:64, 0:128], grad_value[64:128, 0:128]))
        gp[block, :, 512:640] = half(jnp.where(low, grad_key[128:192, 128:256], grad_value[128:192, 128:256]))

    for block in range(4):
        keys_side(block)

    weights = dot_cells(cells(gp, 1, 4), normed)
    put(late.src, 0, weights[0:192])
    weights = jnp.concatenate([dot_cells(cells(gp, 2), normed), weights[192:256]], axis=0)
    put(late.src, 192, weights)
    late.send_core()
    early.y_to_near()

    late.core_to_y()

    norm_spread = Spread(p, gns, gnr, sem_gn)
    gns[...] = half(dot(cells(gp, 0, 1, 2, 3, 4), wp[...])).reshape(4, CELLS, FULL)
    for step in (2, 1, 3):
        norm_spread.copy(norm_spread.other(step)).start()

    early.near_to_far()

    late.y_to_near()
    late.near_to_far()
    early.far_to_all()

    total = wide(pvs[p.head])
    for step in (1, 2, 3):
        other = out_spread.other(step)
        out_spread.arrival(other).wait_recv()
        total = total + wide(pvr[other])
    mixed_ref[...] = half(wide(xv[...]) + total)
    mixed_store.start()

    total = wide(gns[p.head])
    for step in (1, 2, 3):
        other = norm_spread.other(step)
        norm_spread.arrival(other).wait_recv()
        total = total + wide(gnr[other])
    own_norm = norm32[...]
    mean = jnp.mean(total, axis=-1, keepdims=True)
    along = jnp.mean(total * own_norm, axis=-1, keepdims=True)
    d_input = spread[:, 0:1] * (total - mean - own_norm * along)
    gx_ref[...] = half(wide(gg[p.head]) + d_input)
    gx_store.start()


    early.all_to_y()
    late.far_to_all()
    early.y_to_core()
    for spread_copy in (normed_gather, grad_gather, out_spread, norm_spread):
        spread_copy.wait_sent()
    for one in (halo, dout_halo, stat_halo):
        one.wait_sent()
    late.all_to_y()
    early.finish()
    take(early.res, 0, gwo_ref, 0, 192)
    take(early.res, 192, gqkv_ref, 0, 192)
    gwo_store.start()
    query_store.start()
    late.y_to_core()
    early.wait_sent()
    quarters = []
    for step in (0, 1, 3, 2):
        y = lax.rem(p.y + step, N_Y)
        late.cg_copy(y, True).wait_recv()
        for third in range(6):
            to = pl.ds(pl.multiple_of(192 + 96 * y + 16 * third, 16), 16)
            for column in range(6):
                gqkv_ref[to, column * 128 : column * 128 + 128] = late.res[
                    column // 3, y, third * 3 + column % 3
                ]
        to = pl.ds(pl.multiple_of(192 + 96 * y, 16), 96)
        quarters.append(pltpu.make_async_copy(gqkv_ref.at[to], gqkv_out.at[to], sem_out.at[4 + step]))
        quarters[-1].start()
    late.wait_sent()
    for store in (mixed_store, gx_store, gwo_store, query_store, *quarters):
        store.wait()


def store_kernel(*refs):
    given, out, held, sems = refs[:4], refs[4:8], refs[8:12], refs[12]
    loads = [pltpu.make_async_copy(given[i], held[i], sems.at[0, i]) for i in range(4)]
    stores = [pltpu.make_async_copy(held[i], out[i], sems.at[1, i]) for i in range(4)]
    for load in loads:
        load.start()
    for load, store in zip(loads, stores):
        load.wait()
        store.start()
    for store in stores:
        store.wait()


def on_device(activations, qkv_weight, out_weight, valid, grad_y):
    bf, f32 = jnp.bfloat16, jnp.float32
    gathered = pltpu.VMEM((N_HEAD, CELLS, FULL), bf)
    pair = pltpu.SemaphoreType.DMA((2, N_HEAD))
    around = pltpu.SemaphoreType.DMA((2, 14))
    results = pl.pallas_call(
        block_kernel,
        out_shape=[
            jax.ShapeDtypeStruct((CELLS, FULL), bf),
            jax.ShapeDtypeStruct((CELLS, FULL), bf),
            jax.ShapeDtypeStruct((3 * 192, FULL), bf),
            jax.ShapeDtypeStruct((192, FULL), bf),
        ],
        in_specs=[pl.BlockSpec(memory_space=pltpu.HBM)] * 5,
        out_specs=[pl.BlockSpec(memory_space=pltpu.HBM)] * 4,
        scratch_shapes=[
            pltpu.VMEM((CELLS, FULL), bf),
            pltpu.VMEM((CELLS, FULL), bf),
            pltpu.VMEM((3 * 192, FULL), bf),
            pltpu.VMEM((192, FULL), bf),
            pltpu.VMEM((FULL, 640), bf),
            pltpu.VMEM((FULL, 256), bf),
            pltpu.VMEM((4, 192, AROUND), bf),
            pltpu.VMEM((4, 192, AROUND), bf),
            pltpu.SemaphoreType.DMA((8,)),
            pltpu.VMEM((CELLS, FULL), bf),
            pltpu.VMEM((8, N_LON), jnp.int32),
            gathered,
            gathered,
            pltpu.VMEM((CELLS, FULL), f32),
            pltpu.VMEM((CELLS, 128), f32),
            pltpu.VMEM((640, FULL), bf),
            pltpu.VMEM((256, FULL), bf),
            pltpu.VMEM((6, TALL, 640), bf),
            pltpu.VMEM((6, TALL, 256), bf),
            pltpu.VMEM((6, TALL, 128), bf),
            pltpu.VMEM((4, CELLS, AROUND), f32),
            pltpu.VMEM((4, CELLS, AROUND), f32),
            gathered,
            gathered,
            gathered,
            gathered,
            gathered,
            pltpu.SemaphoreType.DMA((11,)),
            pair,
            pair,
            pair,
            pair,
            around,
            around,
            around,
            *Summed.scratch(),
            *Summed.scratch(),
        ],
        compiler_params=pltpu.CompilerParams(
            collective_id=0, has_side_effects=True, vmem_limit_bytes=63 * 2**20
        ),
    )(
        activations.reshape(CELLS, FULL),
        grad_y.reshape(CELLS, FULL),
        qkv_weight,
        out_weight,
        valid,
    )
    mixed, grad_x, grad_qkv, grad_out = pl.pallas_call(
        store_kernel,
        out_shape=[jax.ShapeDtypeStruct(result.shape, bf) for result in results],
        in_specs=[pl.BlockSpec(memory_space=pl.ANY)] * 4,
        out_specs=[pl.BlockSpec(memory_space=pltpu.HBM)] * 4,
        scratch_shapes=[
            *(pltpu.VMEM(result.shape, bf) for result in results),
            pltpu.SemaphoreType.DMA((2, 4)),
        ],
    )(*results)
    return (
        mixed.reshape(activations.shape),
        grad_x.reshape(activations.shape),
        grad_qkv.reshape(qkv_weight.shape),
        grad_out,
    )


def solution(mesh):
    return jax.shard_map(
        on_device,
        mesh=mesh,
        in_specs=(
            P("lat", ("lon", "head"), None),
            P(None, "head", None),
            P("head", None),
            P("lat", "lon"),
            P("lat", ("lon", "head"), None),
        ),
        out_specs=(
            P("lat", ("lon", "head"), None),
            P("lat", ("lon", "head"), None),
            P(None, "head", None),
            P("head", None),
        ),
        check_vma=False,
    )
```

```python
import jax
import jax.numpy as jnp
from jax import lax
from jax.experimental import pallas as pl
from jax.experimental.pallas import tpu as pltpu
from jax.sharding import PartitionSpec as P

MESH = pl.DeviceIdType.MESH
HEAD_SIZE = 64
REACH = 6
EPSILON = 1e-05
NEGATIVE = -1e30
N_HEAD = 4
N_LAT = 4
N_LON = 32
CELLS = 64
FULL = 768
TALL = 160
AROUND = 3 * TALL
N_Z = 16
N_Y = 4
NEAR = 4
CHUNK = 5
TILES = NEAR * CHUNK


class Place:
    def __init__(self):
        self.lat = lax.axis_index("lat")
        self.lon = lax.axis_index("lon")
        self.head = lax.axis_index("head")
        self.core = lax.rem(self.lat, 2)
        self.y = (self.lon // N_Z) * 2 + self.lat // 2
        self.z = lax.rem(self.lon, N_Z)

    def at(self, core=None, y=None, z=None):
        core = self.core if core is None else core
        y = self.y if y is None else y
        z = self.z if z is None else z
        return (lax.rem(y, 2) * 2 + core, (y // 2) * N_Z + z, self.head)


    def beside(self, step_lat, step_lon):
        return (self.lat + step_lat, lax.rem(self.lon + step_lon + N_LON, N_LON), self.head)

    def peer(self, head):
        return (self.lat, self.lon, head)


def remote(src, dst, send_sem, recv_sem, device):
    return pltpu.make_async_remote_copy(
        src_ref=src,
        dst_ref=dst,
        send_sem=send_sem,
        recv_sem=recv_sem,
        device_id=device,
        device_id_type=MESH,
    )


class Summed:
    def __init__(self, place, src, res, cbuf, ybuf, nbuf, fbuf, sem_c, sem_y, sem_n, sem_f, sem_ng, sem_yg, sem_cg):
        self.p = place
        self.src, self.res, self.cbuf, self.ybuf, self.nbuf, self.fbuf = src, res, cbuf, ybuf, nbuf, fbuf
        self.sem_c, self.sem_y, self.sem_n, self.sem_f = sem_c, sem_y, sem_n, sem_f
        self.sem_ng, self.sem_yg, self.sem_cg = sem_ng, sem_yg, sem_cg
        self.two = jnp.where(place.core == 0, 2, N_Z - 2)

    @staticmethod
    def scratch():
        bf = jnp.bfloat16
        sems = pltpu.SemaphoreType.DMA
        return [
            pltpu.VMEM((2, N_Y, TILES, 16, 128), bf),
            pltpu.VMEM((2, N_Y, TILES, 16, 128), bf),
            pltpu.VMEM((N_Y, TILES, 16, 128), bf),
            pltpu.VMEM((N_Y, TILES, 16, 128), bf),
            pltpu.VMEM((NEAR, CHUNK, 16, 128), bf),
            pltpu.VMEM((NEAR, CHUNK, 16, 128), bf),
            sems((2,)),
            sems((2, N_Y, NEAR)),
            sems((2, NEAR)),
            sems((2, NEAR)),
            sems((2, NEAR)),
            sems((2, N_Y, NEAR)),
            sems((2, N_Y)),
        ]

    def clear(self):
        for ref in (self.src,):
            ref[:, :, 18:TILES] = jnp.zeros((2, N_Y, TILES - 18, 16, 128), jnp.bfloat16)

    def chunk(self, away):
        return lax.rem(self.p.z + away, NEAR)

    def tiles(self, away):
        return pl.ds(CHUNK * self.chunk(away), CHUNK)

    def along(self, away):
        step = {1: 1, 2: self.two, 3: N_Z - 1}[away]
        return lax.rem(self.p.z + step, N_Z), lax.rem(self.p.z + N_Z - step, N_Z)

    def core_copy(self):
        p = self.p
        return remote(
            self.src.at[1 - p.core], self.cbuf, self.sem_c.at[0], self.sem_c.at[1], p.at(core=1 - p.core)
        )

    def y_copy(self, step, away, arriving=False):
        p = self.p
        y = lax.rem(p.y + step, N_Y)
        slot = y if arriving else p.y
        return remote(
            self.src.at[p.core, y, self.tiles(away)],
            self.ybuf.at[slot, self.tiles(away)],
            self.sem_y.at[0, y, away],
            self.sem_y.at[1, slot, away],
            p.at(y=y),
        )

    def near_copy(self, away):
        p = self.p
        there, _ = self.along(away)
        return remote(
            self.src.at[p.core, p.y, self.tiles(away)],
            self.nbuf.at[away],
            self.sem_n.at[0, away],
            self.sem_n.at[1, away],
            p.at(z=there),
        )

    def far_copy(self, step, arriving=False):
        p = self.p
        z = lax.rem(p.z + 4 * step, N_Z)
        slot = (z if arriving else p.z) // 4
        return remote(
            self.src.at[p.core, p.y, self.tiles(0)],
            self.fbuf.at[slot],
            self.sem_f.at[0, step],
            self.sem_f.at[1, slot],
            p.at(z=z),
        )

    def back_copy(self, away, arriving=False):
        p = self.p
        _, there = self.along(away)
        here = self.res.at[p.core, p.y, self.tiles(away if arriving else 0)]
        return remote(here, here, self.sem_ng.at[0, away], self.sem_ng.at[1, away], p.at(z=there))

    def yg_copy(self, step, away, arriving=False):
        p = self.p
        y = lax.rem(p.y + step, N_Y)
        slot = y if arriving else p.y
        here = self.res.at[p.core, slot, self.tiles(away)]
        return remote(here, here, self.sem_yg.at[0, y, away], self.sem_yg.at[1, slot, away], p.at(y=y))

    def cg_copy(self, y, arriving=False):
        p = self.p
        here = self.res.at[1 - p.core if arriving else p.core, y]
        return remote(here, here, self.sem_cg.at[0, y], self.sem_cg.at[1, y], p.at(core=1 - p.core))

    def send_core(self):
        self.core_copy().start()

    def core_to_y(self):
        p = self.p
        self.core_copy().wait_recv()
        for step in (2, 1, 3, 0):
            y = lax.rem(p.y + step, N_Y)
            both = self.src[p.core, y].astype(jnp.float32) + self.cbuf[y].astype(jnp.float32)
            self.src[p.core, y] = both.astype(jnp.bfloat16)
        for away in (2, 1, 3, 0):
            for step in (2, 1, 3):
                self.y_copy(step, away).start()

    def y_to_near(self):
        p = self.p
        for away in (2, 1, 3, 0):
            for step in (1, 3, 2):
                self.y_copy(step, away, True).wait_recv()
            tiles = self.tiles(away)
            total = self.src[p.core, p.y, tiles].astype(jnp.float32)
            for step in (1, 2, 3):
                total = total + self.ybuf[lax.rem(p.y + step, N_Y), tiles].astype(jnp.float32)
            self.src[p.core, p.y, tiles] = total.astype(jnp.bfloat16)
            if away:
                self.near_copy(away).start()

    def near_to_far(self):
        p = self.p
        total = self.src[p.core, p.y, self.tiles(0)].astype(jnp.float32)
        for away in (1, 3, 2):
            self.near_copy(away).wait_recv()
            total = total + self.nbuf[away].astype(jnp.float32)
        total = total.astype(jnp.bfloat16)
        self.src[p.core, p.y, self.tiles(0)] = total
        for step in (2, 1, 3):
            self.far_copy(step).start()
        self.fbuf[p.z // 4] = total

    def far_to_all(self):
        p = self.p
        for step in (1, 3, 2):
            self.far_copy(step, True).wait_recv()
        total = self.fbuf[0].astype(jnp.float32)
        for group in range(1, NEAR):
            total = total + self.fbuf[group].astype(jnp.float32)
        self.res[p.core, p.y, self.tiles(0)] = total.astype(jnp.bfloat16)
        for away in (2, 1, 3):
            self.back_copy(away).start()
        for step in (2, 1, 3):
            self.yg_copy(step, 0).start()

    def all_to_y(self):
        for away in (1, 3, 2):
            self.back_copy(away, True).wait_recv()
            for step in (2, 1, 3):
                self.yg_copy(step, away).start()
        self.cg_copy(self.p.y).start()

    def y_to_core(self):
        p = self.p
        for step in (1, 3, 2):
            for away in range(NEAR):
                self.yg_copy(step, away, True).wait_recv()
            self.cg_copy(lax.rem(p.y + step, N_Y)).start()

    def finish(self):
        for y in range(N_Y):
            self.cg_copy(y, True).wait_recv()

    def wait_sent(self):
        self.core_copy().wait_send()
        for step in (1, 2, 3):
            for away in range(NEAR):
                self.y_copy(step, away).wait_send()
                self.yg_copy(step, away).wait_send()
            self.near_copy(step).wait_send()
            self.far_copy(step).wait_send()
            self.back_copy(step).wait_send()
        for y in range(N_Y):
            self.cg_copy(y).wait_send()


def dot(a, b):
    return lax.dot_general(a, b, (((1,), (0,)), ((), ())), preferred_element_type=jnp.float32)


def dot_rows(a, b):
    return lax.dot_general(a, b, (((1,), (1,)), ((), ())), preferred_element_type=jnp.float32)


def dot_cells(a, b):
    return lax.dot_general(a, b, (((0,), (0,)), ((), ())), preferred_element_type=jnp.float32)


def half(values):
    return values.astype(jnp.bfloat16)


def wide(values):
    return values.astype(jnp.float32)


class Halo:
    def __init__(self, place, ref, sems, by_block):
        self.p, self.ref, self.sems, self.by_block = place, ref, sems, by_block

    def message(self, index, block, src_rows, dst_block, dst_rows, step_lat, step_lon):
        src = self.ref.at[block, pl.ds(*src_rows)]
        dst = self.ref.at[dst_block, pl.ds(*dst_rows)]
        device = self.p.beside(step_lat, step_lon)
        return remote(src, dst, self.sems.at[0, index], self.sems.at[1, index], device)

    def north(self, block):
        at = block + 1 if self.by_block else pl.ds(1, 4)
        return self.message(block, at, (48, 48), at, (112, 48), -1, 0)

    def south(self, block):
        at = block + 1 if self.by_block else pl.ds(1, 4)
        return self.message(4 + block, at, (64, 48), at, (0, 48), 1, 0)

    def side(self, row, east):
        src_rows, dst_rows = {0: ((48, 64), (48, 64)), -1: ((48, 48), (112, 48)), 1: ((64, 48), (0, 48))}[row]
        index = 8 + 2 * (row % 3) + east
        return self.message(index, 4 if east else 1, src_rows, 0 if east else 5, dst_rows, row, 1 if east else -1)

    def when(self, row, then):
        if row == -1:
            pl.when(self.p.lat > 0)(then)
        elif row == 1:
            pl.when(self.p.lat < N_LAT - 1)(then)
        else:
            then()

    def send_rows(self, block):
        self.when(-1, lambda: self.north(block).start())
        self.when(1, lambda: self.south(block).start())

    def send_side(self, east):
        for row in (0, -1, 1):
            self.when(row, lambda row=row: self.side(row, east).start())

    def send_all(self):
        self.send_rows(0)
        self.send_side(0)
        self.send_side(1)

    def blocks(self):
        return range(4) if self.by_block else range(1)

    def wait_all(self):
        for block in self.blocks():
            self.when(1, lambda block=block: self.north(block).wait_recv())
            self.when(-1, lambda block=block: self.south(block).wait_recv())
        for east in (0, 1):
            for row in (0, -1, 1):
                self.when(-row, lambda row=row, east=east: self.side(row, east).wait_recv())

    def wait_sent(self):
        for block in self.blocks():
            self.when(-1, lambda block=block: self.north(block).wait_send())
            self.when(1, lambda block=block: self.south(block).wait_send())
        for east in (0, 1):
            for row in (0, -1, 1):
                self.when(row, lambda row=row, east=east: self.side(row, east).wait_send())


class Spread:
    def __init__(self, place, src, dst, sems):
        self.p, self.src, self.dst, self.sems = place, src, dst, sems

    def copy(self, head):
        src = self.src.at[head] if len(self.src.shape) == 3 else self.src
        return remote(
            src, self.dst.at[self.p.head], self.sems.at[0, head], self.sems.at[1, self.p.head], self.p.peer(head)
        )

    def arrival(self, head):
        src = self.src.at[head] if len(self.src.shape) == 3 else self.src
        return remote(src, self.dst.at[head], self.sems.at[0, head], self.sems.at[1, head], self.p.peer(head))

    def other(self, step):
        return lax.rem(self.p.head + step, N_HEAD)

    def wait_sent(self):
        for step in (1, 2, 3):
            self.copy(self.other(step)).wait_send()


def geometry(shape):
    row = lax.broadcasted_iota(jnp.int32, shape, 0)
    lane = lax.broadcasted_iota(jnp.int32, shape, 1)
    block = jnp.where(lane >= TALL, 1, 0) + jnp.where(lane >= 2 * TALL, 1, 0)
    rest = lane - TALL * block
    lat = (rest >> 3) - REACH
    step_lat = lat - (row >> 3)
    step_lon = (block - 1) * 8 + (rest & 7) - (row & 7)
    return lat, step_lat, step_lon


def place_of(row, column):
    return column // 3, row // 96, row % 96 // 16 * 3 + column % 3


def put(src, top, values):
    for row in range(0, values.shape[0], 16):
        for column in range(6):
            src[place_of(top + row, column)] = half(values[row : row + 16, column * 128 : column * 128 + 128])


def take(res, top, out_ref, out_top, rows):
    for row in range(0, rows, 16):
        for column in range(6):
            out_ref[out_top + row : out_top + row + 16, column * 128 : column * 128 + 128] = res[
                place_of(top + row, column)
            ]


N_SUM = 13


def block_kernel(
    x_ref, gy_ref, wqkv_ref, wo_ref, valid_ref, mixed_out, gx_out, gqkv_out, gwo_out,
    mixed_ref, gx_ref, gqkv_ref, gwo_ref, wpt, wopt, soft_v, soft_grad_v, sem_out, xv, valid_v, ng, gg, norm32, spread, wp, wop, ext, dext, stats, mask_q, mask_k, gp, pvs, pvr, gns, gnr,
    sem_in, sem_n, sem_g, sem_pv, sem_gn, sem_ext, sem_dext, sem_stats, *sums,
):
    p = Place()
    barrier = pltpu.get_barrier_semaphore()
    loads = [
        pltpu.make_async_copy(src, dst, sem_in.at[index])
        for index, (src, dst) in enumerate(
            (
                (x_ref, xv),
                (valid_ref, valid_v),
                (gy_ref, gg.at[p.head]),
                (wqkv_ref.at[0, pl.ds(0, 128)], wp.at[pl.ds(0, 128)]),
                (wqkv_ref.at[1, pl.ds(0, 128)], wp.at[pl.ds(128, 128)]),
                (wqkv_ref.at[2, pl.ds(0, 128)], wp.at[pl.ds(256, 128)]),
                (wqkv_ref.at[0, pl.ds(128, 64)], wp.at[pl.ds(384, 64)]),
                (wqkv_ref.at[1, pl.ds(128, 64)], wp.at[pl.ds(512, 64)]),
                (wqkv_ref.at[2, pl.ds(128, 64)], wp.at[pl.ds(576, 64)]),
                (wo_ref.at[pl.ds(0, 128)], wop.at[pl.ds(0, 128)]),
                (wo_ref.at[pl.ds(128, 64)], wop.at[pl.ds(192, 64)]),
            )
        )
    ]

    query_rows = pl.ds(0, 192)
    mixed_store, gx_store, gwo_store, query_store = [
        pltpu.make_async_copy(src, dst, sem_out.at[index])
        for index, (src, dst) in enumerate(
            (
                (mixed_ref, mixed_out),
                (gx_ref, gx_out),
                (gwo_ref, gwo_out),
                (gqkv_ref.at[query_rows], gqkv_out.at[query_rows]),
            )
        )
    ]

    def greet(device):
        pl.semaphore_signal(barrier, inc=1, device_id=device, device_id_type=MESH)

    for load in loads[:3]:
        load.start()
    for step in range(1, N_HEAD):
        greet(p.peer(lax.rem(p.head + step, N_HEAD)))
    for step_lon in (-1, 0, 1):
        if step_lon:
            greet(p.beside(0, step_lon))

        @pl.when(p.lat > 0)
        def _():
            greet(p.beside(-1, step_lon))

        @pl.when(p.lat < N_LAT - 1)
        def _():
            greet(p.beside(1, step_lon))

    for step in range(1, N_Y):
        greet(p.at(y=lax.rem(p.y + step, N_Y)))

    for step in (1, 2, 4, 8, 12, 14, 15):
        greet(p.at(z=lax.rem(p.z + step, N_Z)))

    early = Summed(p, *sums[:N_SUM])
    late = Summed(p, *sums[N_SUM:])
    normed_gather = Spread(p, ng.at[p.head], ng, sem_n)
    grad_gather = Spread(p, gg.at[p.head], gg, sem_g)
    halo = Halo(p, ext, sem_ext, True)
    dout_halo = Halo(p, dext, sem_dext, True)
    stat_halo = Halo(p, stats, sem_stats, False)

    loads[0].wait()
    values = wide(xv[...])
    center = values - jnp.mean(values, axis=-1, keepdims=True)
    inv = lax.rsqrt(jnp.mean(center * center, axis=-1, keepdims=True) + EPSILON)
    norm32[...] = center * inv
    spread[...] = jnp.broadcast_to(inv, spread.shape)
    ng[p.head] = half(center * inv)
    greeted = 3 + 2 + (N_Y - 1) + 7
    edge = jnp.where(p.lat > 0, 3, 0) + jnp.where(p.lat < N_LAT - 1, 3, 0)
    pl.semaphore_wait(barrier, greeted + edge)

    for step in (1, 3, 2):
        normed_gather.copy(normed_gather.other(step)).start()
    for load in loads[3:]:
        load.start()
    loads[2].wait()
    for step in (1, 3, 2):
        grad_gather.copy(grad_gather.other(step)).start()

    loads[1].wait()
    low = lax.broadcasted_iota(jnp.int32, (CELLS, 128), 1) < HEAD_SIZE
    zero = jnp.zeros((CELLS, 128), jnp.bfloat16)
    lane = lax.broadcasted_iota(jnp.int32, (CELLS, 128), 1)
    lat, step_lat, step_lon = geometry((CELLS, AROUND))
    inside = (jnp.abs(step_lat) <= REACH) & (jnp.abs(step_lon) <= REACH)
    middle = (step_lat == 0) & (step_lon == 0)
    there = lat + p.lat * 8
    inside_rows = inside & (there >= 0) & (there < 8 * N_LAT)
    row = lax.broadcasted_iota(jnp.int32, (CELLS, 8), 0)
    column = lax.broadcasted_iota(jnp.int32, (CELLS, 8), 1)
    by_lat = dot(half(jnp.where((row >> 3) == column, 1.0, 0.0)), half(wide(valid_v[...])))
    row = lax.broadcasted_iota(jnp.int32, (CELLS, N_LON), 0)
    column = lax.broadcasted_iota(jnp.int32, (CELLS, N_LON), 1)
    for block in range(4):
        own_flag = half(jnp.where(column == 8 * block + (row & 7), by_lat, 0.0))
        flag = dot(own_flag, jnp.ones((N_LON, 128), jnp.bfloat16))
        ext[block + 1, 48:112, 512:640] = half(flag)
        mask_k[block] = jnp.where(inside_rows & ((flag[:, 0:1] > 0) | middle), 0.0, NEGATIVE)

    for top, at_edge in ((0, p.lat == 0), (112, p.lat == N_LAT - 1)):

        @pl.when(at_edge)
        def _():
            for ref in (ext, dext, stats):
                ref[:, top : top + 48, :] = jnp.zeros((6, 48, ref.shape[2]), jnp.bfloat16)

    early.clear()
    late.clear()
    wp[448:512] = jnp.zeros((64, FULL), jnp.bfloat16)
    wop[128:192] = jnp.zeros((64, FULL), jnp.bfloat16)
    for load in loads[3:]:
        load.wait()
    wpt[...] = wp[...].T
    wopt[...] = wop[...].T

    def first(values):
        return jnp.where(low, values, zero)

    def second(values):
        return jnp.where(low, zero, values)

    def arrived(step, gather, margins, project):
        order = jnp.where(step == 2, 3, jnp.where(step == 3, 2, step))
        block = lax.rem(p.head + order, N_HEAD)

        @pl.when(step > 0)
        def _():
            gather.arrival(block).wait_recv()

        project(block)
        margins.send_rows(block)

        @pl.when(block == 0)
        def _():
            margins.send_side(0)

        @pl.when(block == 3)
        def _():
            margins.send_side(1)

    def project_normed(block):
        projected = dot(ng[block], wpt[...])
        scale = HEAD_SIZE ** (-0.5)
        ext[block + 1, 48:112, 0:128] = half(half(projected[:, 0:128]) * scale)
        ext[block + 1, 48:112, 128:384] = half(projected[:, 128:384])
        ext[block + 1, 48:112, 384:512] = half(projected[:, 512:640])
        ext[block + 1, 48:112, 512:640] = jnp.where(
            low, half(projected[:, 384:512] * scale), ext[block + 1, 48:112, 512:640]
        )

    def project_grad(block):
        dext[block + 1, 48:112] = half(dot(gg[block], wopt[...]))

    @pl.loop(0, N_HEAD)
    def _(step):
        arrived(step, normed_gather, halo, project_normed)

    @pl.loop(0, N_HEAD)
    def _(step):
        arrived(step, grad_gather, dout_halo, project_grad)

    halo.wait_all()
    pick = half(jnp.where(lane == HEAD_SIZE, 1.0, 0.0))
    for block in range(4):
        flag = dot_rows(pick, ext[block : block + 3, :, 512:640].reshape(AROUND, 128))
        mask_q[block] = jnp.where(inside & ((flag > 0) | middle), 0.0, NEGATIVE)
    dout_halo.wait_all()

    def stacked(a, b, c):
        return jnp.concatenate(
            [jnp.concatenate(part, axis=1) for part in (a, b, c)],
            axis=0,
        )

    def thrice(mask):
        return jnp.concatenate([mask, mask, mask], axis=0)

    def around(block, *groups):
        parts = [
            ref[pl.ds(block, 3), :, group * 128 : group * 128 + 128].reshape(AROUND, 128) for ref, group in groups
        ]
        return jnp.concatenate(parts, axis=1)

    def own(block, ref, group):
        return ref[block + 1, 48:112, group * 128 : group * 128 + 128]

    Q01, K01, V01, KV2, Q2 = ((ext, group) for group in range(5))
    D01, D2 = (dext, 0), (dext, 1)
    STAT = (stats, 0)

    def queries_side(block):
        keys, values = around(block, K01, KV2), around(block, V01, KV2)
        q01, d01 = own(block, *Q01), own(block, *D01)
        queries = stacked((first(q01), zero), (second(q01), zero), (zero, first(own(block, *Q2))))
        douts = stacked((first(d01), zero), (second(d01), zero), (zero, own(block, *D2)))
        score = dot_rows(queries, keys) + thrice(mask_q[block])
        best = jnp.max(score, axis=1, keepdims=True)
        chance = jnp.exp(score - best)
        total = jnp.sum(chance, axis=1, keepdims=True)
        level = best + jnp.log(total)
        chance = chance * (1.0 / total)
        inner = dot_rows(douts, values)
        carried = jnp.sum(chance * inner, axis=1, keepdims=True)
        soft_grad = half(chance * (inner - carried))
        soft_v[block] = half(chance)
        soft_grad_v[block] = soft_grad
        tile = jnp.zeros((CELLS, 128), jnp.float32)
        for kind, column in enumerate((level, carried)):
            for head in range(3):
                rest = column[64 * head : 64 * head + 64]
                for digit in range(3):
                    piece = wide(half(rest))
                    rest = rest - piece
                    tile = jnp.where(lane == 9 * kind + 3 * head + digit, piece, tile)
        stats[block + 1, 48:112] = half(tile)

    def queries_rest(block):
        keys, values = around(block, K01, KV2), around(block, V01, KV2)
        attended = dot(soft_v[block], values)
        grad_query = dot(soft_grad_v[block], keys) * HEAD_SIZE ** (-0.5)
        gp[block, :, 640:768] = half(jnp.where(low, attended[0:64, 0:128], attended[64:128, 0:128]))
        gp[block, :, 0:128] = half(jnp.where(low, grad_query[0:64, 0:128], grad_query[64:128, 0:128]))
        gp[block, :, 384:512] = half(jnp.where(low, grad_query[128:192, 128:256], attended[128:192, 128:256]))

    for block in range(4):
        queries_side(block)
    stat_halo.send_all()
    for block in range(4):
        queries_rest(block)

    def cells(ref, *groups):
        return jnp.concatenate([ref[:, :, g * 128 : g * 128 + 128].reshape(4 * CELLS, 128) for g in groups], axis=1)

    grads = gg[...].reshape(4 * CELLS, FULL)
    normed = ng[...].reshape(4 * CELLS, FULL)
    mixed_in = cells(gp, 5, 3)
    weights = dot_cells(mixed_in, grads)
    put(early.src, 0, weights[0:128])
    put(early.src, 128, weights[192:256])
    weights = dot_cells(cells(gp, 0, 3), normed)
    put(early.src, 192, weights[0:192])
    early.send_core()

    early.core_to_y()
    stat_halo.wait_all()

    def minus_one(start):
        return half(jnp.where((lane >= start) & (lane < start + 3), -1.0, 0.0))

    def keys_side(block):
        queries, douts = around(block, Q01, Q2, STAT), around(block, D01, D2, STAT)
        k01, v01, kv2 = own(block, *K01), own(block, *V01), own(block, *KV2)
        keys = stacked(
            (first(k01), zero, minus_one(0)), (second(k01), zero, minus_one(3)), (zero, first(kv2), minus_one(6))
        )
        values = stacked(
            (first(v01), zero, minus_one(9)), (second(v01), zero, minus_one(12)), (zero, second(kv2), minus_one(15))
        )
        chance = jnp.exp(dot_rows(keys, queries) + thrice(mask_k[block]))
        soft_grad = half(chance * dot_rows(values, douts))
        grad_key = dot(soft_grad, queries[:, 0:256])
        grad_value = dot(half(chance), douts[:, 0:256])
        gp[block, :, 128:256] = half(jnp.where(low, grad_key[0:64, 0:128], grad_key[64:128, 0:128]))
        gp[block, :, 256:384] = half(jnp.where(low, grad_value[0:64, 0:128], grad_value[64:128, 0:128]))
        gp[block, :, 512:640] = half(jnp.where(low, grad_key[128:192, 128:256], grad_value[128:192, 128:256]))

    for block in range(4):
        keys_side(block)

    weights = dot_cells(cells(gp, 1, 4), normed)
    put(late.src, 0, weights[0:192])
    weights = jnp.concatenate([dot_cells(cells(gp, 2), normed), weights[192:256]], axis=0)
    put(late.src, 192, weights)
    late.send_core()
    early.y_to_near()

    late.core_to_y()

    norm_spread = Spread(p, gns, gnr, sem_gn)
    gns[...] = half(dot(cells(gp, 0, 1, 2, 3, 4), wp[...])).reshape(4, CELLS, FULL)
    for step in (2, 1, 3):
        norm_spread.copy(norm_spread.other(step)).start()

    out_spread = Spread(p, pvs, pvr, sem_pv)
    pvs[...] = half(dot(mixed_in, wop[...])).reshape(4, CELLS, FULL)
    for step in (2, 1, 3):
        out_spread.copy(out_spread.other(step)).start()
    early.near_to_far()

    late.y_to_near()
    late.near_to_far()
    early.far_to_all()

    total = wide(pvs[p.head])
    for step in (1, 2, 3):
        other = out_spread.other(step)
        out_spread.arrival(other).wait_recv()
        total = total + wide(pvr[other])
    mixed_ref[...] = half(wide(xv[...]) + total)
    mixed_store.start()

    total = wide(gns[p.head])
    for step in (1, 2, 3):
        other = norm_spread.other(step)
        norm_spread.arrival(other).wait_recv()
        total = total + wide(gnr[other])
    own_norm = norm32[...]
    mean = jnp.mean(total, axis=-1, keepdims=True)
    along = jnp.mean(total * own_norm, axis=-1, keepdims=True)
    d_input = spread[:, 0:1] * (total - mean - own_norm * along)
    gx_ref[...] = half(wide(gg[p.head]) + d_input)
    gx_store.start()


    early.all_to_y()
    late.far_to_all()
    early.y_to_core()
    for spread_copy in (normed_gather, grad_gather, out_spread, norm_spread):
        spread_copy.wait_sent()
    for one in (halo, dout_halo, stat_halo):
        one.wait_sent()
    late.all_to_y()
    early.finish()
    take(early.res, 0, gwo_ref, 0, 192)
    take(early.res, 192, gqkv_ref, 0, 192)
    gwo_store.start()
    query_store.start()
    late.y_to_core()
    early.wait_sent()
    quarters = []
    for step in (0, 1, 3, 2):
        y = lax.rem(p.y + step, N_Y)
        late.cg_copy(y, True).wait_recv()
        for third in range(6):
            to = pl.ds(pl.multiple_of(192 + 96 * y + 16 * third, 16), 16)
            for column in range(6):
                gqkv_ref[to, column * 128 : column * 128 + 128] = late.res[
                    column // 3, y, third * 3 + column % 3
                ]
        to = pl.ds(pl.multiple_of(192 + 96 * y, 16), 96)
        quarters.append(pltpu.make_async_copy(gqkv_ref.at[to], gqkv_out.at[to], sem_out.at[4 + step]))
        quarters[-1].start()
    late.wait_sent()
    for store in (mixed_store, gx_store, gwo_store, query_store, *quarters):
        store.wait()


def store_kernel(*refs):
    given, out, held, sems = refs[:4], refs[4:8], refs[8:12], refs[12]
    loads = [pltpu.make_async_copy(given[i], held[i], sems.at[0, i]) for i in range(4)]
    stores = [pltpu.make_async_copy(held[i], out[i], sems.at[1, i]) for i in range(4)]
    for load in loads:
        load.start()
    for load, store in zip(loads, stores):
        load.wait()
        store.start()
    for store in stores:
        store.wait()


def on_device(activations, qkv_weight, out_weight, valid, grad_y):
    bf, f32 = jnp.bfloat16, jnp.float32
    gathered = pltpu.VMEM((N_HEAD, CELLS, FULL), bf)
    pair = pltpu.SemaphoreType.DMA((2, N_HEAD))
    around = pltpu.SemaphoreType.DMA((2, 14))
    results = pl.pallas_call(
        block_kernel,
        out_shape=[
            jax.ShapeDtypeStruct((CELLS, FULL), bf),
            jax.ShapeDtypeStruct((CELLS, FULL), bf),
            jax.ShapeDtypeStruct((3 * 192, FULL), bf),
            jax.ShapeDtypeStruct((192, FULL), bf),
        ],
        in_specs=[pl.BlockSpec(memory_space=pltpu.HBM)] * 5,
        out_specs=[pl.BlockSpec(memory_space=pltpu.HBM)] * 4,
        scratch_shapes=[
            pltpu.VMEM((CELLS, FULL), bf),
            pltpu.VMEM((CELLS, FULL), bf),
            pltpu.VMEM((3 * 192, FULL), bf),
            pltpu.VMEM((192, FULL), bf),
            pltpu.VMEM((FULL, 640), bf),
            pltpu.VMEM((FULL, 256), bf),
            pltpu.VMEM((4, 192, AROUND), bf),
            pltpu.VMEM((4, 192, AROUND), bf),
            pltpu.SemaphoreType.DMA((8,)),
            pltpu.VMEM((CELLS, FULL), bf),
            pltpu.VMEM((8, N_LON), jnp.int32),
            gathered,
            gathered,
            pltpu.VMEM((CELLS, FULL), f32),
            pltpu.VMEM((CELLS, 128), f32),
            pltpu.VMEM((640, FULL), bf),
            pltpu.VMEM((256, FULL), bf),
            pltpu.VMEM((6, TALL, 640), bf),
            pltpu.VMEM((6, TALL, 256), bf),
            pltpu.VMEM((6, TALL, 128), bf),
            pltpu.VMEM((4, CELLS, AROUND), f32),
            pltpu.VMEM((4, CELLS, AROUND), f32),
            gathered,
            gathered,
            gathered,
            gathered,
            gathered,
            pltpu.SemaphoreType.DMA((11,)),
            pair,
            pair,
            pair,
            pair,
            around,
            around,
            around,
            *Summed.scratch(),
            *Summed.scratch(),
        ],
        compiler_params=pltpu.CompilerParams(
            collective_id=0, has_side_effects=True, vmem_limit_bytes=63 * 2**20
        ),
    )(
        activations.reshape(CELLS, FULL),
        grad_y.reshape(CELLS, FULL),
        qkv_weight,
        out_weight,
        valid,
    )
    mixed, grad_x, grad_qkv, grad_out = pl.pallas_call(
        store_kernel,
        out_shape=[jax.ShapeDtypeStruct(result.shape, bf) for result in results],
        in_specs=[pl.BlockSpec(memory_space=pl.ANY)] * 4,
        out_specs=[pl.BlockSpec(memory_space=pltpu.HBM)] * 4,
        scratch_shapes=[
            *(pltpu.VMEM(result.shape, bf) for result in results),
            pltpu.SemaphoreType.DMA((2, 4)),
        ],
    )(*results)
    return (
        mixed.reshape(activations.shape),
        grad_x.reshape(activations.shape),
        grad_qkv.reshape(qkv_weight.shape),
        grad_out,
    )


def solution(mesh):
    return jax.shard_map(
        on_device,
        mesh=mesh,
        in_specs=(
            P("lat", ("lon", "head"), None),
            P(None, "head", None),
            P("head", None),
            P("lat", "lon"),
            P("lat", ("lon", "head"), None),
        ),
        out_specs=(
            P("lat", ("lon", "head"), None),
            P("lat", ("lon", "head"), None),
            P(None, "head", None),
            P("head", None),
        ),
        check_vma=False,
    )
```
